32 devices in a mesh: ctx: 16 (over z, x, core), tp: 2 (over y).
Axes of the slice: x: 2, y: 2, z: 4, core: 2. Of those that a mesh axis runs over, the one named last changes fastest.
Arguments:
- query: bfloat16 [12288, 4096], P('ctx', 'tp'), may hold values from -36 to 36
- key: bfloat16 [12288, 1024], P('ctx', 'tp'), may hold values from -32 to 32
- value: bfloat16 [12288, 1024], P('ctx', 'tp'), may hold values from -6 to 6
- keep_rank: int32 [16, 768], P('ctx'), may hold values from 0 to 767, each once within a row
- kept_count: int32 [16], replicated, may hold values from 1 to 768, 6144 in all
- out_weight: bfloat16 [4096, 8192], P('tp'), may hold values from -0.09375 to 0.09375
Outputs:
- mixed: bfloat16 [6144, 8192], P('ctx', 'tp')
The draws below stay inside these ranges and needn't reach their ends.
Inputs may be any that keep to these rules, and one draw needn't show every extreme that they name: `keep_rank`: each row is a permutation of 0 to 767. `kept_count`: the counts sum to 6144; the largest is exactly 768.
All inputs are finite; a program needn't handle non-finite values.
Results may differ from the reference program's by a relative error of at most 0.019.
The reference program's roundings to bfloat16 on the way count: a program that leaves them out, or rounds other values in their place, can miss the bound.
Values may be sent and summed in bfloat16 or wider, within the bound.
No kernel may reach another device: no remote copies, remote signals or barrier semaphores. Data moves between devices by JAX's collectives and lax.ppermute only.
A program may use at most 128 MiB of HBM per device.

```python
import math
import jax
import jax.numpy as jnp
import numpy as np
from jax import lax

D = 8192
HD = 128
KVH = 8
HQ = 32
ORIG_DEV = 768
KEPT = 6144
ORIG = 12288
N_CTX = 16
N_TP = 2


def draw_query(key, part):
    key = jax.random.fold_in(key, 1)
    return (3.0 * jnp.clip(jax.random.normal(key, (ORIG, HQ * HD), jnp.float32), -6.0, 6.0)).astype(jnp.bfloat16)


def draw_key(key, part):
    key = jax.random.fold_in(key, 2)
    return jnp.clip(jax.random.normal(key, (ORIG, KVH * HD), jnp.float32), -6.0, 6.0).astype(jnp.bfloat16)


def block_scale(stream_key, extent, shards, low, largest):
    factor_of, own = 1.0, jax.random.fold_in(stream_key, 6)
    for axis_at, shards_of in shards:
        draws = jnp.exp(jax.random.uniform(jax.random.fold_in(own, axis_at), (shards_of,), jnp.float32, low / len(shards), largest / len(shards)))
        factor_of = factor_of * jnp.repeat(draws, extent[axis_at] // shards_of).reshape([-1 if axis == axis_at else 1 for axis in range(len(extent))])
    return factor_of


def length_profile(count, total, bound, skew):
    portions = [(1 << 20) // math.isqrt(grade ** skew) + 1 for grade in range(2, count + 1)]
    surplus, counts = total - bound - (count - 1), [1] * (count - 1)
    while surplus > 0:
        movable = [i for i in range(count - 1) if counts[i] < bound]
        mass, budget = sum([portions[i] for i in movable]), surplus
        for i in movable:
            extra = min(bound - counts[i], max(1, budget * portions[i] // mass), surplus)
            counts[i] = counts[i] + extra
            surplus = surplus - extra
    return np.array([bound] + counts)


def uneven_parts(key, count, total, reach, lean):
    if count == 2:
        one = jax.random.randint(key, (), max(1, total - reach), min(reach, total - 1) + 1)
        return jnp.stack([one, total - one])
    sizes = jnp.asarray(length_profile(count, total, reach, lean), jnp.int32)
    couples = (count - 1) // 2
    giver, receiver = sizes[1:1 + 2 * couples:2], sizes[2:2 + 2 * couples:2]
    margin = jnp.minimum(giver - 1, reach - receiver)
    passed = jax.random.randint(jax.random.fold_in(key, 1), (couples,), 0, 1 << 20) % (margin + 1)
    sizes = sizes.at[1:1 + 2 * couples:2].set(giver - passed).at[2:2 + 2 * couples:2].set(receiver + passed)
    return sizes[jax.random.permutation(jax.random.fold_in(key, 2), count)]


def gaussian(key, shape, deviation, reach, shards=(), kind=jnp.bfloat16):
    gain = block_scale(key, shape, shards, -0.22, 0.18) if shards else 1.0
    drawn = jax.random.normal(key, shape, jnp.float32) * deviation * gain
    return jnp.minimum(jnp.maximum(drawn, -reach), reach).astype(kind)


def setup_inputs(seed: int = 0) -> dict:
    keys = jax.random.split(jax.random.key(seed), 7)
    return {
        "query": draw_query(jax.random.fold_in(keys[6], 71), 0),
        "key": draw_key(jax.random.fold_in(keys[6], 71), 0),
        "value": gaussian(keys[2], (ORIG, KVH * HD), 1.0, 6.0, ((0, 16), (1, 2))),
        "keep_rank": jax.vmap(lambda own: jax.random.permutation(own, ORIG_DEV))(jax.random.split(keys[3], N_CTX)).reshape((N_CTX, ORIG_DEV)).astype(jnp.int32),
        "kept_count": uneven_parts(keys[4], N_CTX, KEPT, ORIG_DEV, 2).astype(jnp.int32),
        "out_weight": gaussian(keys[5], (HQ * HD, D), (HQ * HD) ** -0.5, 0.09375, ((0, 2),)),
    }


rope_base = 1000000.0
masked_score = -1e+30

def rotate(rows, positions, heads):
    count_rows = rows.shape[0]
    half_dim = HD // 2
    as_float = rows.astype(jnp.float32).reshape(count_rows, heads, HD)
    inv_freq = rope_base ** (-(jnp.arange(half_dim, dtype=jnp.float32) * 2.0 / HD))
    angles = positions.astype(jnp.float32)[:, None] * inv_freq[None, :]
    cosine = jnp.cos(angles)[:, None, :]
    sine = jnp.sin(angles)[:, None, :]
    first_half = as_float[..., :half_dim]
    second_half = as_float[..., half_dim:]
    turned = jnp.concatenate([first_half * cosine - second_half * sine, second_half * cosine + first_half * sine], axis=-1)
    return turned.reshape(count_rows, heads * HD).astype(jnp.bfloat16)

def reference(query, key, value, keep_rank, kept_count, out_weight):
    kept_mask = (keep_rank < kept_count[:, None]).reshape(-1)
    chosen = jnp.nonzero(kept_mask, size=KEPT)[0].astype(jnp.int32)
    rot_query = rotate(query[chosen], chosen, HQ)
    rot_key = rotate(key[chosen], chosen, KVH)
    kept_value = value[chosen]
    group_size = HQ // KVH
    key_float = rot_key.astype(jnp.float32).reshape(KEPT, KVH, HD)
    value_float = kept_value.astype(jnp.float32).reshape(KEPT, KVH, HD)
    block_rows = 256
    query_blocks = rot_query.reshape(KEPT // block_rows, block_rows, KVH, group_size, HD)
    block_starts = jnp.arange(KEPT // block_rows, dtype=jnp.int32) * block_rows
    key_index = jnp.arange(KEPT, dtype=jnp.int32)

    def attend(pair):
        query_block, block_start = pair
        scores = jnp.einsum('bkgd,pkd->kgbp', query_block.astype(jnp.float32), key_float) / math.sqrt(HD)
        row_index = block_start + jnp.arange(block_rows, dtype=jnp.int32)
        allowed = key_index[None, :] <= row_index[:, None]
        scores = jnp.where(allowed, scores, masked_score)
        row_max = lax.optimization_barrier(jnp.max(scores, axis=-1, keepdims=True))
        weights = jnp.where(allowed, jnp.exp(scores - row_max), 0.0)
        row_total = lax.optimization_barrier(jnp.sum(weights, axis=-1))
        weights_b = weights.astype(jnp.bfloat16)
        summed = jnp.einsum('kgbp,pkd->bkgd', weights_b.astype(jnp.float32), value_float)
        result = summed / jnp.transpose(row_total, (2, 0, 1))[..., None]
        return result.reshape(block_rows, HQ * HD).astype(jnp.bfloat16)
    attention = lax.map(attend, (query_blocks, block_starts)).reshape(KEPT, HQ * HD)
    group_width = HQ * HD // N_TP
    attention_groups = jnp.transpose(attention.reshape(KEPT, N_TP, group_width), (1, 0, 2))
    weight_groups = out_weight.reshape(N_TP, group_width, D)

    def add_group(running, pair):
        attention_part, weight_part = pair
        partial_term = jnp.dot(attention_part, weight_part, preferred_element_type=jnp.float32).astype(jnp.bfloat16)
        partial_term = lax.optimization_barrier(partial_term)
        return (running + partial_term.astype(jnp.float32), None)
    summed_all, _ = lax.scan(add_group, jnp.zeros((KEPT, D), jnp.float32), (attention_groups, weight_groups))
    return summed_all.astype(jnp.bfloat16)
```

```python
import functools
import math

import jax
import jax.numpy as jnp
from jax import lax
from jax.experimental import pallas as pl
from jax.experimental.pallas import tpu as pltpu
from jax.sharding import PartitionSpec as P

HD = 128
TOK_DEV = 384
TILE = 16
PAD = 128
CHUNKS = 2

rope_base = 1000000.0
masked_score = -1e30
exp2_scale = math.log2(math.e) / math.sqrt(HD)
VMEM_BYTES = 58 * 1024 * 1024


def whole_vmem():
    return pl.BlockSpec(memory_space=pltpu.VMEM)


def whole_smem():
    return pl.BlockSpec(memory_space=pltpu.SMEM)


def params():
    return pltpu.CompilerParams(vmem_limit_bytes=VMEM_BYTES)


def turn(rows, cosine, sine):
    as_float = rows.astype(jnp.float32)
    swapped = pltpu.roll(as_float, HD // 2, 1)
    return (as_float * cosine + swapped * sine).astype(jnp.bfloat16)


def one_hot(slots, count):
    ids = lax.broadcasted_iota(jnp.int32, (count, slots.shape[1]), 0)
    return (ids == slots).astype(jnp.float32).astype(jnp.bfloat16)


def pack_kv_kernel(slot_ref, cos_ref, sin_ref, key_ref, value_ref, out_ref, hot_ref):
    @pl.when(pl.program_id(0) == 0)
    def _():
        hot_ref[...] = one_hot(slot_ref[...], hot_ref.shape[0])

    both = jnp.concatenate([turn(key_ref[...], cos_ref[...], sin_ref[...]), value_ref[...]], axis=1)
    out_ref[0] = jnp.dot(hot_ref[...], both, preferred_element_type=jnp.float32).astype(jnp.bfloat16)


def pack_kv(slots, cosine, sine, key, value, cap):
    rows = key.shape[0]
    heads = key.shape[1] // HD
    fixed = lambda i: (0, 0)
    return pl.pallas_call(
        pack_kv_kernel,
        grid=(heads,),
        in_specs=[
            pl.BlockSpec((1, rows), fixed),
            pl.BlockSpec((rows, HD), fixed),
            pl.BlockSpec((rows, HD), fixed),
            pl.BlockSpec((rows, HD), lambda i: (0, i)),
            pl.BlockSpec((rows, HD), lambda i: (0, i)),
        ],
        out_specs=pl.BlockSpec((1, cap, 2 * HD), lambda i: (i, 0, 0)),
        out_shape=jax.ShapeDtypeStruct((heads, cap, 2 * HD), jnp.bfloat16),
        scratch_shapes=[pltpu.VMEM((cap, rows), jnp.bfloat16)],
        compiler_params=params(),
        cost_estimate=pl.CostEstimate(
            flops=2 * heads * cap * rows * 2 * HD, bytes_accessed=rows * heads * HD * 8, transcendentals=0
        ),
    )(slots, cosine, sine, key, value)


def pack_q_kernel(classes, cap, slot_ref, cos_ref, sin_ref, query_ref, *rest):
    out_refs, hot_ref = rest[:-1], rest[-1]

    @pl.when(pl.program_id(0) == 0)
    def _():
        hot_ref[...] = one_hot(slot_ref[...], hot_ref.shape[0])

    cosine, sine = cos_ref[...], sin_ref[...]
    both = jnp.concatenate(
        [turn(query_ref[:, :HD], cosine, sine), turn(query_ref[:, HD:], cosine, sine)], axis=1
    )
    for j, out_ref in enumerate(out_refs):
        for r in range(classes):
            first = (j * classes + r) * cap
            moved = jnp.dot(
                hot_ref[first : first + cap, :], both, preferred_element_type=jnp.float32
            ).astype(jnp.bfloat16)
            out_ref[0, r] = moved[:, :HD]
            out_ref[1, r] = moved[:, HD:]


def pack_q(slots, cosine, sine, query, chunks, classes, cap):
    rows = query.shape[0]
    heads = query.shape[1] // HD
    fixed = lambda i: (0, 0)
    total = chunks * classes * cap
    return pl.pallas_call(
        functools.partial(pack_q_kernel, classes, cap),
        grid=(heads // 2,),
        in_specs=[
            pl.BlockSpec((1, rows), fixed),
            pl.BlockSpec((rows, HD), fixed),
            pl.BlockSpec((rows, HD), fixed),
            pl.BlockSpec((rows, 2 * HD), lambda i: (0, i)),
        ],
        out_specs=[pl.BlockSpec((2, classes, cap, HD), lambda i: (i, 0, 0, 0))] * chunks,
        out_shape=[jax.ShapeDtypeStruct((heads, classes, cap, HD), jnp.bfloat16)] * chunks,
        scratch_shapes=[pltpu.VMEM((total, rows), jnp.bfloat16)],
        compiler_params=params(),
        cost_estimate=pl.CostEstimate(
            flops=2 * heads * total * rows * HD, bytes_accessed=rows * heads * HD * 4, transcendentals=0
        ),
    )(slots, cosine, sine, query)


def piece_rows(cap):
    return max(rows for rows in range(TILE, PAD + 1, TILE) if cap % rows == 0)


def merge_pieces(first_tile, pieces, piece, source, add):
    def one(i, carry):
        at = pl.multiple_of(first_tile * TILE + i * piece, TILE)
        add(at, source(pl.multiple_of(i * piece, TILE)))
        return carry

    lax.fori_loop(0, pieces, one, 0)


def compact_kv_kernel(per, total, tile_ref, piece_ref, *rest):
    parts, (key_out, value_out), (key_all, value_all) = rest[:-4], rest[-4:-2], rest[-2:]
    piece = piece_rows(parts[0].shape[1])
    key_all[...] = jnp.zeros_like(key_all)
    value_all[...] = jnp.zeros_like(value_all)

    def add(at, rows):
        key_all[pl.ds(at, piece), :] += rows[:, :HD]
        value_all[pl.ds(at, piece), :] += rows[:, HD:]

    for k, part in enumerate(parts):
        for z in range(per):
            entry = k * per + z
            merge_pieces(
                tile_ref[entry], piece_ref[entry], piece, lambda at: part[z, pl.ds(at, piece), :], add
            )
    key_out[...] = key_all[:total, :]
    value_out[:, :HD] = value_all[:total, :]
    value_out[:, HD:] = jnp.ones((total, HD), jnp.bfloat16)


def compact_kv(tiles, pieces, parts, total):
    per = parts[0].shape[0]
    return pl.pallas_call(
        functools.partial(compact_kv_kernel, per, total),
        in_specs=[whole_smem(), whole_smem()] + [whole_vmem()] * len(parts),
        out_specs=[whole_vmem()] * 2,
        out_shape=[
            jax.ShapeDtypeStruct((total, HD), jnp.bfloat16),
            jax.ShapeDtypeStruct((total, 2 * HD), jnp.bfloat16),
        ],
        scratch_shapes=[pltpu.VMEM((total + PAD, HD), jnp.bfloat16)] * 2,
        compiler_params=params(),
        cost_estimate=pl.CostEstimate(flops=total * HD * 8, bytes_accessed=total * HD * 16, transcendentals=0),
    )(tiles, pieces, *parts)


def attend_kernel(ctx_size, block, base_ref, tile_ref, piece_ref, got_ref, key_ref, value_ref, out_ref,
                  query_all, scores, run_max, run_acc):
    span = 2 * TOK_DEV
    pair = 2 * block
    piece = piece_rows(got_ref.shape[1])
    query_all[...] = jnp.zeros_like(query_all)

    def add(at, rows):
        query_all[pl.ds(at, piece), :] += rows

    for s in range(ctx_size):
        merge_pieces(tile_ref[s], piece_ref[s], piece, lambda at: got_ref[s, pl.ds(at, piece), :], add)

    def score(to, i, k):
        rows = query_all[pl.ds(pl.multiple_of(i * pair, TILE), pair), :]
        keys = key_ref[pl.ds(pl.multiple_of(k * span, TILE), span), :]
        scores[to] = lax.dot_general(
            rows, keys, (((1,), (1,)), ((), ())), preferred_element_type=jnp.float32
        )

    def absorb(found, k):
        before = run_max[...]
        after = jnp.maximum(before, jnp.max(found, axis=1, keepdims=True))
        weights = jnp.exp2((found - jnp.concatenate([after] * (span // HD), axis=1)) * exp2_scale)
        rescale = jnp.exp2((before - after) * exp2_scale)
        run_max[...] = after
        values = value_ref[pl.ds(pl.multiple_of(k * span, TILE), span), :]
        run_acc[...] = run_acc[...] * jnp.concatenate([rescale, rescale], axis=1) + jnp.dot(
            weights.astype(jnp.bfloat16), values, preferred_element_type=jnp.float32
        )

    supers = ctx_size // 2
    base = base_ref[0]
    score(0, 0, 0)

    def one_super(i, step):
        run_max[...] = jnp.full_like(run_max, masked_score)
        run_acc[...] = jnp.zeros_like(run_acc)

        def one_block(k, step):
            now = step % 2
            score(1 - now, i, k + 1)
            absorb(scores[now], k)
            return step + 1

        step = lax.fori_loop(0, i, one_block, step)
        now = step % 2
        score(1 - now, jnp.minimum(i + 1, supers - 1), 0)
        row = lax.broadcasted_iota(jnp.int32, (pair, span), 0)
        col = lax.broadcasted_iota(jnp.int32, (pair, span), 1)
        row = jnp.where(row >= block, row + (TOK_DEV - block), row) + base
        absorb(jnp.where(col <= row, scores[now], masked_score), i)
        result = (run_acc[:, :HD] / run_acc[:, HD:]).astype(jnp.bfloat16)
        out_ref[2 * i] = result[:block]
        out_ref[2 * i + 1] = result[block:]
        return step + 1

    lax.fori_loop(0, supers, one_super, 0)


def attend(base, tiles, pieces, got, keys, values, block):
    ctx_size = got.shape[0]
    total = keys.shape[0]
    pairs = total * ctx_size * block // 2
    return pl.pallas_call(
        functools.partial(attend_kernel, ctx_size, block),
        in_specs=[whole_smem()] * 3 + [whole_vmem()] * 3,
        out_specs=whole_vmem(),
        out_shape=jax.ShapeDtypeStruct((ctx_size, block, HD), jnp.bfloat16),
        scratch_shapes=[
            pltpu.VMEM((ctx_size * block + PAD, HD), jnp.bfloat16),
            pltpu.VMEM((2, 2 * block, 2 * TOK_DEV), jnp.float32),
            pltpu.VMEM((2 * block, HD), jnp.float32),
            pltpu.VMEM((2 * block, 2 * HD), jnp.float32),
        ],
        compiler_params=params(),
        cost_estimate=pl.CostEstimate(
            flops=pairs * 8 * HD, bytes_accessed=total * HD * 8, transcendentals=pairs
        ),
    )(base, tiles, pieces, got, keys, values)


def project_kernel(classes, column_ref, got_ref, weight_ref, out_ref, rows_ref):
    block = got_ref.shape[1]

    @pl.when(pl.program_id(0) == 0)
    def _():
        for d in range(got_ref.shape[0]):
            h, r = d // classes, d % classes
            rows_ref[r * block : (r + 1) * block, h * HD : (h + 1) * HD] = got_ref[d]

    out_ref[...] = jnp.dot(
        rows_ref[...], weight_ref[...], preferred_element_type=jnp.float32
    ).astype(jnp.bfloat16)


def project(first_column, got, weight, columns, classes):
    ctx_size, block, _ = got.shape
    rows, depth = classes * block, weight.shape[0]
    step = min(512, columns)
    return pl.pallas_call(
        functools.partial(project_kernel, classes),
        grid_spec=pltpu.PrefetchScalarGridSpec(
            num_scalar_prefetch=1,
            grid=(columns // step,),
            in_specs=[
                pl.BlockSpec((ctx_size, block, HD), lambda i, first: (0, 0, 0)),
                pl.BlockSpec((depth, step), lambda i, first: (0, first[0] + i)),
            ],
            out_specs=pl.BlockSpec((rows, step), lambda i, first: (0, i)),
            scratch_shapes=[pltpu.VMEM((rows, depth), jnp.bfloat16)],
        ),
        out_shape=jax.ShapeDtypeStruct((rows, columns), jnp.bfloat16),
        compiler_params=params(),
        cost_estimate=pl.CostEstimate(
            flops=2 * rows * depth * columns, bytes_accessed=2 * depth * columns, transcendentals=0
        ),
    )((first_column // step).astype(jnp.int32).reshape(1), got, weight)


def tables(query_rows):
    half_dim = HD // 2
    positions = lax.axis_index("ctx") * query_rows + jnp.arange(query_rows, dtype=jnp.int32)
    inv_freq = rope_base ** (-(jnp.arange(half_dim, dtype=jnp.float32) * 2.0 / HD))
    angles = positions.astype(jnp.float32)[:, None] * inv_freq[None, :]
    cosine, sine = jnp.cos(angles), jnp.sin(angles)
    return jnp.concatenate([cosine, cosine], axis=1), jnp.concatenate([-sine, sine], axis=1)


def rows_below(start, cls, block):
    return start // TOK_DEV * block + jnp.clip(start % TOK_DEV - cls * block, 0, block)


def piece_table(starts, ends, cls, block, cap):
    piece = piece_rows(cap)
    low, high = rows_below(starts, cls, block), rows_below(ends, cls, block)
    return low // TILE, jnp.where(high > low, (high - low + low % TILE + piece - 1) // piece, 0)


def local(query, key, value, keep_rank, kept_count, out_weight):
    ctx_size = lax.axis_size("ctx")
    tp_size = lax.axis_size("tp")
    me = lax.axis_index("ctx")
    tp_me = lax.axis_index("tp")
    orig_rows = query.shape[0]
    heads = query.shape[1] // HD
    kv_heads = key.shape[1] // HD
    members = ctx_size // kv_heads
    classes = ctx_size // heads
    chunks = CHUNKS if classes == 1 else 1
    block = TOK_DEV // (chunks * classes)
    total = ctx_size * TOK_DEV
    reach = orig_rows // TOK_DEV
    cap = reach * block + TILE
    cap_kv = orig_rows + TILE

    ends = jnp.cumsum(kept_count)
    starts = ends - kept_count
    ids = jnp.arange(ctx_size, dtype=jnp.int32)
    my_count = jnp.sum(jnp.where(ids == me, kept_count, 0))
    my_start = jnp.sum(jnp.where(ids == me, starts, 0))
    is_kept = keep_rank[0] < my_count
    order = jnp.cumsum(is_kept.astype(jnp.int32)) - 1
    place = my_start + order
    kv_slots = jnp.where(is_kept, order + my_start % TILE, -1)[None, :]
    within = place % TOK_DEV
    cls = within // block
    low = rows_below(my_start, cls, block)
    q_slots = jnp.where(
        is_kept, cls * cap + place // TOK_DEV * block + within % block - low + low % TILE, -1
    )[None, :]
    cosine, sine = tables(orig_rows)

    packed_kv = pack_kv(kv_slots, cosine, sine, key, value, cap_kv)
    if kv_heads > 1:
        across = [[z * members + m for z in range(kv_heads)] for m in range(members)]
        packed_kv = lax.all_to_all(
            packed_kv, "ctx", split_axis=0, concat_axis=0, tiled=True, axis_index_groups=across
        )
    parts = [packed_kv]
    bit = members // 2
    offsets = [0]
    while bit >= 1:
        swap = [(d, d ^ bit) for d in range(ctx_size)]
        parts = parts + [lax.ppermute(part, "ctx", swap) for part in parts]
        offsets = offsets + [offset ^ bit for offset in offsets]
        bit //= 2

    packed_q = pack_q(q_slots, cosine, sine, query, chunks, classes, cap)
    got_q = [
        lax.all_to_all(
            one.reshape(ctx_size, cap, HD), "ctx", split_axis=0, concat_axis=0, tiled=True
        )
        for one in packed_q
    ]

    member = me % members
    kv_sources = (
        ids[:kv_heads][None, :] * members + (member ^ jnp.array(offsets, jnp.int32))[:, None]
    ).reshape(-1)
    kv_starts = jnp.sum(jnp.where(kv_sources[:, None] == ids[None, :], starts[None, :], 0), axis=1)
    kv_ends = jnp.sum(jnp.where(kv_sources[:, None] == ids[None, :], ends[None, :], 0), axis=1)
    kv_tiles, kv_pieces = piece_table(kv_starts, kv_ends, 0, TOK_DEV, cap_kv)
    keys, values = compact_kv(kv_tiles, kv_pieces, parts, total)

    mine, other = [], []
    for j in range(chunks):
        cls_j = j * classes + me % classes
        tiles, pieces = piece_table(starts, ends, cls_j, block, cap)
        done = attend(
            (cls_j * block).reshape(1), tiles, pieces, got_q[j], keys, values, block
        )
        got = lax.all_to_all(done, "ctx", split_axis=0, concat_axis=0, tiled=True)
        columns = out_weight.shape[1] // tp_size
        if tp_size == 2:
            theirs = project((1 - tp_me) * columns, got, out_weight, columns, classes)
            other.append(lax.ppermute(theirs, "tp", [(0, 1), (1, 0)]))
            mine.append(project(tp_me * columns, got, out_weight, columns, classes))
        else:
            full = project(jnp.int32(0) * tp_me, got, out_weight, columns * tp_size, classes)
            split = jnp.transpose(full.reshape(full.shape[0], tp_size, columns), (1, 0, 2))
            swapped = lax.all_to_all(split, "tp", split_axis=0, concat_axis=0, tiled=True)
            mine.append(jnp.sum(swapped.astype(jnp.float32), axis=0))
            other.append(jnp.zeros((), jnp.float32))
    return jnp.concatenate(
        [
            (a.astype(jnp.float32) + b.astype(jnp.float32)).astype(jnp.bfloat16)
            for a, b in zip(mine, other)
        ],
        axis=0,
    )


def solution(mesh):
    placed = (P("ctx", "tp"), P("ctx", "tp"), P("ctx", "tp"), P("ctx", None), P(), P("tp", None))
    return jax.shard_map(
        local, mesh=mesh, in_specs=placed, out_specs=P("ctx", "tp"), check_vma=False
    )
```

```python
import functools
import math

import jax
import jax.numpy as jnp
from jax import lax
from jax.experimental import pallas as pl
from jax.experimental.pallas import tpu as pltpu
from jax.sharding import PartitionSpec as P

HD = 128
TOK_DEV = 384
TILE = 16
PAD = 128
CHUNKS = 2

rope_base = 1000000.0
masked_score = -1e30
exp2_scale = math.log2(math.e) / math.sqrt(HD)
VMEM_BYTES = 58 * 1024 * 1024


def whole_vmem():
    return pl.BlockSpec(memory_space=pltpu.VMEM)


def whole_smem():
    return pl.BlockSpec(memory_space=pltpu.SMEM)


def params():
    return pltpu.CompilerParams(vmem_limit_bytes=VMEM_BYTES)


def turn(rows, cosine, sine):
    as_float = rows.astype(jnp.float32)
    swapped = pltpu.roll(as_float, HD // 2, 1)
    return (as_float * cosine + swapped * sine).astype(jnp.bfloat16)


def rows_below(start, cls, block):
    whole = lax.div(start, TOK_DEV)
    return whole * block + jnp.clip(start - whole * TOK_DEV - cls * block, 0, block)


def slots_kernel(reach, groups, block, cap, me_ref, count_ref, rank_ref, kv_out, q_out):
    me = me_ref[0]
    rows = rank_ref.shape[1]
    start = jnp.int32(0)
    for s in range(count_ref.shape[0]):
        start = start + jnp.where(s < me, count_ref[s], 0)
    kept = rank_ref[...] < count_ref[me]
    upper = lax.broadcasted_iota(jnp.int32, (rows, rows), 0) <= lax.broadcasted_iota(
        jnp.int32, (rows, rows), 1
    )
    flags = jnp.broadcast_to(kept.astype(jnp.float32), (8, rows)).astype(jnp.bfloat16)
    order = (
        jnp.dot(
            flags, upper.astype(jnp.float32).astype(jnp.bfloat16), preferred_element_type=jnp.float32
        )[:1].astype(jnp.int32)
        - 1
    )
    kv_out[...] = jnp.where(kept, order + (start & (TILE - 1)), -1)
    place = start + order
    first = lax.div(start, TOK_DEV)
    device = first + jnp.zeros_like(place)
    for step in range(1, reach + 1):
        device = device + (place >= (first + step) * TOK_DEV).astype(jnp.int32)
    within = place - device * TOK_DEV
    cls = jnp.zeros_like(place)
    for step in range(1, groups):
        cls = cls + (within >= step * block).astype(jnp.int32)
    low = first * block + jnp.clip(start - first * TOK_DEV - cls * block, 0, block)
    slot = cls * cap + device * block + within - cls * block - low + (low & (TILE - 1))
    q_out[...] = jnp.where(kept, slot, -1)


def find_slots(me, counts, ranks, reach, groups, block, cap):
    shape = jax.ShapeDtypeStruct(ranks.shape, jnp.int32)
    return pl.pallas_call(
        functools.partial(slots_kernel, reach, groups, block, cap),
        in_specs=[whole_smem(), whole_smem(), whole_vmem()],
        out_specs=[whole_vmem()] * 2,
        out_shape=[shape, shape],
        compiler_params=params(),
        cost_estimate=pl.CostEstimate(flops=2**20, bytes_accessed=2**14, transcendentals=0),
    )(me, counts, ranks)


def pack_kernel(turned, classes, cap, width, slot_ref, cos_ref, sin_ref, row_ref, *rest):
    out_refs, hot_ref = rest[:-1], rest[-1]

    @pl.when(pl.program_id(0) == 0)
    def _():
        ids = lax.broadcasted_iota(jnp.int32, hot_ref.shape, 0)
        hot_ref[...] = (ids == slot_ref[...]).astype(jnp.float32).astype(jnp.bfloat16)

    if turned:
        rows = jnp.concatenate(
            [
                turn(row_ref[:, h * HD : (h + 1) * HD], cos_ref[...], sin_ref[...])
                for h in range(width)
            ],
            axis=1,
        )
    else:
        rows = row_ref[...]
    for j, out_ref in enumerate(out_refs):
        for r in range(classes):
            first = (j * classes + r) * cap
            moved = jnp.dot(
                hot_ref[first : first + cap, :], rows, preferred_element_type=jnp.float32
            ).astype(jnp.bfloat16)
            for h in range(width):
                out_ref[h, r] = moved[:, h * HD : (h + 1) * HD]


def pack(slots, cosine, sine, rows, turned, chunks, classes, cap):
    count = rows.shape[0]
    heads = rows.shape[1] // HD
    width = min(2, heads)
    fixed = lambda i: (0, 0)
    total = chunks * classes * cap
    return pl.pallas_call(
        functools.partial(pack_kernel, turned, classes, cap, width),
        grid=(heads // width,),
        in_specs=[
            pl.BlockSpec((1, count), fixed),
            pl.BlockSpec((count, HD), fixed),
            pl.BlockSpec((count, HD), fixed),
            pl.BlockSpec((count, width * HD), lambda i: (0, i)),
        ],
        out_specs=[pl.BlockSpec((width, classes, cap, HD), lambda i: (i, 0, 0, 0))] * chunks,
        out_shape=[jax.ShapeDtypeStruct((heads, classes, cap, HD), jnp.bfloat16)] * chunks,
        scratch_shapes=[pltpu.VMEM((total, count), jnp.bfloat16)],
        compiler_params=params(),
        cost_estimate=pl.CostEstimate(
            flops=2 * heads * total * count * HD, bytes_accessed=count * heads * HD * 4, transcendentals=0
        ),
    )(slots, cosine, sine, rows)


def piece_rows(cap):
    return max(rows for rows in range(TILE, PAD + 1, TILE) if cap % rows == 0)


def merge_pieces(low, high, piece, source, add):
    shift = low & (TILE - 1)
    pieces = jnp.where(high > low, lax.div(high - low + shift + piece - 1, piece), 0)
    first = low - shift

    def one(i, carry):
        at = pl.multiple_of(first + i * piece, TILE)
        add(at, source(pl.multiple_of(i * piece, TILE)))
        return carry

    lax.fori_loop(0, pieces, one, 0)


def compact_kernel(offsets, per, total, doubled, member_ref, count_ref, *rest):
    parts, out, all_rows, starts = rest[:-3], rest[-3], rest[-2], rest[-1]
    members = len(parts)
    piece = piece_rows(parts[0].shape[1])
    all_rows[...] = jnp.zeros_like(all_rows)
    start = jnp.int32(0)
    for s in range(count_ref.shape[0]):
        starts[s] = start
        start = start + count_ref[s]

    def add(at, rows):
        all_rows[pl.ds(at, piece), :] += rows

    for part, offset in zip(parts, offsets):
        for z in range(per):
            source = z * members + (member_ref[0] ^ offset)
            low = starts[source]
            merge_pieces(
                low,
                low + count_ref[source],
                piece,
                lambda at: part[z, pl.ds(at, piece), :],
                add,
            )
    out[:, :HD] = all_rows[:total, :]
    out[:, HD:] = all_rows[:total, :] if doubled else jnp.ones((total, HD), jnp.bfloat16)


def compact(member, counts, parts, offsets, total, doubled):
    per = parts[0].shape[0]
    return pl.pallas_call(
        functools.partial(compact_kernel, offsets, per, total, doubled),
        in_specs=[whole_smem(), whole_smem()] + [whole_vmem()] * len(parts),
        out_specs=whole_vmem(),
        out_shape=jax.ShapeDtypeStruct((total, 2 * HD), jnp.bfloat16),
        scratch_shapes=[
            pltpu.VMEM((total + PAD, HD), jnp.bfloat16),
            pltpu.SMEM(counts.shape, jnp.int32),
        ],
        compiler_params=params(),
        cost_estimate=pl.CostEstimate(flops=total * HD * 8, bytes_accessed=total * HD * 8, transcendentals=0),
    )(member, counts, *parts)


def attend_kernel(ctx_size, block, cls_ref, count_ref, got_ref, key_ref, value_ref, out_ref,
                  query_all, query_two, scores_a, scores_b, top_a, top_b, run_max, run_acc):
    span = 2 * TOK_DEV
    pair = 2 * block
    supers = ctx_size // 2
    steps = supers * (supers + 1) // 2
    cls = cls_ref[0]
    piece = piece_rows(got_ref.shape[1])
    query_all[...] = jnp.zeros_like(query_all)

    def add(at, rows):
        query_all[pl.ds(at, piece), :] += rows

    start = jnp.int32(0)
    for s in range(ctx_size):
        end = start + count_ref[s]
        merge_pieces(
            rows_below(start, cls, block),
            rows_below(end, cls, block),
            piece,
            lambda at: got_ref[s, pl.ds(at, piece), :],
            add,
        )
        start = end

    def split(i, carry):
        rows = pl.ds(pl.multiple_of(i * pair, TILE), pair)
        scaled = query_all[rows, :].astype(jnp.float32) * exp2_scale
        high = scaled.astype(jnp.bfloat16)
        query_two[rows, :HD] = high
        query_two[rows, HD:] = (scaled - high.astype(jnp.float32)).astype(jnp.bfloat16)
        return carry

    lax.fori_loop(0, supers, split, 0)

    def row_top(found):
        return jnp.broadcast_to(jnp.max(found, axis=1, keepdims=True), (pair, HD))

    def score(scores, top, i, k):
        rows = query_two[pl.ds(pl.multiple_of(jnp.minimum(i, supers - 1) * pair, TILE), pair), :]
        keys = key_ref[pl.ds(pl.multiple_of(k * span, TILE), span), :]
        found = lax.dot_general(
            rows, keys, (((1,), (1,)), ((), ())), preferred_element_type=jnp.float32
        )
        scores[...] = found
        top[...] = row_top(found)

    def mask(scores, top):
        row = lax.broadcasted_iota(jnp.int32, (pair, span), 0)
        col = lax.broadcasted_iota(jnp.int32, (pair, span), 1)
        row = jnp.where(row >= block, row + (TOK_DEV - block), row) + cls * block
        found = jnp.where(col <= row, scores[...], masked_score)
        scores[...] = found
        top[...] = row_top(found)

    def absorb(scores, top, k):
        before = run_max[...]
        after = jnp.maximum(before, top[...])
        rescale = jnp.exp2(before - after)
        run_max[...] = after
        weights = jnp.exp2(scores[...] - jnp.concatenate([after] * (span // HD), axis=1))
        values = value_ref[pl.ds(pl.multiple_of(k * span, TILE), span), :]
        run_acc[...] = run_acc[...] * jnp.concatenate([rescale, rescale], axis=1) + jnp.dot(
            weights.astype(jnp.bfloat16), values, preferred_element_type=jnp.float32
        )

    def clear():
        run_max[...] = jnp.full_like(run_max, masked_score)
        run_acc[...] = jnp.zeros_like(run_acc)

    def one_step(now, later, i, k):
        last = k == i
        next_i = jnp.where(last, i + 1, i)
        next_k = jnp.where(last, 0, k + 1)
        score(*later, next_i, next_k)
        absorb(*now, k)

        @pl.when(last)
        def _():
            result = (run_acc[:, :HD] / run_acc[:, HD:]).astype(jnp.bfloat16)
            out_ref[2 * i] = result[:block]
            out_ref[2 * i + 1] = result[block:]
            clear()

        @pl.when(next_k == next_i)
        def _():
            mask(*later)

        return next_i, next_k

    buffers_a, buffers_b = (scores_a, top_a), (scores_b, top_b)
    clear()
    score(*buffers_a, 0, 0)
    mask(*buffers_a)

    def two_steps(t, at):
        at = one_step(buffers_a, buffers_b, *at)
        return one_step(buffers_b, buffers_a, *at)

    lax.fori_loop(0, steps // 2, two_steps, (jnp.int32(0), jnp.int32(0)))


def attend(cls, counts, got, keys, values, block):
    ctx_size = got.shape[0]
    total = keys.shape[0]
    pairs = total * ctx_size * block // 2
    return pl.pallas_call(
        functools.partial(attend_kernel, ctx_size, block),
        in_specs=[whole_smem()] * 2 + [whole_vmem()] * 3,
        out_specs=whole_vmem(),
        out_shape=jax.ShapeDtypeStruct((ctx_size, block, HD), jnp.bfloat16),
        scratch_shapes=[
            pltpu.VMEM((ctx_size * block + PAD, HD), jnp.bfloat16),
            pltpu.VMEM((ctx_size * block, 2 * HD), jnp.bfloat16),
            pltpu.VMEM((2 * block, 2 * TOK_DEV), jnp.float32),
            pltpu.VMEM((2 * block, 2 * TOK_DEV), jnp.float32),
            pltpu.VMEM((2 * block, HD), jnp.float32),
            pltpu.VMEM((2 * block, HD), jnp.float32),
            pltpu.VMEM((2 * block, HD), jnp.float32),
            pltpu.VMEM((2 * block, 2 * HD), jnp.float32),
        ],
        compiler_params=params(),
        cost_estimate=pl.CostEstimate(
            flops=pairs * 8 * HD, bytes_accessed=total * HD * 8, transcendentals=pairs
        ),
    )(cls, counts, got, keys, values)


def project_kernel(classes, column_ref, got_ref, weight_ref, out_ref, rows_ref):
    block = got_ref.shape[1]

    @pl.when(pl.program_id(0) == 0)
    def _():
        for d in range(got_ref.shape[0]):
            h, r = d // classes, d % classes
            rows_ref[r * block : (r + 1) * block, h * HD : (h + 1) * HD] = got_ref[d]

    out_ref[...] = jnp.dot(
        rows_ref[...], weight_ref[...], preferred_element_type=jnp.float32
    ).astype(jnp.bfloat16)


def project(first_column, got, weight, columns, classes):
    ctx_size, block, _ = got.shape
    rows, depth = classes * block, weight.shape[0]
    step = min(512, columns)
    return pl.pallas_call(
        functools.partial(project_kernel, classes),
        grid_spec=pltpu.PrefetchScalarGridSpec(
            num_scalar_prefetch=1,
            grid=(columns // step,),
            in_specs=[
                pl.BlockSpec((ctx_size, block, HD), lambda i, first: (0, 0, 0)),
                pl.BlockSpec((depth, step), lambda i, first: (0, first[0] + i)),
            ],
            out_specs=pl.BlockSpec((rows, step), lambda i, first: (0, i)),
            scratch_shapes=[pltpu.VMEM((rows, depth), jnp.bfloat16)],
        ),
        out_shape=jax.ShapeDtypeStruct((rows, columns), jnp.bfloat16),
        compiler_params=params(),
        cost_estimate=pl.CostEstimate(
            flops=2 * rows * depth * columns, bytes_accessed=2 * depth * columns, transcendentals=0
        ),
    )((first_column // step).astype(jnp.int32).reshape(1), got, weight)


def tables(query_rows):
    half_dim = HD // 2
    positions = lax.axis_index("ctx") * query_rows + jnp.arange(query_rows, dtype=jnp.int32)
    lane = jnp.arange(HD, dtype=jnp.int32)
    pair_id = jnp.where(lane < half_dim, lane, lane - half_dim)
    inv_freq = rope_base ** (-(pair_id.astype(jnp.float32) * 2.0 / HD))
    angles = positions.astype(jnp.float32)[:, None] * inv_freq[None, :]
    sine = jnp.sin(angles)
    return jnp.cos(angles), jnp.where(lane[None, :] < half_dim, -sine, sine)


def local(query, key, value, keep_rank, kept_count, out_weight):
    ctx_size = lax.axis_size("ctx")
    tp_size = lax.axis_size("tp")
    me = lax.axis_index("ctx")
    tp_me = lax.axis_index("tp")
    orig_rows = query.shape[0]
    heads = query.shape[1] // HD
    kv_heads = key.shape[1] // HD
    members = ctx_size // kv_heads
    classes = ctx_size // heads
    chunks = CHUNKS if classes == 1 else 1
    block = TOK_DEV // (chunks * classes)
    total = ctx_size * TOK_DEV
    reach = orig_rows // TOK_DEV
    cap = reach * block + TILE
    cap_kv = orig_rows + TILE
    columns = out_weight.shape[1] // tp_size

    kv_slots, q_slots = find_slots(
        me.reshape(1), kept_count, keep_rank, reach, chunks * classes, block, cap
    )
    cosine, sine = tables(orig_rows)

    across = [[z * members + m for z in range(kv_heads)] for m in range(members)]

    def spread(rows, turned):
        (packed,) = pack(kv_slots, cosine, sine, rows, turned, 1, 1, cap_kv)
        packed = packed.reshape(kv_heads, cap_kv, HD)
        if kv_heads > 1:
            packed = lax.all_to_all(
                packed, "ctx", split_axis=0, concat_axis=0, tiled=True, axis_index_groups=across
            )
        parts, offsets = [packed], [0]
        bit = members // 2
        while bit >= 1:
            swap = [(d, d ^ bit) for d in range(ctx_size)]
            parts = parts + [lax.ppermute(part, "ctx", swap) for part in parts]
            offsets = offsets + [offset ^ bit for offset in offsets]
            bit //= 2
        return compact((me & (members - 1)).reshape(1), kept_count, parts, offsets, total, turned)

    keys = spread(key, True)
    values = spread(value, False)
    packed_q = pack(q_slots, cosine, sine, query, True, chunks, classes, cap)
    got_q = [
        lax.all_to_all(
            one.reshape(ctx_size, cap, HD), "ctx", split_axis=0, concat_axis=0, tiled=True
        )
        for one in packed_q
    ]

    mine, other = [], []
    for j in range(chunks):
        cls_j = j * classes + (me & (classes - 1))
        done = attend(cls_j.reshape(1), kept_count, got_q[j], keys, values, block)
        got = lax.all_to_all(done, "ctx", split_axis=0, concat_axis=0, tiled=True)
        if tp_size == 2:
            theirs = project((1 - tp_me) * columns, got, out_weight, columns, classes)
            other.append(lax.ppermute(theirs, "tp", [(0, 1), (1, 0)]))
            mine.append(project(tp_me * columns, got, out_weight, columns, classes))
        else:
            full = project(jnp.int32(0) * tp_me, got, out_weight, columns * tp_size, classes)
            split = jnp.transpose(full.reshape(full.shape[0], tp_size, columns), (1, 0, 2))
            swapped = lax.all_to_all(split, "tp", split_axis=0, concat_axis=0, tiled=True)
            mine.append(jnp.sum(swapped.astype(jnp.float32), axis=0))
            other.append(jnp.zeros((), jnp.float32))
    return jnp.concatenate(
        [
            (a.astype(jnp.float32) + b.astype(jnp.float32)).astype(jnp.bfloat16)
            for a, b in zip(mine, other)
        ],
        axis=0,
    )


def solution(mesh):
    placed = (P("ctx", "tp"), P("ctx", "tp"), P("ctx", "tp"), P("ctx", None), P(), P("tp", None))
    return jax.shard_map(
        local, mesh=mesh, in_specs=placed, out_specs=P("ctx", "tp"), check_vma=False
    )
```

```python
import functools
import math

import jax
import jax.numpy as jnp
from jax import lax
from jax.experimental import pallas as pl
from jax.experimental.pallas import tpu as pltpu
from jax.sharding import PartitionSpec as P

HD = 128
TOK_DEV = 384
TILE = 16
PAD = 128
CHUNKS = 2

rope_base = 1000000.0
masked_score = -1e30
exp2_scale = math.log2(math.e) / math.sqrt(HD)
VMEM_BYTES = 58 * 1024 * 1024


def whole_vmem():
    return pl.BlockSpec(memory_space=pltpu.VMEM)


def whole_smem():
    return pl.BlockSpec(memory_space=pltpu.SMEM)


def params():
    return pltpu.CompilerParams(vmem_limit_bytes=VMEM_BYTES)


def turn(rows, cosine, sine):
    as_float = rows.astype(jnp.float32)
    swapped = pltpu.roll(as_float, HD // 2, 1)
    return (as_float * cosine + swapped * sine).astype(jnp.bfloat16)


def rows_below(start, cls, block):
    whole = lax.div(start, TOK_DEV)
    return whole * block + jnp.clip(start - whole * TOK_DEV - cls * block, 0, block)


def slots_kernel(reach, groups, block, cap, me_ref, count_ref, rank_ref, kv_out, q_out):
    me = me_ref[0]
    rows = rank_ref.shape[1]
    start = jnp.int32(0)
    for s in range(count_ref.shape[0]):
        start = start + jnp.where(s < me, count_ref[s], 0)
    kept = rank_ref[...] < count_ref[me]
    upper = lax.broadcasted_iota(jnp.int32, (rows, rows), 0) <= lax.broadcasted_iota(
        jnp.int32, (rows, rows), 1
    )
    flags = jnp.broadcast_to(kept.astype(jnp.float32), (8, rows)).astype(jnp.bfloat16)
    order = (
        jnp.dot(
            flags, upper.astype(jnp.float32).astype(jnp.bfloat16), preferred_element_type=jnp.float32
        )[:1].astype(jnp.int32)
        - 1
    )
    kv_out[...] = jnp.where(kept, order + (start & (TILE - 1)), -1)
    place = start + order
    first = lax.div(start, TOK_DEV)
    device = first + jnp.zeros_like(place)
    for step in range(1, reach + 1):
        device = device + (place >= (first + step) * TOK_DEV).astype(jnp.int32)
    within = place - device * TOK_DEV
    cls = jnp.zeros_like(place)
    for step in range(1, groups):
        cls = cls + (within >= step * block).astype(jnp.int32)
    low = first * block + jnp.clip(start - first * TOK_DEV - cls * block, 0, block)
    slot = cls * cap + device * block + within - cls * block - low + (low & (TILE - 1))
    q_out[...] = jnp.where(kept, slot, -1)


def find_slots(me, counts, ranks, reach, groups, block, cap):
    shape = jax.ShapeDtypeStruct(ranks.shape, jnp.int32)
    return pl.pallas_call(
        functools.partial(slots_kernel, reach, groups, block, cap),
        in_specs=[whole_smem(), whole_smem(), whole_vmem()],
        out_specs=[whole_vmem()] * 2,
        out_shape=[shape, shape],
        compiler_params=params(),
        cost_estimate=pl.CostEstimate(flops=2**20, bytes_accessed=2**14, transcendentals=0),
    )(me, counts, ranks)


def pack_kernel(turned, classes, cap, width, slot_ref, cos_ref, sin_ref, row_ref, *rest):
    out_refs, hot_ref = rest[:-1], rest[-1]

    @pl.when(pl.program_id(0) == 0)
    def _():
        ids = lax.broadcasted_iota(jnp.int32, hot_ref.shape, 0)
        hot_ref[...] = (ids == slot_ref[...]).astype(jnp.float32).astype(jnp.bfloat16)

    if turned:
        rows = jnp.concatenate(
            [
                turn(row_ref[:, h * HD : (h + 1) * HD], cos_ref[...], sin_ref[...])
                for h in range(width)
            ],
            axis=1,
        )
    else:
        rows = row_ref[...]
    for j, out_ref in enumerate(out_refs):
        for r in range(classes):
            first = (j * classes + r) * cap
            moved = jnp.dot(
                hot_ref[first : first + cap, :], rows, preferred_element_type=jnp.float32
            ).astype(jnp.bfloat16)
            for h in range(width):
                out_ref[h, r] = moved[:, h * HD : (h + 1) * HD]


def pack(slots, cosine, sine, rows, turned, chunks, classes, cap):
    count = rows.shape[0]
    heads = rows.shape[1] // HD
    width = min(2, heads)
    fixed = lambda i: (0, 0)
    total = chunks * classes * cap
    return pl.pallas_call(
        functools.partial(pack_kernel, turned, classes, cap, width),
        grid=(heads // width,),
        in_specs=[
            pl.BlockSpec((1, count), fixed),
            pl.BlockSpec((count, HD), fixed),
            pl.BlockSpec((count, HD), fixed),
            pl.BlockSpec((count, width * HD), lambda i: (0, i)),
        ],
        out_specs=[pl.BlockSpec((width, classes, cap, HD), lambda i: (i, 0, 0, 0))] * chunks,
        out_shape=[jax.ShapeDtypeStruct((heads, classes, cap, HD), jnp.bfloat16)] * chunks,
        scratch_shapes=[pltpu.VMEM((total, count), jnp.bfloat16)],
        compiler_params=params(),
        cost_estimate=pl.CostEstimate(
            flops=2 * heads * total * count * HD, bytes_accessed=count * heads * HD * 4, transcendentals=0
        ),
    )(slots, cosine, sine, rows)


def piece_rows(cap):
    return max(rows for rows in range(TILE, PAD + 1, TILE) if cap % rows == 0)


def merge_pieces(low, high, piece, source, add):
    shift = low & (TILE - 1)
    pieces = jnp.where(high > low, lax.div(high - low + shift + piece - 1, piece), 0)
    first = low - shift

    def one(i, carry):
        at = pl.multiple_of(first + i * piece, TILE)
        add(at, source(pl.multiple_of(i * piece, TILE)))
        return carry

    lax.fori_loop(0, pieces, one, 0)


def compact_kernel(offsets, per, total, doubled, member_ref, count_ref, *rest):
    parts, out, all_rows, starts = rest[:-3], rest[-3], rest[-2], rest[-1]
    members = len(parts)
    piece = piece_rows(parts[0].shape[1])
    all_rows[...] = jnp.zeros_like(all_rows)
    start = jnp.int32(0)
    for s in range(count_ref.shape[0]):
        starts[s] = start
        start = start + count_ref[s]

    def add(at, rows):
        all_rows[pl.ds(at, piece), :] += rows

    for part, offset in zip(parts, offsets):
        for z in range(per):
            source = z * members + (member_ref[0] ^ offset)
            low = starts[source]
            merge_pieces(
                low,
                low + count_ref[source],
                piece,
                lambda at: part[z, pl.ds(at, piece), :],
                add,
            )
    out[:, :HD] = all_rows[:total, :]
    out[:, HD:] = all_rows[:total, :] if doubled else jnp.ones((total, HD), jnp.bfloat16)


def compact(member, counts, parts, offsets, total, doubled):
    per = parts[0].shape[0]
    return pl.pallas_call(
        functools.partial(compact_kernel, offsets, per, total, doubled),
        in_specs=[whole_smem(), whole_smem()] + [whole_vmem()] * len(parts),
        out_specs=whole_vmem(),
        out_shape=jax.ShapeDtypeStruct((total, 2 * HD), jnp.bfloat16),
        scratch_shapes=[
            pltpu.VMEM((total + PAD, HD), jnp.bfloat16),
            pltpu.SMEM(counts.shape, jnp.int32),
        ],
        compiler_params=params(),
        cost_estimate=pl.CostEstimate(flops=total * HD * 8, bytes_accessed=total * HD * 8, transcendentals=0),
    )(member, counts, *parts)


def attend_kernel(ctx_size, block, cls_ref, count_ref, got_ref, key_ref, value_ref, out_ref,
                  query_all, query_two, scores_a, scores_b, top_a, top_b, run_max, run_acc):
    span = 2 * TOK_DEV
    pair = 2 * block
    supers = ctx_size // 2
    steps = supers * (supers + 1) // 2
    cls = cls_ref[0]
    piece = piece_rows(got_ref.shape[1])
    query_all[...] = jnp.zeros_like(query_all)

    def add(at, rows):
        query_all[pl.ds(at, piece), :] += rows

    start = jnp.int32(0)
    for s in range(ctx_size):
        end = start + count_ref[s]
        merge_pieces(
            rows_below(start, cls, block),
            rows_below(end, cls, block),
            piece,
            lambda at: got_ref[s, pl.ds(at, piece), :],
            add,
        )
        start = end

    def split(i, carry):
        rows = pl.ds(pl.multiple_of(i * pair, TILE), pair)
        scaled = query_all[rows, :].astype(jnp.float32) * exp2_scale
        high = scaled.astype(jnp.bfloat16)
        query_two[rows, :HD] = high
        query_two[rows, HD:] = (scaled - high.astype(jnp.float32)).astype(jnp.bfloat16)
        return carry

    lax.fori_loop(0, supers, split, 0)

    def row_top(found):
        return jnp.broadcast_to(jnp.max(found, axis=1, keepdims=True), (pair, HD))

    def score(scores, top, i, k):
        rows = query_two[pl.ds(pl.multiple_of(jnp.minimum(i, supers - 1) * pair, TILE), pair), :]
        keys = key_ref[pl.ds(pl.multiple_of(k * span, TILE), span), :]
        found = lax.dot_general(
            rows, keys, (((1,), (1,)), ((), ())), preferred_element_type=jnp.float32
        )
        scores[...] = found
        top[...] = row_top(found)

    def mask(scores, top):
        row = lax.broadcasted_iota(jnp.int32, (pair, span), 0)
        col = lax.broadcasted_iota(jnp.int32, (pair, span), 1)
        row = jnp.where(row >= block, row + (TOK_DEV - block), row) + cls * block
        found = jnp.where(col <= row, scores[...], masked_score)
        scores[...] = found
        top[...] = row_top(found)

    def absorb(scores, top, k):
        before = run_max[...]
        after = jnp.maximum(before, top[...])
        rescale = jnp.exp2(before - after)
        run_max[...] = after
        weights = jnp.exp2(scores[...] - jnp.concatenate([after] * (span // HD), axis=1))
        values = value_ref[pl.ds(pl.multiple_of(k * span, TILE), span), :]
        run_acc[...] = run_acc[...] * jnp.concatenate([rescale, rescale], axis=1) + jnp.dot(
            weights.astype(jnp.bfloat16), values, preferred_element_type=jnp.float32
        )

    def clear():
        run_max[...] = jnp.full_like(run_max, masked_score)
        run_acc[...] = jnp.zeros_like(run_acc)

    def one_step(now, later, i, k):
        last = k == i
        next_i = jnp.where(last, i + 1, i)
        next_k = jnp.where(last, 0, k + 1)
        score(*later, next_i, next_k)
        absorb(*now, k)

        @pl.when(last)
        def _():
            result = (run_acc[:, :HD] / run_acc[:, HD:]).astype(jnp.bfloat16)
            out_ref[2 * i] = result[:block]
            out_ref[2 * i + 1] = result[block:]
            clear()

        @pl.when(next_k == next_i)
        def _():
            mask(*later)

        return next_i, next_k

    buffers_a, buffers_b = (scores_a, top_a), (scores_b, top_b)
    clear()
    score(*buffers_a, 0, 0)
    mask(*buffers_a)

    def two_steps(t, at):
        at = one_step(buffers_a, buffers_b, *at)
        return one_step(buffers_b, buffers_a, *at)

    lax.fori_loop(0, steps // 2, two_steps, (jnp.int32(0), jnp.int32(0)))


def attend(cls, counts, got, keys, values, block):
    ctx_size = got.shape[0]
    total = keys.shape[0]
    pairs = total * ctx_size * block // 2
    return pl.pallas_call(
        functools.partial(attend_kernel, ctx_size, block),
        in_specs=[whole_smem()] * 2 + [whole_vmem()] * 3,
        out_specs=whole_vmem(),
        out_shape=jax.ShapeDtypeStruct((ctx_size, block, HD), jnp.bfloat16),
        scratch_shapes=[
            pltpu.VMEM((ctx_size * block + PAD, HD), jnp.bfloat16),
            pltpu.VMEM((ctx_size * block, 2 * HD), jnp.bfloat16),
            pltpu.VMEM((2 * block, 2 * TOK_DEV), jnp.float32),
            pltpu.VMEM((2 * block, 2 * TOK_DEV), jnp.float32),
            pltpu.VMEM((2 * block, HD), jnp.float32),
            pltpu.VMEM((2 * block, HD), jnp.float32),
            pltpu.VMEM((2 * block, HD), jnp.float32),
            pltpu.VMEM((2 * block, 2 * HD), jnp.float32),
        ],
        compiler_params=params(),
        cost_estimate=pl.CostEstimate(
            flops=pairs * 8 * HD, bytes_accessed=total * HD * 8, transcendentals=pairs
        ),
    )(cls, counts, got, keys, values)


def project_kernel(classes, column_ref, got_ref, weight_ref, out_ref, rows_ref):
    block = got_ref.shape[1]

    @pl.when(pl.program_id(0) == 0)
    def _():
        for d in range(got_ref.shape[0]):
            h, r = d // classes, d % classes
            rows_ref[r * block : (r + 1) * block, h * HD : (h + 1) * HD] = got_ref[d]

    out_ref[...] = jnp.dot(
        rows_ref[...], weight_ref[...], preferred_element_type=jnp.float32
    ).astype(jnp.bfloat16)


def project(first_column, got, weight, columns, classes):
    ctx_size, block, _ = got.shape
    rows, depth = classes * block, weight.shape[0]
    step = min(512, columns)
    return pl.pallas_call(
        functools.partial(project_kernel, classes),
        grid_spec=pltpu.PrefetchScalarGridSpec(
            num_scalar_prefetch=1,
            grid=(columns // step,),
            in_specs=[
                pl.BlockSpec((ctx_size, block, HD), lambda i, first: (0, 0, 0)),
                pl.BlockSpec((depth, step), lambda i, first: (0, first[0] + i)),
            ],
            out_specs=pl.BlockSpec((rows, step), lambda i, first: (0, i)),
            scratch_shapes=[pltpu.VMEM((rows, depth), jnp.bfloat16)],
        ),
        out_shape=jax.ShapeDtypeStruct((rows, columns), jnp.bfloat16),
        compiler_params=params(),
        cost_estimate=pl.CostEstimate(
            flops=2 * rows * depth * columns, bytes_accessed=2 * depth * columns, transcendentals=0
        ),
    )((first_column // step).astype(jnp.int32).reshape(1), got, weight)


def tables(query_rows):
    half_dim = HD // 2
    positions = lax.axis_index("ctx") * query_rows + jnp.arange(query_rows, dtype=jnp.int32)
    lane = jnp.arange(HD, dtype=jnp.int32)
    pair_id = jnp.where(lane < half_dim, lane, lane - half_dim)
    inv_freq = rope_base ** (-(pair_id.astype(jnp.float32) * 2.0 / HD))
    angles = positions.astype(jnp.float32)[:, None] * inv_freq[None, :]
    sine = jnp.sin(angles)
    return jnp.cos(angles), jnp.where(lane[None, :] < half_dim, -sine, sine)


def local(query, key, value, keep_rank, kept_count, out_weight):
    ctx_size = lax.axis_size("ctx")
    tp_size = lax.axis_size("tp")
    me = lax.axis_index("ctx")
    tp_me = lax.axis_index("tp")
    orig_rows = query.shape[0]
    heads = query.shape[1] // HD
    kv_heads = key.shape[1] // HD
    members = ctx_size // kv_heads
    classes = ctx_size // heads
    chunks = CHUNKS if classes == 1 else 1
    block = TOK_DEV // (chunks * classes)
    total = ctx_size * TOK_DEV
    reach = orig_rows // TOK_DEV
    cap = reach * block + TILE
    cap_kv = orig_rows + TILE
    columns = out_weight.shape[1] // tp_size

    kv_slots, q_slots = find_slots(
        me.reshape(1), kept_count, keep_rank, reach, chunks * classes, block, cap
    )
    cosine, sine = tables(orig_rows)

    across = [[z * members + m for z in range(kv_heads)] for m in range(members)]

    member = (me & (members - 1)).reshape(1)

    def pack_shared(rows, turned):
        (packed,) = pack(kv_slots, cosine, sine, rows, turned, 1, 1, cap_kv)
        return packed.reshape(kv_heads, cap_kv, HD)

    def send_across(packed):
        if kv_heads == 1:
            return packed
        return lax.all_to_all(
            packed, "ctx", split_axis=0, concat_axis=0, tiled=True, axis_index_groups=across
        )

    def swap(parts, bit):
        pairs = [(d, d ^ bit) for d in range(ctx_size)]
        return parts + [lax.ppermute(part, "ctx", pairs) for part in parts]

    bits = [members >> n for n in range(1, members.bit_length())]
    offsets = [0]
    for bit in bits:
        offsets = offsets + [offset ^ bit for offset in offsets]

    def send_query(packed):
        return lax.all_to_all(
            packed.reshape(ctx_size, cap, HD), "ctx", split_axis=0, concat_axis=0, tiled=True
        )

    key_parts = [send_across(pack_shared(key, True))]
    value_packed, key_parts = lax.optimization_barrier((pack_shared(value, False), key_parts))
    key_parts = swap(key_parts, bits[0])
    value_parts = [send_across(value_packed)]
    packed_q = list(pack(q_slots, cosine, sine, query, True, chunks, classes, cap))
    packed_q[0], key_parts, value_parts = lax.optimization_barrier(
        (packed_q[0], key_parts, value_parts)
    )
    got_q = [send_query(packed_q[0])]
    value_parts = swap(value_parts, bits[0])
    for bit in bits[1:]:
        key_parts = swap(key_parts, bit)
    if chunks > 1:
        packed_q[1], key_parts, value_parts = lax.optimization_barrier(
            (packed_q[1], key_parts, value_parts)
        )
    for bit in bits[1:]:
        value_parts = swap(value_parts, bit)
    got_q = got_q + [send_query(packed) for packed in packed_q[1:]]
    keys = compact(member, kept_count, key_parts, offsets, total, True)
    values = compact(member, kept_count, value_parts, offsets, total, False)

    mine, other = [], []
    for j in range(chunks):
        cls_j = j * classes + (me & (classes - 1))
        done = attend(cls_j.reshape(1), kept_count, got_q[j], keys, values, block)
        got = lax.all_to_all(done, "ctx", split_axis=0, concat_axis=0, tiled=True)
        if tp_size == 2:
            theirs = project((1 - tp_me) * columns, got, out_weight, columns, classes)
            other.append(lax.ppermute(theirs, "tp", [(0, 1), (1, 0)]))
            mine.append(project(tp_me * columns, got, out_weight, columns, classes))
        else:
            full = project(jnp.int32(0) * tp_me, got, out_weight, columns * tp_size, classes)
            split = jnp.transpose(full.reshape(full.shape[0], tp_size, columns), (1, 0, 2))
            swapped = lax.all_to_all(split, "tp", split_axis=0, concat_axis=0, tiled=True)
            mine.append(jnp.sum(swapped.astype(jnp.float32), axis=0))
            other.append(jnp.zeros((), jnp.float32))
    return jnp.concatenate(
        [
            (a.astype(jnp.float32) + b.astype(jnp.float32)).astype(jnp.bfloat16)
            for a, b in zip(mine, other)
        ],
        axis=0,
    )


def solution(mesh):
    placed = (P("ctx", "tp"), P("ctx", "tp"), P("ctx", "tp"), P("ctx", None), P(), P("tp", None))
    return jax.shard_map(
        local, mesh=mesh, in_specs=placed, out_specs=P("ctx", "tp"), check_vma=False
    )
```

```python
import functools
import math

import jax
import jax.numpy as jnp
from jax import lax
from jax.experimental import pallas as pl
from jax.experimental.pallas import tpu as pltpu
from jax.sharding import PartitionSpec as P

HD = 128
TOK_DEV = 384
TILE = 16
PAD = 128
CHUNKS = 2

rope_base = 1000000.0
masked_score = -1e30
exp2_scale = math.log2(math.e) / math.sqrt(HD)
VMEM_BYTES = 58 * 1024 * 1024


def whole_vmem():
    return pl.BlockSpec(memory_space=pltpu.VMEM)


def whole_smem():
    return pl.BlockSpec(memory_space=pltpu.SMEM)


def params():
    return pltpu.CompilerParams(vmem_limit_bytes=VMEM_BYTES)


def turn(rows, cosine, sine):
    as_float = rows.astype(jnp.float32)
    swapped = pltpu.roll(as_float, HD // 2, 1)
    return (as_float * cosine + swapped * sine).astype(jnp.bfloat16)


def rows_below(start, cls, block):
    whole = lax.div(start, TOK_DEV)
    return whole * block + jnp.clip(start - whole * TOK_DEV - cls * block, 0, block)


def slots_kernel(reach, groups, block, cap, me_ref, count_ref, rank_ref, kv_out, q_out):
    me = me_ref[0]
    rows = rank_ref.shape[1]
    start = jnp.int32(0)
    for s in range(count_ref.shape[0]):
        start = start + jnp.where(s < me, count_ref[s], 0)
    kept = rank_ref[...] < count_ref[me]
    upper = lax.broadcasted_iota(jnp.int32, (rows, rows), 0) <= lax.broadcasted_iota(
        jnp.int32, (rows, rows), 1
    )
    flags = jnp.broadcast_to(kept.astype(jnp.float32), (8, rows)).astype(jnp.bfloat16)
    order = (
        jnp.dot(
            flags, upper.astype(jnp.float32).astype(jnp.bfloat16), preferred_element_type=jnp.float32
        )[:1].astype(jnp.int32)
        - 1
    )
    kv_out[...] = jnp.where(kept, order + (start & (TILE - 1)), -1)
    place = start + order
    first = lax.div(start, TOK_DEV)
    device = first + jnp.zeros_like(place)
    for step in range(1, reach + 1):
        device = device + (place >= (first + step) * TOK_DEV).astype(jnp.int32)
    within = place - device * TOK_DEV
    cls = jnp.zeros_like(place)
    for step in range(1, groups):
        cls = cls + (within >= step * block).astype(jnp.int32)
    low = first * block + jnp.clip(start - first * TOK_DEV - cls * block, 0, block)
    slot = cls * cap + device * block + within - cls * block - low + (low & (TILE - 1))
    q_out[...] = jnp.where(kept, slot, -1)


def find_slots(me, counts, ranks, reach, groups, block, cap):
    shape = jax.ShapeDtypeStruct(ranks.shape, jnp.int32)
    return pl.pallas_call(
        functools.partial(slots_kernel, reach, groups, block, cap),
        in_specs=[whole_smem(), whole_smem(), whole_vmem()],
        out_specs=[whole_vmem()] * 2,
        out_shape=[shape, shape],
        compiler_params=params(),
        cost_estimate=pl.CostEstimate(flops=2**20, bytes_accessed=2**14, transcendentals=0),
    )(me, counts, ranks)


def pack_kernel(turned, classes, cap, width, slot_ref, cos_ref, sin_ref, row_ref, *rest):
    out_refs, hot_ref = rest[:-1], rest[-1]

    @pl.when(pl.program_id(0) == 0)
    def _():
        ids = lax.broadcasted_iota(jnp.int32, hot_ref.shape, 0)
        hot_ref[...] = (ids == slot_ref[...]).astype(jnp.float32).astype(jnp.bfloat16)

    if turned:
        rows = jnp.concatenate(
            [
                turn(row_ref[:, h * HD : (h + 1) * HD], cos_ref[...], sin_ref[...])
                for h in range(width)
            ],
            axis=1,
        )
    else:
        rows = row_ref[...]
    for j, out_ref in enumerate(out_refs):
        for r in range(classes):
            first = (j * classes + r) * cap
            moved = jnp.dot(
                hot_ref[first : first + cap, :], rows, preferred_element_type=jnp.float32
            ).astype(jnp.bfloat16)
            for h in range(width):
                out_ref[h, r] = moved[:, h * HD : (h + 1) * HD]


def pack(slots, cosine, sine, rows, turned, chunks, classes, cap):
    count = rows.shape[0]
    heads = rows.shape[1] // HD
    width = min(2, heads)
    fixed = lambda i: (0, 0)
    total = chunks * classes * cap
    return pl.pallas_call(
        functools.partial(pack_kernel, turned, classes, cap, width),
        grid=(heads // width,),
        in_specs=[
            pl.BlockSpec((1, count), fixed),
            pl.BlockSpec((count, HD), fixed),
            pl.BlockSpec((count, HD), fixed),
            pl.BlockSpec((count, width * HD), lambda i: (0, i)),
        ],
        out_specs=[pl.BlockSpec((width, classes, cap, HD), lambda i: (i, 0, 0, 0))] * chunks,
        out_shape=[jax.ShapeDtypeStruct((heads, classes, cap, HD), jnp.bfloat16)] * chunks,
        scratch_shapes=[pltpu.VMEM((total, count), jnp.bfloat16)],
        compiler_params=params(),
        cost_estimate=pl.CostEstimate(
            flops=2 * heads * total * count * HD, bytes_accessed=count * heads * HD * 4, transcendentals=0
        ),
    )(slots, cosine, sine, rows)


def piece_rows(cap):
    return max(rows for rows in range(TILE, PAD + 1, TILE) if cap % rows == 0)


def merge_pieces(low, high, piece, source, add):
    shift = low & (TILE - 1)
    pieces = jnp.where(high > low, lax.div(high - low + shift + piece - 1, piece), 0)
    first = low - shift

    def one(i, carry):
        at = pl.multiple_of(first + i * piece, TILE)
        add(at, source(pl.multiple_of(i * piece, TILE)))
        return carry

    lax.fori_loop(0, pieces, one, 0)


def compact_kernel(offsets, per, total, doubled, member_ref, count_ref, *rest):
    parts, out, all_rows, starts = rest[:-3], rest[-3], rest[-2], rest[-1]
    members = len(parts)
    piece = piece_rows(parts[0].shape[1])
    all_rows[...] = jnp.zeros_like(all_rows)
    start = jnp.int32(0)
    for s in range(count_ref.shape[0]):
        starts[s] = start
        start = start + count_ref[s]

    def add(at, rows):
        all_rows[pl.ds(at, piece), :] += rows

    for part, offset in zip(parts, offsets):
        for z in range(per):
            source = z * members + (member_ref[0] ^ offset)
            low = starts[source]
            merge_pieces(
                low,
                low + count_ref[source],
                piece,
                lambda at: part[z, pl.ds(at, piece), :],
                add,
            )
    if doubled:
        for first in range(0, total, 2 * TOK_DEV):
            turned = jnp.transpose(all_rows[first : first + 2 * TOK_DEV, :])
            out[:HD, first : first + 2 * TOK_DEV] = turned
            out[HD:, first : first + 2 * TOK_DEV] = turned
    else:
        out[:, :HD] = all_rows[:total, :]
        out[:, HD:] = jnp.ones((total, HD), jnp.bfloat16)


def compact(member, counts, parts, offsets, total, doubled):
    per = parts[0].shape[0]
    return pl.pallas_call(
        functools.partial(compact_kernel, offsets, per, total, doubled),
        in_specs=[whole_smem(), whole_smem()] + [whole_vmem()] * len(parts),
        out_specs=whole_vmem(),
        out_shape=jax.ShapeDtypeStruct(
            (2 * HD, total) if doubled else (total, 2 * HD), jnp.bfloat16
        ),
        scratch_shapes=[
            pltpu.VMEM((total + PAD, HD), jnp.bfloat16),
            pltpu.SMEM(counts.shape, jnp.int32),
        ],
        compiler_params=params(),
        cost_estimate=pl.CostEstimate(flops=total * HD * 8, bytes_accessed=total * HD * 8, transcendentals=0),
    )(member, counts, *parts)


def attend_kernel(ctx_size, block, cls_ref, count_ref, got_ref, key_ref, value_ref, out_ref,
                  query_all, query_two, scores_a, scores_b, top_a, top_b, run_max, run_acc):
    span = 2 * TOK_DEV
    pair = 2 * block
    supers = ctx_size // 2
    steps = supers * (supers + 1) // 2
    cls = cls_ref[0]
    piece = piece_rows(got_ref.shape[1])
    query_all[...] = jnp.zeros_like(query_all)

    def add(at, rows):
        query_all[pl.ds(at, piece), :] += rows

    start = jnp.int32(0)
    for s in range(ctx_size):
        end = start + count_ref[s]
        merge_pieces(
            rows_below(start, cls, block),
            rows_below(end, cls, block),
            piece,
            lambda at: got_ref[s, pl.ds(at, piece), :],
            add,
        )
        start = end

    def split(i, carry):
        rows = pl.ds(pl.multiple_of(i * pair, TILE), pair)
        scaled = query_all[rows, :].astype(jnp.float32) * exp2_scale
        high = scaled.astype(jnp.bfloat16)
        query_two[rows, :HD] = high
        query_two[rows, HD:] = (scaled - high.astype(jnp.float32)).astype(jnp.bfloat16)
        return carry

    lax.fori_loop(0, supers, split, 0)

    def row_top(found):
        return jnp.broadcast_to(jnp.max(found, axis=1, keepdims=True), (pair, HD))

    def score(scores, top, i, k):
        rows = query_two[pl.ds(pl.multiple_of(jnp.minimum(i, supers - 1) * pair, TILE), pair), :]
        keys = key_ref[:, pl.ds(pl.multiple_of(k * span, HD), span)]
        found = jnp.dot(rows, keys, preferred_element_type=jnp.float32)
        scores[...] = found
        top[...] = row_top(found)

    def mask(scores, top):
        row = lax.broadcasted_iota(jnp.int32, (pair, span), 0)
        col = lax.broadcasted_iota(jnp.int32, (pair, span), 1)
        row = jnp.where(row >= block, row + (TOK_DEV - block), row) + cls * block
        found = jnp.where(col <= row, scores[...], masked_score)
        scores[...] = found
        top[...] = row_top(found)

    def absorb(scores, top, k):
        before = run_max[...]
        after = jnp.maximum(before, top[...])
        rescale = jnp.exp2(before - after)
        run_max[...] = after
        weights = jnp.exp2(scores[...] - jnp.concatenate([after] * (span // HD), axis=1))
        values = value_ref[pl.ds(pl.multiple_of(k * span, TILE), span), :]
        run_acc[...] = run_acc[...] * jnp.concatenate([rescale, rescale], axis=1) + jnp.dot(
            weights.astype(jnp.bfloat16), values, preferred_element_type=jnp.float32
        )

    def clear():
        run_max[...] = jnp.full_like(run_max, masked_score)
        run_acc[...] = jnp.zeros_like(run_acc)

    def one_step(now, later, i, k):
        last = k == i
        next_i = jnp.where(last, i + 1, i)
        next_k = jnp.where(last, 0, k + 1)
        score(*later, next_i, next_k)
        absorb(*now, k)

        @pl.when(last)
        def _():
            result = (run_acc[:, :HD] / run_acc[:, HD:]).astype(jnp.bfloat16)
            out_ref[2 * i] = result[:block]
            out_ref[2 * i + 1] = result[block:]
            clear()

        @pl.when(next_k == next_i)
        def _():
            mask(*later)

        return next_i, next_k

    buffers_a, buffers_b = (scores_a, top_a), (scores_b, top_b)
    clear()
    score(*buffers_a, 0, 0)
    mask(*buffers_a)

    def two_steps(t, at):
        at = one_step(buffers_a, buffers_b, *at)
        return one_step(buffers_b, buffers_a, *at)

    lax.fori_loop(0, steps // 2, two_steps, (jnp.int32(0), jnp.int32(0)))


def attend(cls, counts, got, keys, values, block):
    ctx_size = got.shape[0]
    total = values.shape[0]
    pairs = total * ctx_size * block // 2
    return pl.pallas_call(
        functools.partial(attend_kernel, ctx_size, block),
        in_specs=[whole_smem()] * 2 + [whole_vmem()] * 3,
        out_specs=whole_vmem(),
        out_shape=jax.ShapeDtypeStruct((ctx_size, block, HD), jnp.bfloat16),
        scratch_shapes=[
            pltpu.VMEM((ctx_size * block + PAD, HD), jnp.bfloat16),
            pltpu.VMEM((ctx_size * block, 2 * HD), jnp.bfloat16),
            pltpu.VMEM((2 * block, 2 * TOK_DEV), jnp.float32),
            pltpu.VMEM((2 * block, 2 * TOK_DEV), jnp.float32),
            pltpu.VMEM((2 * block, HD), jnp.float32),
            pltpu.VMEM((2 * block, HD), jnp.float32),
            pltpu.VMEM((2 * block, HD), jnp.float32),
            pltpu.VMEM((2 * block, 2 * HD), jnp.float32),
        ],
        compiler_params=params(),
        cost_estimate=pl.CostEstimate(
            flops=pairs * 8 * HD, bytes_accessed=total * HD * 8, transcendentals=pairs
        ),
    )(cls, counts, got, keys, values)


def project_kernel(classes, chunks, column_ref, *rest):
    got_refs, (weight_ref, out_ref, rows_ref) = rest[:chunks], rest[chunks:]
    block = got_refs[0].shape[1]

    @pl.when(pl.program_id(0) == 0)
    def _():
        for j, got_ref in enumerate(got_refs):
            for d in range(got_ref.shape[0]):
                h, r = d // classes, d % classes
                first = (j * classes + r) * block
                rows_ref[first : first + block, h * HD : (h + 1) * HD] = got_ref[d]

    out_ref[...] = jnp.dot(
        rows_ref[...], weight_ref[...], preferred_element_type=jnp.float32
    ).astype(jnp.bfloat16)


def project(first_column, got, weight, columns, classes):
    ctx_size, block, _ = got[0].shape
    rows, depth = len(got) * classes * block, weight.shape[0]
    step = min(512, columns)
    return pl.pallas_call(
        functools.partial(project_kernel, classes, len(got)),
        grid_spec=pltpu.PrefetchScalarGridSpec(
            num_scalar_prefetch=1,
            grid=(columns // step,),
            in_specs=[pl.BlockSpec((ctx_size, block, HD), lambda i, first: (0, 0, 0))] * len(got)
            + [pl.BlockSpec((depth, step), lambda i, first: (0, first[0] + i))],
            out_specs=pl.BlockSpec((rows, step), lambda i, first: (0, i)),
            scratch_shapes=[pltpu.VMEM((rows, depth), jnp.bfloat16)],
        ),
        out_shape=jax.ShapeDtypeStruct((rows, columns), jnp.bfloat16),
        compiler_params=params(),
        cost_estimate=pl.CostEstimate(
            flops=2 * rows * depth * columns, bytes_accessed=2 * depth * columns, transcendentals=0
        ),
    )((first_column // step).astype(jnp.int32).reshape(1), *got, weight)


def join_kernel(chunks, parts, head_ref, *rest):
    got_refs, weight_refs = rest[:chunks], rest[chunks : chunks + parts]
    own_ref, out_ref, rows_ref = rest[chunks + parts :]
    block = got_refs[0].shape[1]
    depth = weight_refs[0].shape[0]

    @pl.when(pl.program_id(0) == 0)
    def _():
        for j, got_ref in enumerate(got_refs):
            for p in range(parts):
                for n in range(depth // HD):
                    at = p * depth + n * HD
                    rows_ref[j * block : (j + 1) * block, at : at + HD] = got_ref[head_ref[p] + n]

    total = jnp.zeros(out_ref.shape, jnp.float32)
    for p, weight_ref in enumerate(weight_refs):
        total = total + jnp.dot(
            rows_ref[:, p * depth : (p + 1) * depth],
            weight_ref[...],
            preferred_element_type=jnp.float32,
        )
    theirs = total.astype(jnp.bfloat16).astype(jnp.float32)
    out_ref[...] = (own_ref[...].astype(jnp.float32) + theirs).astype(jnp.bfloat16)


def join(first_heads, got, weights, own):
    ctx_size, block, _ = got[0].shape
    rows, columns = own.shape
    depth = weights[0].shape[0]
    step = min(512, columns)
    tile = pl.BlockSpec((rows, step), lambda i, first: (0, i))
    return pl.pallas_call(
        functools.partial(join_kernel, len(got), len(weights)),
        grid_spec=pltpu.PrefetchScalarGridSpec(
            num_scalar_prefetch=1,
            grid=(columns // step,),
            in_specs=[pl.BlockSpec((ctx_size, block, HD), lambda i, first: (0, 0, 0))] * len(got)
            + [pl.BlockSpec((depth, step), lambda i, first: (0, i))] * len(weights)
            + [tile],
            out_specs=tile,
            scratch_shapes=[pltpu.VMEM((rows, depth * len(weights)), jnp.bfloat16)],
        ),
        out_shape=jax.ShapeDtypeStruct((rows, columns), jnp.bfloat16),
        compiler_params=params(),
        cost_estimate=pl.CostEstimate(
            flops=2 * rows * depth * len(weights) * columns,
            bytes_accessed=2 * depth * len(weights) * columns,
            transcendentals=0,
        ),
    )(first_heads, *got, *weights, own)


def tables(query_rows):
    half_dim = HD // 2
    positions = lax.axis_index("ctx") * query_rows + jnp.arange(query_rows, dtype=jnp.int32)
    lane = jnp.arange(HD, dtype=jnp.int32)
    pair_id = jnp.where(lane < half_dim, lane, lane - half_dim)
    inv_freq = rope_base ** (-(pair_id.astype(jnp.float32) * 2.0 / HD))
    angles = positions.astype(jnp.float32)[:, None] * inv_freq[None, :]
    sine = jnp.sin(angles)
    return jnp.cos(angles), jnp.where(lane[None, :] < half_dim, -sine, sine)


def local(query, key, value, keep_rank, kept_count, out_weight):
    ctx_size = lax.axis_size("ctx")
    tp_size = lax.axis_size("tp")
    me = lax.axis_index("ctx")
    tp_me = lax.axis_index("tp")
    orig_rows = query.shape[0]
    heads = query.shape[1] // HD
    kv_heads = key.shape[1] // HD
    members = ctx_size // kv_heads
    classes = ctx_size // heads
    chunks = CHUNKS if classes == 1 else 1
    block = TOK_DEV // (chunks * classes)
    total = ctx_size * TOK_DEV
    reach = orig_rows // TOK_DEV
    cap = reach * block + TILE
    cap_kv = orig_rows + TILE
    columns = out_weight.shape[1] // tp_size

    kv_slots, q_slots = find_slots(
        me.reshape(1), kept_count, keep_rank, reach, chunks * classes, block, cap
    )
    cosine, sine = tables(orig_rows)

    across = [[z * members + m for z in range(kv_heads)] for m in range(members)]

    member = (me & (members - 1)).reshape(1)

    def pack_shared(rows, turned):
        (packed,) = pack(kv_slots, cosine, sine, rows, turned, 1, 1, cap_kv)
        return packed.reshape(kv_heads, cap_kv, HD)

    def send_across(packed):
        if kv_heads == 1:
            return packed
        return lax.all_to_all(
            packed, "ctx", split_axis=0, concat_axis=0, tiled=True, axis_index_groups=across
        )

    def swap(parts, bit):
        pairs = [(d, d ^ bit) for d in range(ctx_size)]
        return parts + [lax.ppermute(part, "ctx", pairs) for part in parts]

    bits = [members >> n for n in range(1, members.bit_length())]
    offsets = [0]
    for bit in bits:
        offsets = offsets + [offset ^ bit for offset in offsets]

    def send_query(packed):
        return lax.all_to_all(
            packed.reshape(ctx_size, cap, HD), "ctx", split_axis=0, concat_axis=0, tiled=True
        )

    traded = tp_size == 2 and classes == 1
    both = [(0, 1), (1, 0)]

    def chip_swap(part, bit):
        return lax.ppermute(part, "ctx", [(d, d ^ bit) for d in range(ctx_size)])

    core, side = me & 1, (me >> 1) & 1
    depth = out_weight.shape[0] // 8

    def weight_rows(p):
        first = core * (4 * depth) + jnp.where(side == 0, p, 3 - p) * depth
        return lax.dynamic_slice(out_weight, (first, (1 - tp_me) * columns), (depth, columns))

    key_parts = [send_across(pack_shared(key, True))]
    value_packed, key_parts = lax.optimization_barrier((pack_shared(value, False), key_parts))
    key_parts = swap(key_parts, bits[0])
    value_parts = [send_across(value_packed)]
    packed_q = list(pack(q_slots, cosine, sine, query, True, chunks, classes, cap))
    came = [lax.ppermute(weight_rows(0), "tp", both)] if traded else []
    packed_q[0], key_parts, value_parts, came = lax.optimization_barrier(
        (packed_q[0], key_parts, value_parts, came)
    )
    got_q = [send_query(packed_q[0])]
    value_parts = swap(value_parts, bits[0])
    for bit in bits[1:]:
        key_parts = swap(key_parts, bit)
    if traded:
        slice_1, came = lax.optimization_barrier((weight_rows(1), came))
        came = came + [lax.ppermute(slice_1, "tp", both)]
    if chunks > 1:
        packed_q[1], value_parts, came = lax.optimization_barrier((packed_q[1], value_parts, came))
    for bit in bits[1:]:
        value_parts = swap(value_parts, bit)
    got_q = got_q + [send_query(packed) for packed in packed_q[1:]]
    keys = compact(member, kept_count, key_parts, offsets, total, True)
    values = compact(member, kept_count, value_parts, offsets, total, False)
    crossed = []
    if traded:
        crossed = [chip_swap(part, 1) for part in came]
        slice_2, came = lax.optimization_barrier((weight_rows(2), came))
        came = came + [lax.ppermute(slice_2, "tp", both), chip_swap(came[0], 2)]

    got, done = [], None
    for j in range(chunks):
        cls_j = j * classes + (me & (classes - 1))
        if j > 0:
            got_q[j], done = lax.optimization_barrier((got_q[j], done))
            got.append(lax.all_to_all(done, "ctx", split_axis=0, concat_axis=0, tiled=True))
        done = attend(cls_j.reshape(1), kept_count, got_q[j], keys, values, block)
    if traded:
        done, came, crossed = lax.optimization_barrier((done, came, crossed))
    got.append(lax.all_to_all(done, "ctx", split_axis=0, concat_axis=0, tiled=True))
    if traded:
        theirs = [lax.ppermute(one, "tp", both) for one in got]
        came = came + crossed + [chip_swap(part, 1) for part in came[2:]]
        own = project(tp_me * columns, got, out_weight, columns, classes)
        per = depth // HD
        order = [jnp.where(side == 0, p, 3 - p) for p in range(3)] + [jnp.where(side == 0, 3, 0)]
        first_heads = jnp.stack(
            [(c * 4 + p) * per for c in (core, 1 - core) for p in order]
        ).astype(jnp.int32)
        return join(first_heads, theirs, came, own)
    full = project(jnp.int32(0) * tp_me, got, out_weight, columns * tp_size, classes)
    split = jnp.transpose(full.reshape(full.shape[0], tp_size, columns), (1, 0, 2))
    swapped = lax.all_to_all(split, "tp", split_axis=0, concat_axis=0, tiled=True)
    return jnp.sum(swapped.astype(jnp.float32), axis=0).astype(jnp.bfloat16)


def solution(mesh):
    placed = (P("ctx", "tp"), P("ctx", "tp"), P("ctx", "tp"), P("ctx", None), P(), P("tp", None))
    return jax.shard_map(
        local, mesh=mesh, in_specs=placed, out_specs=P("ctx", "tp"), check_vma=False
    )
```

```python
import functools
import math

import jax
import jax.numpy as jnp
from jax import lax
from jax.experimental import pallas as pl
from jax.experimental.pallas import tpu as pltpu
from jax.sharding import PartitionSpec as P

HD = 128
TOK_DEV = 384
TILE = 16
PAD = 128
CHUNKS = 2

rope_base = 1000000.0
masked_score = -1e30
exp2_scale = math.log2(math.e) / math.sqrt(HD)
VMEM_BYTES = 58 * 1024 * 1024


def whole_vmem():
    return pl.BlockSpec(memory_space=pltpu.VMEM)


def whole_smem():
    return pl.BlockSpec(memory_space=pltpu.SMEM)


def params():
    return pltpu.CompilerParams(vmem_limit_bytes=VMEM_BYTES)


def turn(rows, cosine, sine):
    as_float = rows.astype(jnp.float32)
    swapped = pltpu.roll(as_float, HD // 2, 1)
    return (as_float * cosine + swapped * sine).astype(jnp.bfloat16)


def rows_below(start, cls, block):
    whole = lax.div(start, TOK_DEV)
    return whole * block + jnp.clip(start - whole * TOK_DEV - cls * block, 0, block)


def slots_kernel(reach, groups, block, cap, me_ref, count_ref, rank_ref, kv_out, q_out):
    me = me_ref[0]
    rows = rank_ref.shape[1]
    start = jnp.int32(0)
    for s in range(count_ref.shape[0]):
        start = start + jnp.where(s < me, count_ref[s], 0)
    kept = rank_ref[...] < count_ref[me]
    upper = lax.broadcasted_iota(jnp.int32, (rows, rows), 0) <= lax.broadcasted_iota(
        jnp.int32, (rows, rows), 1
    )
    flags = jnp.broadcast_to(kept.astype(jnp.float32), (8, rows)).astype(jnp.bfloat16)
    order = (
        jnp.dot(
            flags, upper.astype(jnp.float32).astype(jnp.bfloat16), preferred_element_type=jnp.float32
        )[:1].astype(jnp.int32)
        - 1
    )
    kv_out[...] = jnp.where(kept, order + (start & (TILE - 1)), -1)
    place = start + order
    first = lax.div(start, TOK_DEV)
    device = first + jnp.zeros_like(place)
    for step in range(1, reach + 1):
        device = device + (place >= (first + step) * TOK_DEV).astype(jnp.int32)
    within = place - device * TOK_DEV
    cls = jnp.zeros_like(place)
    for step in range(1, groups):
        cls = cls + (within >= step * block).astype(jnp.int32)
    low = first * block + jnp.clip(start - first * TOK_DEV - cls * block, 0, block)
    slot = cls * cap + device * block + within - cls * block - low + (low & (TILE - 1))
    q_out[...] = jnp.where(kept, slot, -1)


def find_slots(me, counts, ranks, reach, groups, block, cap):
    shape = jax.ShapeDtypeStruct(ranks.shape, jnp.int32)
    return pl.pallas_call(
        functools.partial(slots_kernel, reach, groups, block, cap),
        in_specs=[whole_smem(), whole_smem(), whole_vmem()],
        out_specs=[whole_vmem()] * 2,
        out_shape=[shape, shape],
        compiler_params=params(),
        cost_estimate=pl.CostEstimate(flops=2**20, bytes_accessed=2**14, transcendentals=0),
    )(me, counts, ranks)


def pack_kernel(turned, classes, cap, width, slot_ref, cos_ref, sin_ref, row_ref, *rest):
    out_refs, hot_ref = rest[:-1], rest[-1]

    @pl.when(pl.program_id(0) == 0)
    def _():
        ids = lax.broadcasted_iota(jnp.int32, hot_ref.shape, 0)
        hot_ref[...] = (ids == slot_ref[...]).astype(jnp.float32).astype(jnp.bfloat16)

    if turned:
        rows = jnp.concatenate(
            [
                turn(row_ref[:, h * HD : (h + 1) * HD], cos_ref[...], sin_ref[...])
                for h in range(width)
            ],
            axis=1,
        )
    else:
        rows = row_ref[...]
    for j, out_ref in enumerate(out_refs):
        for r in range(classes):
            first = (j * classes + r) * cap
            moved = jnp.dot(
                hot_ref[first : first + cap, :], rows, preferred_element_type=jnp.float32
            ).astype(jnp.bfloat16)
            for h in range(width):
                out_ref[h, r] = moved[:, h * HD : (h + 1) * HD]


def pack(slots, cosine, sine, rows, turned, chunks, classes, cap):
    count = rows.shape[0]
    heads = rows.shape[1] // HD
    width = min(2, heads)
    fixed = lambda i: (0, 0)
    total = chunks * classes * cap
    return pl.pallas_call(
        functools.partial(pack_kernel, turned, classes, cap, width),
        grid=(heads // width,),
        in_specs=[
            pl.BlockSpec((1, count), fixed),
            pl.BlockSpec((count, HD), fixed),
            pl.BlockSpec((count, HD), fixed),
            pl.BlockSpec((count, width * HD), lambda i: (0, i)),
        ],
        out_specs=[pl.BlockSpec((width, classes, cap, HD), lambda i: (i, 0, 0, 0))] * chunks,
        out_shape=[jax.ShapeDtypeStruct((heads, classes, cap, HD), jnp.bfloat16)] * chunks,
        scratch_shapes=[pltpu.VMEM((total, count), jnp.bfloat16)],
        compiler_params=params(),
        cost_estimate=pl.CostEstimate(
            flops=2 * heads * total * count * HD, bytes_accessed=count * heads * HD * 4, transcendentals=0
        ),
    )(slots, cosine, sine, rows)


def piece_rows(cap):
    return max(rows for rows in range(TILE, PAD + 1, TILE) if cap % rows == 0)


def merge_pieces(low, high, piece, source, add):
    shift = low & (TILE - 1)
    pieces = jnp.where(high > low, lax.div(high - low + shift + piece - 1, piece), 0)
    first = low - shift

    def one(i, carry):
        at = pl.multiple_of(first + i * piece, TILE)
        add(at, source(pl.multiple_of(i * piece, TILE)))
        return carry

    lax.fori_loop(0, pieces, one, 0)


def compact_kernel(offsets, per, total, doubled, member_ref, count_ref, *rest):
    parts, out, all_rows, starts = rest[:-3], rest[-3], rest[-2], rest[-1]
    members = len(parts)
    piece = piece_rows(parts[0].shape[1])
    all_rows[...] = jnp.zeros_like(all_rows)
    start = jnp.int32(0)
    for s in range(count_ref.shape[0]):
        starts[s] = start
        start = start + count_ref[s]

    def add(at, rows):
        all_rows[pl.ds(at, piece), :] += rows

    for part, offset in zip(parts, offsets):
        for z in range(per):
            source = z * members + (member_ref[0] ^ offset)
            low = starts[source]
            merge_pieces(
                low,
                low + count_ref[source],
                piece,
                lambda at: part[z, pl.ds(at, piece), :],
                add,
            )
    if doubled:
        for first in range(0, total, 2 * TOK_DEV):
            turned = jnp.transpose(all_rows[first : first + 2 * TOK_DEV, :])
            out[:HD, first : first + 2 * TOK_DEV] = turned
            out[HD:, first : first + 2 * TOK_DEV] = turned
    else:
        out[:, :HD] = all_rows[:total, :]
        out[:, HD:] = jnp.ones((total, HD), jnp.bfloat16)


def compact(member, counts, parts, offsets, total, doubled):
    per = parts[0].shape[0]
    return pl.pallas_call(
        functools.partial(compact_kernel, offsets, per, total, doubled),
        in_specs=[whole_smem(), whole_smem()] + [whole_vmem()] * len(parts),
        out_specs=whole_vmem(),
        out_shape=jax.ShapeDtypeStruct(
            (2 * HD, total) if doubled else (total, 2 * HD), jnp.bfloat16
        ),
        scratch_shapes=[
            pltpu.VMEM((total + PAD, HD), jnp.bfloat16),
            pltpu.SMEM(counts.shape, jnp.int32),
        ],
        compiler_params=params(),
        cost_estimate=pl.CostEstimate(flops=total * HD * 8, bytes_accessed=total * HD * 8, transcendentals=0),
    )(member, counts, *parts)


def attend_kernel(ctx_size, block, cls_ref, count_ref, got_ref, key_ref, value_ref, out_ref,
                  query_all, query_two, scores_a, scores_b, top_a, top_b, run_max, run_acc):
    span = 2 * TOK_DEV
    pair = 4 * block
    supers = ctx_size // 4
    steps = supers * (supers + 1)
    cls = cls_ref[0]
    piece = piece_rows(got_ref.shape[1])
    query_all[...] = jnp.zeros_like(query_all)

    def add(at, rows):
        query_all[pl.ds(at, piece), :] += rows

    start = jnp.int32(0)
    for s in range(ctx_size):
        end = start + count_ref[s]
        merge_pieces(
            rows_below(start, cls, block),
            rows_below(end, cls, block),
            piece,
            lambda at: got_ref[s, pl.ds(at, piece), :],
            add,
        )
        start = end

    def split(i, carry):
        rows = pl.ds(pl.multiple_of(i * pair, TILE), pair)
        scaled = query_all[rows, :].astype(jnp.float32) * exp2_scale
        high = scaled.astype(jnp.bfloat16)
        query_two[rows, :HD] = high
        query_two[rows, HD:] = (scaled - high.astype(jnp.float32)).astype(jnp.bfloat16)
        return carry

    lax.fori_loop(0, supers, split, 0)

    def row_top(found):
        return jnp.broadcast_to(jnp.max(found, axis=1, keepdims=True), (pair, HD))

    def score(scores, top, i, k):
        rows = query_two[pl.ds(pl.multiple_of(jnp.minimum(i, supers - 1) * pair, TILE), pair), :]
        keys = key_ref[:, pl.ds(pl.multiple_of(k * span, HD), span)]
        found = jnp.dot(rows, keys, preferred_element_type=jnp.float32)
        scores[...] = found
        top[...] = row_top(found)

    def mask(scores, top, first):
        row_ids = lax.broadcasted_iota(jnp.int32, (pair, HD), 0)
        row = row_ids + cls * block - first
        for n in range(1, 4):
            row = row + jnp.where(row_ids >= n * block, TOK_DEV - block, 0)
        col = lax.broadcasted_iota(jnp.int32, (pair, span), 1)
        found = jnp.where(
            col <= jnp.concatenate([row] * (span // HD), axis=1), scores[...], masked_score
        )
        scores[...] = found
        top[...] = row_top(found)

    def absorb(scores, top, k):
        before = run_max[...]
        after = jnp.maximum(before, top[...])
        rescale = jnp.exp2(before - after)
        run_max[...] = after
        weights = jnp.exp2(scores[...] - jnp.concatenate([after] * (span // HD), axis=1))
        values = value_ref[pl.ds(pl.multiple_of(k * span, TILE), span), :]
        run_acc[...] = run_acc[...] * jnp.concatenate([rescale, rescale], axis=1) + jnp.dot(
            weights.astype(jnp.bfloat16), values, preferred_element_type=jnp.float32
        )

    def clear():
        run_max[...] = jnp.full_like(run_max, masked_score)
        run_acc[...] = jnp.zeros_like(run_acc)

    def one_step(now, later, i, k):
        last = k == 2 * i + 1
        next_i = jnp.where(last, i + 1, i)
        next_k = jnp.where(last, 0, k + 1)
        score(*later, next_i, next_k)
        absorb(*now, k)

        @pl.when(last)
        def _():
            result = (run_acc[:, :HD] / run_acc[:, HD:]).astype(jnp.bfloat16)
            for n in range(4):
                out_ref[4 * i + n] = result[n * block : (n + 1) * block]
            clear()

        @pl.when(next_k >= 2 * next_i)
        def _():
            mask(*later, (next_k - 2 * next_i) * span)

        return next_i, next_k

    buffers_a, buffers_b = (scores_a, top_a), (scores_b, top_b)
    clear()
    score(*buffers_a, 0, 0)
    mask(*buffers_a, 0)

    def two_steps(t, at):
        at = one_step(buffers_a, buffers_b, *at)
        return one_step(buffers_b, buffers_a, *at)

    lax.fori_loop(0, steps // 2, two_steps, (jnp.int32(0), jnp.int32(0)))


def attend(cls, counts, got, keys, values, block):
    ctx_size = got.shape[0]
    total = values.shape[0]
    pairs = total * ctx_size * block // 2
    return pl.pallas_call(
        functools.partial(attend_kernel, ctx_size, block),
        in_specs=[whole_smem()] * 2 + [whole_vmem()] * 3,
        out_specs=whole_vmem(),
        out_shape=jax.ShapeDtypeStruct((ctx_size, block, HD), jnp.bfloat16),
        scratch_shapes=[
            pltpu.VMEM((ctx_size * block + PAD, HD), jnp.bfloat16),
            pltpu.VMEM((ctx_size * block, 2 * HD), jnp.bfloat16),
            pltpu.VMEM((4 * block, 2 * TOK_DEV), jnp.float32),
            pltpu.VMEM((4 * block, 2 * TOK_DEV), jnp.float32),
            pltpu.VMEM((4 * block, HD), jnp.float32),
            pltpu.VMEM((4 * block, HD), jnp.float32),
            pltpu.VMEM((4 * block, HD), jnp.float32),
            pltpu.VMEM((4 * block, 2 * HD), jnp.float32),
        ],
        compiler_params=params(),
        cost_estimate=pl.CostEstimate(
            flops=pairs * 8 * HD, bytes_accessed=total * HD * 8, transcendentals=pairs
        ),
    )(cls, counts, got, keys, values)


def project_kernel(classes, chunks, column_ref, *rest):
    got_refs, (weight_ref, out_ref, rows_ref) = rest[:chunks], rest[chunks:]
    block = got_refs[0].shape[1]

    @pl.when(pl.program_id(0) == 0)
    def _():
        for j, got_ref in enumerate(got_refs):
            for d in range(got_ref.shape[0]):
                h, r = d // classes, d % classes
                first = (j * classes + r) * block
                rows_ref[first : first + block, h * HD : (h + 1) * HD] = got_ref[d]

    out_ref[...] = jnp.dot(
        rows_ref[...], weight_ref[...], preferred_element_type=jnp.float32
    ).astype(jnp.bfloat16)


def project(first_column, got, weight, columns, classes):
    ctx_size, block, _ = got[0].shape
    rows, depth = len(got) * classes * block, weight.shape[0]
    step = min(512, columns)
    return pl.pallas_call(
        functools.partial(project_kernel, classes, len(got)),
        grid_spec=pltpu.PrefetchScalarGridSpec(
            num_scalar_prefetch=1,
            grid=(columns // step,),
            in_specs=[pl.BlockSpec((ctx_size, block, HD), lambda i, first: (0, 0, 0))] * len(got)
            + [pl.BlockSpec((depth, step), lambda i, first: (0, first[0] + i))],
            out_specs=pl.BlockSpec((rows, step), lambda i, first: (0, i)),
            scratch_shapes=[pltpu.VMEM((rows, depth), jnp.bfloat16)],
        ),
        out_shape=jax.ShapeDtypeStruct((rows, columns), jnp.bfloat16),
        compiler_params=params(),
        cost_estimate=pl.CostEstimate(
            flops=2 * rows * depth * columns, bytes_accessed=2 * depth * columns, transcendentals=0
        ),
    )((first_column // step).astype(jnp.int32).reshape(1), *got, weight)


def join_kernel(chunks, parts, head_ref, *rest):
    got_refs, weight_refs = rest[:chunks], rest[chunks : chunks + parts]
    own_ref, out_ref, rows_ref = rest[chunks + parts :]
    block = got_refs[0].shape[1]
    depth = weight_refs[0].shape[0]

    @pl.when(pl.program_id(0) == 0)
    def _():
        for j, got_ref in enumerate(got_refs):
            for p in range(parts):
                for n in range(depth // HD):
                    at = p * depth + n * HD
                    rows_ref[j * block : (j + 1) * block, at : at + HD] = got_ref[head_ref[p] + n]

    total = jnp.zeros(out_ref.shape, jnp.float32)
    for p, weight_ref in enumerate(weight_refs):
        total = total + jnp.dot(
            rows_ref[:, p * depth : (p + 1) * depth],
            weight_ref[...],
            preferred_element_type=jnp.float32,
        )
    theirs = total.astype(jnp.bfloat16).astype(jnp.float32)
    out_ref[...] = (own_ref[...].astype(jnp.float32) + theirs).astype(jnp.bfloat16)


def join(first_heads, got, weights, own):
    ctx_size, block, _ = got[0].shape
    rows, columns = own.shape
    depth = weights[0].shape[0]
    step = min(512, columns)
    tile = pl.BlockSpec((rows, step), lambda i, first: (0, i))
    return pl.pallas_call(
        functools.partial(join_kernel, len(got), len(weights)),
        grid_spec=pltpu.PrefetchScalarGridSpec(
            num_scalar_prefetch=1,
            grid=(columns // step,),
            in_specs=[pl.BlockSpec((ctx_size, block, HD), lambda i, first: (0, 0, 0))] * len(got)
            + [pl.BlockSpec((depth, step), lambda i, first: (0, i))] * len(weights)
            + [tile],
            out_specs=tile,
            scratch_shapes=[pltpu.VMEM((rows, depth * len(weights)), jnp.bfloat16)],
        ),
        out_shape=jax.ShapeDtypeStruct((rows, columns), jnp.bfloat16),
        compiler_params=params(),
        cost_estimate=pl.CostEstimate(
            flops=2 * rows * depth * len(weights) * columns,
            bytes_accessed=2 * depth * len(weights) * columns,
            transcendentals=0,
        ),
    )(first_heads, *got, *weights, own)


def tables(query_rows):
    half_dim = HD // 2
    positions = lax.axis_index("ctx") * query_rows + jnp.arange(query_rows, dtype=jnp.int32)
    lane = jnp.arange(HD, dtype=jnp.int32)
    pair_id = jnp.where(lane < half_dim, lane, lane - half_dim)
    inv_freq = rope_base ** (-(pair_id.astype(jnp.float32) * 2.0 / HD))
    angles = positions.astype(jnp.float32)[:, None] * inv_freq[None, :]
    sine = jnp.sin(angles)
    return jnp.cos(angles), jnp.where(lane[None, :] < half_dim, -sine, sine)


def local(query, key, value, keep_rank, kept_count, out_weight):
    ctx_size = lax.axis_size("ctx")
    tp_size = lax.axis_size("tp")
    me = lax.axis_index("ctx")
    tp_me = lax.axis_index("tp")
    orig_rows = query.shape[0]
    heads = query.shape[1] // HD
    kv_heads = key.shape[1] // HD
    members = ctx_size // kv_heads
    classes = ctx_size // heads
    chunks = CHUNKS if classes == 1 else 1
    block = TOK_DEV // (chunks * classes)
    total = ctx_size * TOK_DEV
    reach = orig_rows // TOK_DEV
    cap = reach * block + TILE
    cap_kv = orig_rows + TILE
    columns = out_weight.shape[1] // tp_size

    kv_slots, q_slots = find_slots(
        me.reshape(1), kept_count, keep_rank, reach, chunks * classes, block, cap
    )
    cosine, sine = tables(orig_rows)

    across = [[z * members + m for z in range(kv_heads)] for m in range(members)]

    member = (me & (members - 1)).reshape(1)

    def pack_shared(rows, turned):
        (packed,) = pack(kv_slots, cosine, sine, rows, turned, 1, 1, cap_kv)
        return packed.reshape(kv_heads, cap_kv, HD)

    def send_across(packed):
        if kv_heads == 1:
            return packed
        return lax.all_to_all(
            packed, "ctx", split_axis=0, concat_axis=0, tiled=True, axis_index_groups=across
        )

    def swap(parts, bit):
        pairs = [(d, d ^ bit) for d in range(ctx_size)]
        return parts + [lax.ppermute(part, "ctx", pairs) for part in parts]

    bits = [members >> n for n in range(1, members.bit_length())]
    offsets = [0]
    for bit in bits:
        offsets = offsets + [offset ^ bit for offset in offsets]

    def send_query(packed):
        return lax.all_to_all(
            packed.reshape(ctx_size, cap, HD), "ctx", split_axis=0, concat_axis=0, tiled=True
        )

    traded = tp_size == 2 and classes == 1
    both = [(0, 1), (1, 0)]

    def chip_swap(part, bit):
        return lax.ppermute(part, "ctx", [(d, d ^ bit) for d in range(ctx_size)])

    core, side = me & 1, (me >> 1) & 1
    depth = out_weight.shape[0] // 8

    def weight_rows(p):
        first = core * (4 * depth) + jnp.where(side == 0, p, 3 - p) * depth
        return lax.dynamic_slice(out_weight, (first, (1 - tp_me) * columns), (depth, columns))

    key_parts = [send_across(pack_shared(key, True))]
    value_packed, key_parts = lax.optimization_barrier((pack_shared(value, False), key_parts))
    key_parts = swap(key_parts, bits[0])
    value_parts = [send_across(value_packed)]
    packed_q = list(pack(q_slots, cosine, sine, query, True, chunks, classes, cap))
    came = [lax.ppermute(weight_rows(p), "tp", both) for p in range(3)] if traded else []
    packed_q[0], key_parts, value_parts = lax.optimization_barrier(
        (packed_q[0], key_parts, value_parts)
    )
    got_q = [send_query(packed_q[0])]
    value_parts = swap(value_parts, bits[0])
    for bit in bits[1:]:
        key_parts = swap(key_parts, bit)
    keys = compact(member, kept_count, key_parts, offsets, total, True)
    if chunks > 1:
        packed_q[1], value_parts, keys = lax.optimization_barrier((packed_q[1], value_parts, keys))
    for bit in bits[1:]:
        value_parts = swap(value_parts, bit)
    got_q = got_q + [send_query(packed) for packed in packed_q[1:]]
    values = compact(member, kept_count, value_parts, offsets, total, False)
    if traded:
        came = came + [chip_swap(came[0], 2)]

    got, done = [], None
    for j in range(chunks):
        cls_j = j * classes + (me & (classes - 1))
        if j > 0:
            got_q[j], done = lax.optimization_barrier((got_q[j], done))
            got.append(lax.all_to_all(done, "ctx", split_axis=0, concat_axis=0, tiled=True))
        done = attend(cls_j.reshape(1), kept_count, got_q[j], keys, values, block)
    if traded:
        done, came = lax.optimization_barrier((done, came))
    got.append(lax.all_to_all(done, "ctx", split_axis=0, concat_axis=0, tiled=True))
    if traded:
        theirs = [lax.ppermute(one, "tp", both) for one in got]
        came = came + [chip_swap(part, 1) for part in came]
        own = project(tp_me * columns, got, out_weight, columns, classes)
        per = depth // HD
        order = [jnp.where(side == 0, p, 3 - p) for p in range(3)] + [jnp.where(side == 0, 3, 0)]
        first_heads = jnp.stack(
            [(c * 4 + p) * per for c in (core, 1 - core) for p in order]
        ).astype(jnp.int32)
        return join(first_heads, theirs, came, own)
    full = project(jnp.int32(0) * tp_me, got, out_weight, columns * tp_size, classes)
    split = jnp.transpose(full.reshape(full.shape[0], tp_size, columns), (1, 0, 2))
    swapped = lax.all_to_all(split, "tp", split_axis=0, concat_axis=0, tiled=True)
    return jnp.sum(swapped.astype(jnp.float32), axis=0).astype(jnp.bfloat16)


def solution(mesh):
    placed = (P("ctx", "tp"), P("ctx", "tp"), P("ctx", "tp"), P("ctx", None), P(), P("tp", None))
    return jax.shard_map(
        local, mesh=mesh, in_specs=placed, out_specs=P("ctx", "tp"), check_vma=False
    )
```

```python
import functools
import math

import jax
import jax.numpy as jnp
from jax import lax
from jax.experimental import pallas as pl
from jax.experimental.pallas import tpu as pltpu
from jax.sharding import PartitionSpec as P

HD = 128
TOK_DEV = 384
TILE = 16
PAD = 128
CHUNKS = 2

rope_base = 1000000.0
masked_score = -1e30
exp2_scale = math.log2(math.e) / math.sqrt(HD)
VMEM_BYTES = 58 * 1024 * 1024


def whole_vmem():
    return pl.BlockSpec(memory_space=pltpu.VMEM)


def whole_smem():
    return pl.BlockSpec(memory_space=pltpu.SMEM)


def params():
    return pltpu.CompilerParams(vmem_limit_bytes=VMEM_BYTES)


def turn(rows, cosine, sine):
    as_float = rows.astype(jnp.float32)
    swapped = pltpu.roll(as_float, HD // 2, 1)
    return (as_float * cosine + swapped * sine).astype(jnp.bfloat16)


def rows_below(start, cls, block):
    whole = lax.div(start, TOK_DEV)
    return whole * block + jnp.clip(start - whole * TOK_DEV - cls * block, 0, block)


def slots_kernel(reach, groups, block, cap, me_ref, count_ref, rank_ref, kv_out, q_out):
    me = me_ref[0]
    rows = rank_ref.shape[1]
    start = jnp.int32(0)
    for s in range(count_ref.shape[0]):
        start = start + jnp.where(s < me, count_ref[s], 0)
    kept = rank_ref[...] < count_ref[me]
    upper = lax.broadcasted_iota(jnp.int32, (rows, rows), 0) <= lax.broadcasted_iota(
        jnp.int32, (rows, rows), 1
    )
    flags = jnp.broadcast_to(kept.astype(jnp.float32), (8, rows)).astype(jnp.bfloat16)
    order = (
        jnp.dot(
            flags, upper.astype(jnp.float32).astype(jnp.bfloat16), preferred_element_type=jnp.float32
        )[:1].astype(jnp.int32)
        - 1
    )
    kv_out[...] = jnp.where(kept, order + (start & (TILE - 1)), -1)
    place = start + order
    first = lax.div(start, TOK_DEV)
    device = first + jnp.zeros_like(place)
    for step in range(1, reach + 1):
        device = device + (place >= (first + step) * TOK_DEV).astype(jnp.int32)
    within = place - device * TOK_DEV
    cls = jnp.zeros_like(place)
    for step in range(1, groups):
        cls = cls + (within >= step * block).astype(jnp.int32)
    low = first * block + jnp.clip(start - first * TOK_DEV - cls * block, 0, block)
    slot = cls * cap + device * block + within - cls * block - low + (low & (TILE - 1))
    q_out[...] = jnp.where(kept, slot, -1)


def find_slots(me, counts, ranks, reach, groups, block, cap):
    shape = jax.ShapeDtypeStruct(ranks.shape, jnp.int32)
    return pl.pallas_call(
        functools.partial(slots_kernel, reach, groups, block, cap),
        in_specs=[whole_smem(), whole_smem(), whole_vmem()],
        out_specs=[whole_vmem()] * 2,
        out_shape=[shape, shape],
        compiler_params=params(),
        cost_estimate=pl.CostEstimate(flops=2**20, bytes_accessed=2**14, transcendentals=0),
    )(me, counts, ranks)


def pack_kernel(turned, classes, cap, width, slot_ref, cos_ref, sin_ref, row_ref, *rest):
    out_refs, hot_ref = rest[:-1], rest[-1]

    @pl.when(pl.program_id(0) == 0)
    def _():
        ids = lax.broadcasted_iota(jnp.int32, hot_ref.shape, 0)
        hot_ref[...] = (ids == slot_ref[...]).astype(jnp.float32).astype(jnp.bfloat16)

    if turned:
        rows = jnp.concatenate(
            [
                turn(row_ref[:, h * HD : (h + 1) * HD], cos_ref[...], sin_ref[...])
                for h in range(width)
            ],
            axis=1,
        )
    else:
        rows = row_ref[...]
    for j, out_ref in enumerate(out_refs):
        for r in range(classes):
            first = (j * classes + r) * cap
            moved = jnp.dot(
                hot_ref[first : first + cap, :], rows, preferred_element_type=jnp.float32
            ).astype(jnp.bfloat16)
            for h in range(width):
                out_ref[h, r] = moved[:, h * HD : (h + 1) * HD]


def pack(slots, cosine, sine, rows, turned, chunks, classes, cap):
    count = rows.shape[0]
    heads = rows.shape[1] // HD
    width = min(2, heads)
    fixed = lambda i: (0, 0)
    total = chunks * classes * cap
    return pl.pallas_call(
        functools.partial(pack_kernel, turned, classes, cap, width),
        grid=(heads // width,),
        in_specs=[
            pl.BlockSpec((1, count), fixed),
            pl.BlockSpec((count, HD), fixed),
            pl.BlockSpec((count, HD), fixed),
            pl.BlockSpec((count, width * HD), lambda i: (0, i)),
        ],
        out_specs=[pl.BlockSpec((width, classes, cap, HD), lambda i: (i, 0, 0, 0))] * chunks,
        out_shape=[jax.ShapeDtypeStruct((heads, classes, cap, HD), jnp.bfloat16)] * chunks,
        scratch_shapes=[pltpu.VMEM((total, count), jnp.bfloat16)],
        compiler_params=params(),
        cost_estimate=pl.CostEstimate(
            flops=2 * heads * total * count * HD, bytes_accessed=count * heads * HD * 4, transcendentals=0
        ),
    )(slots, cosine, sine, rows)


def piece_rows(cap):
    return max(rows for rows in range(TILE, PAD + 1, TILE) if cap % rows == 0)


def merge_pieces(low, high, piece, source, add):
    shift = low & (TILE - 1)
    pieces = jnp.where(high > low, lax.div(high - low + shift + piece - 1, piece), 0)
    first = low - shift

    def one(i, carry):
        at = pl.multiple_of(first + i * piece, TILE)
        add(at, source(pl.multiple_of(i * piece, TILE)))
        return carry

    lax.fori_loop(0, pieces, one, 0)


def compact_kernel(offsets, per, total, as_keys, member_ref, count_ref, *rest):
    parts, out, all_rows, starts = rest[:-3], rest[-3], rest[-2], rest[-1]
    members = len(parts)
    piece = piece_rows(parts[0].shape[1])
    all_rows[...] = jnp.zeros_like(all_rows)
    start = jnp.int32(0)
    for s in range(count_ref.shape[0]):
        starts[s] = start
        start = start + count_ref[s]

    def add(at, rows):
        all_rows[pl.ds(at, piece), :] += rows

    for part, offset in zip(parts, offsets):
        for z in range(per):
            source = z * members + (member_ref[0] ^ offset)
            low = starts[source]
            merge_pieces(
                low,
                low + count_ref[source],
                piece,
                lambda at: part[z, pl.ds(at, piece), :],
                add,
            )
    if as_keys:
        for first in range(0, total, 2 * TOK_DEV):
            out[:, first : first + 2 * TOK_DEV] = jnp.transpose(
                all_rows[first : first + 2 * TOK_DEV, :]
            )
    else:
        out[:, :HD] = all_rows[:total, :]
        out[:, HD:] = jnp.ones((total, HD), jnp.bfloat16)


def compact(member, counts, parts, offsets, total, as_keys):
    per = parts[0].shape[0]
    return pl.pallas_call(
        functools.partial(compact_kernel, offsets, per, total, as_keys),
        in_specs=[whole_smem(), whole_smem()] + [whole_vmem()] * len(parts),
        out_specs=whole_vmem(),
        out_shape=jax.ShapeDtypeStruct(
            (HD, total) if as_keys else (total, 2 * HD), jnp.bfloat16
        ),
        scratch_shapes=[
            pltpu.VMEM((total + PAD, HD), jnp.bfloat16),
            pltpu.SMEM(counts.shape, jnp.int32),
        ],
        compiler_params=params(),
        cost_estimate=pl.CostEstimate(flops=total * HD * 8, bytes_accessed=total * HD * 8, transcendentals=0),
    )(member, counts, *parts)


def attend_kernel(ctx_size, block, cls_ref, count_ref, got_ref, key_ref, value_ref, out_ref,
                  query_all, scores_a, scores_b, top_a, top_b, run_max, run_acc):
    span = 2 * TOK_DEV
    pair = 4 * block
    supers = ctx_size // 4
    steps = supers * (supers + 1)
    cls = cls_ref[0]
    piece = piece_rows(got_ref.shape[1])
    query_all[...] = jnp.zeros_like(query_all)

    def add(at, rows):
        query_all[pl.ds(at, piece), :] += rows

    start = jnp.int32(0)
    for s in range(ctx_size):
        end = start + count_ref[s]
        merge_pieces(
            rows_below(start, cls, block),
            rows_below(end, cls, block),
            piece,
            lambda at: got_ref[s, pl.ds(at, piece), :],
            add,
        )
        start = end

    def row_top(found):
        return jnp.broadcast_to(jnp.max(found, axis=1, keepdims=True), (pair, HD))

    def score(scores, top, i, k):
        rows = query_all[pl.ds(pl.multiple_of(jnp.minimum(i, supers - 1) * pair, TILE), pair), :]
        keys = key_ref[:, pl.ds(pl.multiple_of(k * span, HD), span)]
        found = jnp.dot(rows, keys, preferred_element_type=jnp.float32)
        scores[...] = found
        top[...] = row_top(found)

    def mask(scores, top, first):
        row_ids = lax.broadcasted_iota(jnp.int32, (pair, HD), 0)
        row = row_ids + cls * block - first
        for n in range(1, 4):
            row = row + jnp.where(row_ids >= n * block, TOK_DEV - block, 0)
        col = lax.broadcasted_iota(jnp.int32, (pair, span), 1)
        found = jnp.where(
            col <= jnp.concatenate([row] * (span // HD), axis=1), scores[...], masked_score
        )
        scores[...] = found
        top[...] = row_top(found)

    def absorb(scores, top, k):
        before = run_max[...]
        after = jnp.maximum(before, top[...])
        rescale = jnp.exp2((before - after) * exp2_scale)
        run_max[...] = after
        weights = jnp.exp2(
            (scores[...] - jnp.concatenate([after] * (span // HD), axis=1)) * exp2_scale
        )
        values = value_ref[pl.ds(pl.multiple_of(k * span, TILE), span), :]
        run_acc[...] = run_acc[...] * jnp.concatenate([rescale, rescale], axis=1) + jnp.dot(
            weights.astype(jnp.bfloat16), values, preferred_element_type=jnp.float32
        )

    def clear():
        run_max[...] = jnp.full_like(run_max, masked_score)
        run_acc[...] = jnp.zeros_like(run_acc)

    def one_step(now, later, i, k):
        last = k == 2 * i + 1
        next_i = jnp.where(last, i + 1, i)
        next_k = jnp.where(last, 0, k + 1)
        score(*later, next_i, next_k)
        absorb(*now, k)

        @pl.when(last)
        def _():
            result = (run_acc[:, :HD] / run_acc[:, HD:]).astype(jnp.bfloat16)
            for n in range(4):
                out_ref[4 * i + n] = result[n * block : (n + 1) * block]
            clear()

        @pl.when(next_k >= 2 * next_i)
        def _():
            mask(*later, (next_k - 2 * next_i) * span)

        return next_i, next_k

    buffers_a, buffers_b = (scores_a, top_a), (scores_b, top_b)
    clear()
    score(*buffers_a, 0, 0)
    mask(*buffers_a, 0)

    def two_steps(t, at):
        at = one_step(buffers_a, buffers_b, *at)
        return one_step(buffers_b, buffers_a, *at)

    lax.fori_loop(0, steps // 2, two_steps, (jnp.int32(0), jnp.int32(0)))


def attend(cls, counts, got, keys, values, block):
    ctx_size = got.shape[0]
    total = values.shape[0]
    pairs = total * ctx_size * block // 2
    return pl.pallas_call(
        functools.partial(attend_kernel, ctx_size, block),
        in_specs=[whole_smem()] * 2 + [whole_vmem()] * 3,
        out_specs=whole_vmem(),
        out_shape=jax.ShapeDtypeStruct((ctx_size, block, HD), jnp.bfloat16),
        scratch_shapes=[
            pltpu.VMEM((ctx_size * block + PAD, HD), jnp.bfloat16),
            pltpu.VMEM((4 * block, 2 * TOK_DEV), jnp.float32),
            pltpu.VMEM((4 * block, 2 * TOK_DEV), jnp.float32),
            pltpu.VMEM((4 * block, HD), jnp.float32),
            pltpu.VMEM((4 * block, HD), jnp.float32),
            pltpu.VMEM((4 * block, HD), jnp.float32),
            pltpu.VMEM((4 * block, 2 * HD), jnp.float32),
        ],
        compiler_params=params(),
        cost_estimate=pl.CostEstimate(
            flops=pairs * 8 * HD, bytes_accessed=total * HD * 8, transcendentals=pairs
        ),
    )(cls, counts, got, keys, values)


def project_kernel(classes, chunks, column_ref, *rest):
    got_refs, (weight_ref, out_ref, rows_ref) = rest[:chunks], rest[chunks:]
    block = got_refs[0].shape[1]

    @pl.when(pl.program_id(0) == 0)
    def _():
        for j, got_ref in enumerate(got_refs):
            for d in range(got_ref.shape[0]):
                h, r = d // classes, d % classes
                first = (j * classes + r) * block
                rows_ref[first : first + block, h * HD : (h + 1) * HD] = got_ref[d]

    out_ref[...] = jnp.dot(
        rows_ref[...], weight_ref[...], preferred_element_type=jnp.float32
    ).astype(jnp.bfloat16)


def project(first_column, got, weight, columns, classes):
    ctx_size, block, _ = got[0].shape
    rows, depth = len(got) * classes * block, weight.shape[0]
    step = min(512, columns)
    return pl.pallas_call(
        functools.partial(project_kernel, classes, len(got)),
        grid_spec=pltpu.PrefetchScalarGridSpec(
            num_scalar_prefetch=1,
            grid=(columns // step,),
            in_specs=[pl.BlockSpec((ctx_size, block, HD), lambda i, first: (0, 0, 0))] * len(got)
            + [pl.BlockSpec((depth, step), lambda i, first: (0, first[0] + i))],
            out_specs=pl.BlockSpec((rows, step), lambda i, first: (0, i)),
            scratch_shapes=[pltpu.VMEM((rows, depth), jnp.bfloat16)],
        ),
        out_shape=jax.ShapeDtypeStruct((rows, columns), jnp.bfloat16),
        compiler_params=params(),
        cost_estimate=pl.CostEstimate(
            flops=2 * rows * depth * columns, bytes_accessed=2 * depth * columns, transcendentals=0
        ),
    )((first_column // step).astype(jnp.int32).reshape(1), *got, weight)


def join_kernel(chunks, parts, head_ref, *rest):
    got_refs, weight_refs = rest[:chunks], rest[chunks : chunks + parts]
    own_ref, out_ref, rows_ref = rest[chunks + parts :]
    block = got_refs[0].shape[1]
    firsts = [sum(ref.shape[0] for ref in weight_refs[:p]) for p in range(parts)]

    @pl.when(pl.program_id(0) == 0)
    def _():
        for j, got_ref in enumerate(got_refs):
            for p in range(parts):
                for n in range(weight_refs[p].shape[0] // HD):
                    at = firsts[p] + n * HD
                    rows_ref[j * block : (j + 1) * block, at : at + HD] = got_ref[head_ref[p] + n]

    total = jnp.zeros(out_ref.shape, jnp.float32)
    for first, weight_ref in zip(firsts, weight_refs):
        total = total + jnp.dot(
            rows_ref[:, first : first + weight_ref.shape[0]],
            weight_ref[...],
            preferred_element_type=jnp.float32,
        )
    theirs = total.astype(jnp.bfloat16).astype(jnp.float32)
    out_ref[...] = (own_ref[...].astype(jnp.float32) + theirs).astype(jnp.bfloat16)


def join(first_heads, got, weights, own):
    ctx_size, block, _ = got[0].shape
    rows, columns = own.shape
    depth = sum(weight.shape[0] for weight in weights)
    step = min(512, columns)
    tile = pl.BlockSpec((rows, step), lambda i, first: (0, i))
    return pl.pallas_call(
        functools.partial(join_kernel, len(got), len(weights)),
        grid_spec=pltpu.PrefetchScalarGridSpec(
            num_scalar_prefetch=1,
            grid=(columns // step,),
            in_specs=[pl.BlockSpec((ctx_size, block, HD), lambda i, first: (0, 0, 0))] * len(got)
            + [pl.BlockSpec((weight.shape[0], step), lambda i, first: (0, i)) for weight in weights]
            + [tile],
            out_specs=tile,
            scratch_shapes=[pltpu.VMEM((rows, depth), jnp.bfloat16)],
        ),
        out_shape=jax.ShapeDtypeStruct((rows, columns), jnp.bfloat16),
        compiler_params=params(),
        cost_estimate=pl.CostEstimate(
            flops=2 * rows * depth * columns,
            bytes_accessed=2 * depth * columns,
            transcendentals=0,
        ),
    )(first_heads, *got, *weights, own)


def tables(query_rows):
    half_dim = HD // 2
    positions = lax.axis_index("ctx") * query_rows + jnp.arange(query_rows, dtype=jnp.int32)
    lane = jnp.arange(HD, dtype=jnp.int32)
    pair_id = jnp.where(lane < half_dim, lane, lane - half_dim)
    inv_freq = rope_base ** (-(pair_id.astype(jnp.float32) * 2.0 / HD))
    angles = positions.astype(jnp.float32)[:, None] * inv_freq[None, :]
    sine = jnp.sin(angles)
    return jnp.cos(angles), jnp.where(lane[None, :] < half_dim, -sine, sine)


def local(query, key, value, keep_rank, kept_count, out_weight):
    ctx_size = lax.axis_size("ctx")
    tp_size = lax.axis_size("tp")
    me = lax.axis_index("ctx")
    tp_me = lax.axis_index("tp")
    orig_rows = query.shape[0]
    heads = query.shape[1] // HD
    kv_heads = key.shape[1] // HD
    members = ctx_size // kv_heads
    classes = ctx_size // heads
    chunks = CHUNKS if classes == 1 else 1
    block = TOK_DEV // (chunks * classes)
    total = ctx_size * TOK_DEV
    reach = orig_rows // TOK_DEV
    cap = reach * block + TILE
    cap_kv = orig_rows + TILE
    columns = out_weight.shape[1] // tp_size

    kv_slots, q_slots = find_slots(
        me.reshape(1), kept_count, keep_rank, reach, chunks * classes, block, cap
    )
    cosine, sine = tables(orig_rows)

    across = [[z * members + m for z in range(kv_heads)] for m in range(members)]

    member = (me & (members - 1)).reshape(1)

    def pack_shared(rows, turned):
        (packed,) = pack(kv_slots, cosine, sine, rows, turned, 1, 1, cap_kv)
        return packed.reshape(kv_heads, cap_kv, HD)

    def send_across(packed):
        if kv_heads == 1:
            return packed
        return lax.all_to_all(
            packed, "ctx", split_axis=0, concat_axis=0, tiled=True, axis_index_groups=across
        )

    def swap(parts, bit):
        pairs = [(d, d ^ bit) for d in range(ctx_size)]
        return parts + [lax.ppermute(part, "ctx", pairs) for part in parts]

    bits = [members >> n for n in range(1, members.bit_length())]
    offsets = [0]
    for bit in bits:
        offsets = offsets + [offset ^ bit for offset in offsets]

    def send_query(packed):
        return lax.all_to_all(
            packed.reshape(ctx_size, cap, HD), "ctx", split_axis=0, concat_axis=0, tiled=True
        )

    traded = tp_size == 2 and classes == 1 and heads == 16 and chunks == 2
    both = [(0, 1), (1, 0)]

    def chip_swap(part, bit):
        return lax.ppermute(part, "ctx", [(d, d ^ bit) for d in range(ctx_size)])

    core, side = me & 1, (me >> 1) & 1
    sizes = [1, 1, 2, 2]

    def weight_rows(p):
        low = sum(sizes[:p])
        first = jnp.where(side == 0, low, 8 - low - sizes[p]) + core * 8
        return lax.dynamic_slice(
            out_weight, (first * HD, (1 - tp_me) * columns), (sizes[p] * HD, columns)
        )

    def trade(part):
        return lax.ppermute(part, "tp", both)

    key_parts = [send_across(pack_shared(key, True))]
    slices = [weight_rows(p) for p in range(len(sizes))] if traded else []
    value_packed, key_parts, slices = lax.optimization_barrier(
        (pack_shared(value, False), key_parts, slices)
    )
    key_parts = swap(key_parts, bits[0])
    value_parts = [send_across(value_packed)]
    packed_q = list(pack(q_slots, cosine, sine, query, True, chunks, classes, cap))
    came = [trade(slices[0])] if traded else []
    packed_q[0], key_parts, value_parts, came, slices = lax.optimization_barrier(
        (packed_q[0], key_parts, value_parts, came, slices)
    )
    if traded:
        came = came + [trade(slices[1])]
    got_q = [send_query(packed_q[0])]
    value_parts = swap(value_parts, bits[0])
    for bit in bits[1:]:
        key_parts = swap(key_parts, bit)
    keys = compact(member, kept_count, key_parts, offsets, total, True)
    if chunks > 1:
        packed_q[1], value_parts, keys, came, slices = lax.optimization_barrier(
            (packed_q[1], value_parts, keys, came, slices)
        )
    for bit in bits[1:]:
        value_parts = swap(value_parts, bit)
    got_q = got_q + [send_query(packed) for packed in packed_q[1:]]
    values = compact(member, kept_count, value_parts, offsets, total, False)
    if traded:
        came = came + [trade(slices[2])]
        aside = [chip_swap(part, 2) for part in came[:2]]

    got, done = [], None
    for j in range(chunks):
        cls_j = j * classes + (me & (classes - 1))
        if j > 0:
            got_q[j], done, came, slices = lax.optimization_barrier((got_q[j], done, came, slices))
            got.append(lax.all_to_all(done, "ctx", split_axis=0, concat_axis=0, tiled=True))
        done = attend(cls_j.reshape(1), kept_count, got_q[j], keys, values, block)
    if traded:
        came = came + [trade(slices[3])]
        done, aside = lax.optimization_barrier((done, aside))
    got.append(lax.all_to_all(done, "ctx", split_axis=0, concat_axis=0, tiled=True))
    if traded:
        theirs = [trade(one) for one in got]
        came = came + aside
        came = came + [chip_swap(part, 1) for part in came]
        own = project(tp_me * columns, got, out_weight, columns, classes)
        ups = [sum(sizes[:p]) for p in range(5)]
        order = [
            jnp.where(side == 0, up, 8 - up - size) for up, size in zip(ups, sizes)
        ] + [jnp.where(side == 0, 7 - n, n) for n in range(2)]
        first_heads = jnp.stack([c * 8 + at for c in (core, 1 - core) for at in order])
        return join(first_heads.astype(jnp.int32), theirs, came, own)
    full = project(jnp.int32(0) * tp_me, got, out_weight, columns * tp_size, classes)
    split = jnp.transpose(full.reshape(full.shape[0], tp_size, columns), (1, 0, 2))
    swapped = lax.all_to_all(split, "tp", split_axis=0, concat_axis=0, tiled=True)
    return jnp.sum(swapped.astype(jnp.float32), axis=0).astype(jnp.bfloat16)


def solution(mesh):
    placed = (P("ctx", "tp"), P("ctx", "tp"), P("ctx", "tp"), P("ctx", None), P(), P("tp", None))
    return jax.shard_map(
        local, mesh=mesh, in_specs=placed, out_specs=P("ctx", "tp"), check_vma=False
    )
```

```python
import functools
import math

import jax
import jax.numpy as jnp
from jax import lax
from jax.experimental import pallas as pl
from jax.experimental.pallas import tpu as pltpu
from jax.sharding import PartitionSpec as P

HD = 128
TOK_DEV = 384
TILE = 16
PAD = 128
CHUNKS = 2

rope_base = 1000000.0
masked_score = -1e30
exp2_scale = math.log2(math.e) / math.sqrt(HD)
VMEM_BYTES = 58 * 1024 * 1024


def whole_vmem():
    return pl.BlockSpec(memory_space=pltpu.VMEM)


def whole_smem():
    return pl.BlockSpec(memory_space=pltpu.SMEM)


def params():
    return pltpu.CompilerParams(vmem_limit_bytes=VMEM_BYTES)


def small_cost():
    return pl.CostEstimate(flops=1024, bytes_accessed=1024, transcendentals=0)


def turn(rows, cosine, sine):
    as_float = rows.astype(jnp.float32)
    swapped = pltpu.roll(as_float, HD // 2, 1)
    return (as_float * cosine + swapped * sine).astype(jnp.bfloat16)


def rows_below(start, cls, block):
    whole = lax.div(start, TOK_DEV)
    return whole * block + jnp.clip(start - whole * TOK_DEV - cls * block, 0, block)


def slots_kernel(reach, groups, block, cap, me_ref, count_ref, rank_ref, kv_out, q_out):
    me = me_ref[0]
    rows = rank_ref.shape[1]
    start = jnp.int32(0)
    for s in range(count_ref.shape[0]):
        start = start + jnp.where(s < me, count_ref[s], 0)
    kept = rank_ref[...] < count_ref[me]
    upper = lax.broadcasted_iota(jnp.int32, (rows, rows), 0) <= lax.broadcasted_iota(
        jnp.int32, (rows, rows), 1
    )
    flags = jnp.broadcast_to(kept.astype(jnp.float32), (8, rows)).astype(jnp.bfloat16)
    order = (
        jnp.dot(
            flags, upper.astype(jnp.float32).astype(jnp.bfloat16), preferred_element_type=jnp.float32
        )[:1].astype(jnp.int32)
        - 1
    )
    kv_out[...] = jnp.where(kept, order + (start & (TILE - 1)), -1)
    place = start + order
    first = lax.div(start, TOK_DEV)
    device = first + jnp.zeros_like(place)
    for step in range(1, reach + 1):
        device = device + (place >= (first + step) * TOK_DEV).astype(jnp.int32)
    within = place - device * TOK_DEV
    cls = jnp.zeros_like(place)
    for step in range(1, groups):
        cls = cls + (within >= step * block).astype(jnp.int32)
    low = first * block + jnp.clip(start - first * TOK_DEV - cls * block, 0, block)
    slot = cls * cap + device * block + within - cls * block - low + (low & (TILE - 1))
    q_out[...] = jnp.where(kept, slot, -1)


def find_slots(me, counts, ranks, reach, groups, block, cap):
    shape = jax.ShapeDtypeStruct(ranks.shape, jnp.int32)
    return pl.pallas_call(
        functools.partial(slots_kernel, reach, groups, block, cap),
        in_specs=[whole_smem(), whole_smem(), whole_vmem()],
        out_specs=[whole_vmem()] * 2,
        out_shape=[shape, shape],
        compiler_params=params(),
        cost_estimate=small_cost(),
    )(me, counts, ranks)


def pack_kernel(turned, classes, cap, width, slot_ref, cos_ref, sin_ref, row_ref, *rest):
    out_refs, hot_ref = rest[:-1], rest[-1]

    @pl.when(pl.program_id(0) == 0)
    def _():
        ids = lax.broadcasted_iota(jnp.int32, hot_ref.shape, 0)
        hot_ref[...] = (ids == slot_ref[...]).astype(jnp.float32).astype(jnp.bfloat16)

    if turned:
        rows = jnp.concatenate(
            [
                turn(row_ref[:, h * HD : (h + 1) * HD], cos_ref[...], sin_ref[...])
                for h in range(width)
            ],
            axis=1,
        )
    else:
        rows = row_ref[...]
    for j, out_ref in enumerate(out_refs):
        for r in range(classes):
            first = (j * classes + r) * cap
            moved = jnp.dot(
                hot_ref[first : first + cap, :], rows, preferred_element_type=jnp.float32
            ).astype(jnp.bfloat16)
            for h in range(width):
                out_ref[h, r] = moved[:, h * HD : (h + 1) * HD]


def pack(slots, cosine, sine, rows, turned, chunks, classes, cap):
    count = rows.shape[0]
    heads = rows.shape[1] // HD
    width = min(2, heads)
    fixed = lambda i: (0, 0)
    total = chunks * classes * cap
    return pl.pallas_call(
        functools.partial(pack_kernel, turned, classes, cap, width),
        grid=(heads // width,),
        in_specs=[
            pl.BlockSpec((1, count), fixed),
            pl.BlockSpec((count, HD), fixed),
            pl.BlockSpec((count, HD), fixed),
            pl.BlockSpec((count, width * HD), lambda i: (0, i)),
        ],
        out_specs=[pl.BlockSpec((width, classes, cap, HD), lambda i: (i, 0, 0, 0))] * chunks,
        out_shape=[jax.ShapeDtypeStruct((heads, classes, cap, HD), jnp.bfloat16)] * chunks,
        scratch_shapes=[pltpu.VMEM((total, count), jnp.bfloat16)],
        compiler_params=params(),
        cost_estimate=small_cost(),
    )(slots, cosine, sine, rows)


def piece_rows(cap):
    return max(rows for rows in range(TILE, PAD + 1, TILE) if cap % rows == 0)


def merge_pieces(low, high, piece, source, add):
    shift = low & (TILE - 1)
    pieces = jnp.where(high > low, lax.div(high - low + shift + piece - 1, piece), 0)
    first = low - shift

    def one(i, carry):
        at = pl.multiple_of(first + i * piece, TILE)
        add(at, source(pl.multiple_of(i * piece, TILE)))
        return carry

    lax.fori_loop(0, pieces, one, 0)


def compact_kernel(offsets, per, total, as_keys, member_ref, count_ref, *rest):
    parts, out, all_rows, starts = rest[:-3], rest[-3], rest[-2], rest[-1]
    members = len(parts)
    piece = piece_rows(parts[0].shape[1])
    all_rows[...] = jnp.zeros_like(all_rows)
    start = jnp.int32(0)
    for s in range(count_ref.shape[0]):
        starts[s] = start
        start = start + count_ref[s]

    def add(at, rows):
        all_rows[pl.ds(at, piece), :] += rows

    for part, offset in zip(parts, offsets):
        for z in range(per):
            source = z * members + (member_ref[0] ^ offset)
            low = starts[source]
            merge_pieces(
                low,
                low + count_ref[source],
                piece,
                lambda at: part[z, pl.ds(at, piece), :],
                add,
            )
    if as_keys:
        for first in range(0, total, 2 * TOK_DEV):
            out[:, first : first + 2 * TOK_DEV] = jnp.transpose(
                all_rows[first : first + 2 * TOK_DEV, :]
            )
    else:
        out[:, :HD] = all_rows[:total, :]
        out[:, HD:] = jnp.ones((total, HD), jnp.bfloat16)


def compact(member, counts, parts, offsets, total, as_keys):
    per = parts[0].shape[0]
    return pl.pallas_call(
        functools.partial(compact_kernel, offsets, per, total, as_keys),
        in_specs=[whole_smem(), whole_smem()] + [whole_vmem()] * len(parts),
        out_specs=whole_vmem(),
        out_shape=jax.ShapeDtypeStruct(
            (HD, total) if as_keys else (total, 2 * HD), jnp.bfloat16
        ),
        scratch_shapes=[
            pltpu.VMEM((total + PAD, HD), jnp.bfloat16),
            pltpu.SMEM(counts.shape, jnp.int32),
        ],
        compiler_params=params(),
        cost_estimate=small_cost(),
    )(member, counts, *parts)


def attend_kernel(ctx_size, block, cls_ref, count_ref, got_ref, key_ref, value_ref, out_ref,
                  query_all, scores_a, scores_b, top_a, top_b, run_max, run_acc):
    span = 2 * TOK_DEV
    pair = 4 * block
    supers = ctx_size // 4
    steps = supers * (supers + 1)
    cls = cls_ref[0]
    piece = piece_rows(got_ref.shape[1])
    query_all[...] = jnp.zeros_like(query_all)

    def add(at, rows):
        query_all[pl.ds(at, piece), :] += rows

    start = jnp.int32(0)
    for s in range(ctx_size):
        end = start + count_ref[s]
        merge_pieces(
            rows_below(start, cls, block),
            rows_below(end, cls, block),
            piece,
            lambda at: got_ref[s, pl.ds(at, piece), :],
            add,
        )
        start = end

    def row_top(found):
        return jnp.broadcast_to(jnp.max(found, axis=1, keepdims=True), (pair, HD))

    def score(scores, top, i, k):
        rows = query_all[pl.ds(pl.multiple_of(jnp.minimum(i, supers - 1) * pair, TILE), pair), :]
        keys = key_ref[:, pl.ds(pl.multiple_of(k * span, HD), span)]
        found = jnp.dot(rows, keys, preferred_element_type=jnp.float32)
        scores[...] = found
        top[...] = row_top(found)

    def mask(scores, top, first):
        row_ids = lax.broadcasted_iota(jnp.int32, (pair, HD), 0)
        row = row_ids + cls * block - first
        for n in range(1, 4):
            row = row + jnp.where(row_ids >= n * block, TOK_DEV - block, 0)
        col = lax.broadcasted_iota(jnp.int32, (pair, span), 1)
        found = jnp.where(
            col <= jnp.concatenate([row] * (span // HD), axis=1), scores[...], masked_score
        )
        scores[...] = found
        top[...] = row_top(found)

    def absorb(scores, top, k):
        before = run_max[...]
        after = jnp.maximum(before, top[...])
        rescale = jnp.exp2((before - after) * exp2_scale)
        run_max[...] = after
        weights = jnp.exp2(
            (scores[...] - jnp.concatenate([after] * (span // HD), axis=1)) * exp2_scale
        )
        values = value_ref[pl.ds(pl.multiple_of(k * span, TILE), span), :]
        run_acc[...] = run_acc[...] * jnp.concatenate([rescale, rescale], axis=1) + jnp.dot(
            weights.astype(jnp.bfloat16), values, preferred_element_type=jnp.float32
        )

    def clear():
        run_max[...] = jnp.full_like(run_max, masked_score)
        run_acc[...] = jnp.zeros_like(run_acc)

    def one_step(now, later, i, k):
        last = k == 2 * i + 1
        next_i = jnp.where(last, i + 1, i)
        next_k = jnp.where(last, 0, k + 1)
        score(*later, next_i, next_k)
        absorb(*now, k)

        @pl.when(last)
        def _():
            result = (run_acc[:, :HD] / run_acc[:, HD:]).astype(jnp.bfloat16)
            for n in range(4):
                out_ref[4 * i + n] = result[n * block : (n + 1) * block]
            clear()

        @pl.when(next_k >= 2 * next_i)
        def _():
            mask(*later, (next_k - 2 * next_i) * span)

        return next_i, next_k

    buffers_a, buffers_b = (scores_a, top_a), (scores_b, top_b)
    clear()
    score(*buffers_a, 0, 0)
    mask(*buffers_a, 0)

    def two_steps(t, at):
        at = one_step(buffers_a, buffers_b, *at)
        return one_step(buffers_b, buffers_a, *at)

    lax.fori_loop(0, steps // 2, two_steps, (jnp.int32(0), jnp.int32(0)))


def attend(cls, counts, got, keys, values, block):
    ctx_size = got.shape[0]
    total = values.shape[0]
    pairs = total * ctx_size * block // 2
    return pl.pallas_call(
        functools.partial(attend_kernel, ctx_size, block),
        in_specs=[whole_smem()] * 2 + [whole_vmem()] * 3,
        out_specs=whole_vmem(),
        out_shape=jax.ShapeDtypeStruct((ctx_size, block, HD), jnp.bfloat16),
        scratch_shapes=[
            pltpu.VMEM((ctx_size * block + PAD, HD), jnp.bfloat16),
            pltpu.VMEM((4 * block, 2 * TOK_DEV), jnp.float32),
            pltpu.VMEM((4 * block, 2 * TOK_DEV), jnp.float32),
            pltpu.VMEM((4 * block, HD), jnp.float32),
            pltpu.VMEM((4 * block, HD), jnp.float32),
            pltpu.VMEM((4 * block, HD), jnp.float32),
            pltpu.VMEM((4 * block, 2 * HD), jnp.float32),
        ],
        compiler_params=params(),
        cost_estimate=small_cost(),
    )(cls, counts, got, keys, values)


def project_kernel(classes, chunks, column_ref, *rest):
    got_refs, (weight_ref, out_ref, rows_ref) = rest[:chunks], rest[chunks:]
    block = got_refs[0].shape[1]

    @pl.when(pl.program_id(0) == 0)
    def _():
        for j, got_ref in enumerate(got_refs):
            for d in range(got_ref.shape[0]):
                h, r = d // classes, d % classes
                first = (j * classes + r) * block
                rows_ref[first : first + block, h * HD : (h + 1) * HD] = got_ref[d]

    out_ref[...] = jnp.dot(
        rows_ref[...], weight_ref[...], preferred_element_type=jnp.float32
    ).astype(jnp.bfloat16)


def project(first_column, got, weight, columns, classes):
    ctx_size, block, _ = got[0].shape
    rows, depth = len(got) * classes * block, weight.shape[0]
    step = min(512, columns)
    return pl.pallas_call(
        functools.partial(project_kernel, classes, len(got)),
        grid_spec=pltpu.PrefetchScalarGridSpec(
            num_scalar_prefetch=1,
            grid=(columns // step,),
            in_specs=[pl.BlockSpec((ctx_size, block, HD), lambda i, first: (0, 0, 0))] * len(got)
            + [pl.BlockSpec((depth, step), lambda i, first: (0, first[0] + i))],
            out_specs=pl.BlockSpec((rows, step), lambda i, first: (0, i)),
            scratch_shapes=[pltpu.VMEM((rows, depth), jnp.bfloat16)],
        ),
        out_shape=jax.ShapeDtypeStruct((rows, columns), jnp.bfloat16),
        compiler_params=params(),
        cost_estimate=small_cost(),
    )((first_column // step).astype(jnp.int32).reshape(1), *got, weight)


def join_kernel(chunks, parts, head_ref, *rest):
    got_refs, weight_refs = rest[:chunks], rest[chunks : chunks + parts]
    own_ref, out_ref, rows_ref = rest[chunks + parts :]
    block = got_refs[0].shape[1]
    firsts = [sum(ref.shape[0] for ref in weight_refs[:p]) for p in range(parts)]

    @pl.when(pl.program_id(0) == 0)
    def _():
        for j, got_ref in enumerate(got_refs):
            for p in range(parts):
                for n in range(weight_refs[p].shape[0] // HD):
                    at = firsts[p] + n * HD
                    rows_ref[j * block : (j + 1) * block, at : at + HD] = got_ref[head_ref[p] + n]

    total = jnp.zeros(out_ref.shape, jnp.float32)
    for first, weight_ref in zip(firsts, weight_refs):
        total = total + jnp.dot(
            rows_ref[:, first : first + weight_ref.shape[0]],
            weight_ref[...],
            preferred_element_type=jnp.float32,
        )
    theirs = total.astype(jnp.bfloat16).astype(jnp.float32)
    out_ref[...] = (own_ref[...].astype(jnp.float32) + theirs).astype(jnp.bfloat16)


def join(first_heads, got, weights, own):
    ctx_size, block, _ = got[0].shape
    rows, columns = own.shape
    depth = sum(weight.shape[0] for weight in weights)
    step = min(512, columns)
    tile = pl.BlockSpec((rows, step), lambda i, first: (0, i))
    return pl.pallas_call(
        functools.partial(join_kernel, len(got), len(weights)),
        grid_spec=pltpu.PrefetchScalarGridSpec(
            num_scalar_prefetch=1,
            grid=(columns // step,),
            in_specs=[pl.BlockSpec((ctx_size, block, HD), lambda i, first: (0, 0, 0))] * len(got)
            + [pl.BlockSpec((weight.shape[0], step), lambda i, first: (0, i)) for weight in weights]
            + [tile],
            out_specs=tile,
            scratch_shapes=[pltpu.VMEM((rows, depth), jnp.bfloat16)],
        ),
        out_shape=jax.ShapeDtypeStruct((rows, columns), jnp.bfloat16),
        compiler_params=params(),
        cost_estimate=small_cost(),
    )(first_heads, *got, *weights, own)


def tables(query_rows):
    half_dim = HD // 2
    positions = lax.axis_index("ctx") * query_rows + jnp.arange(query_rows, dtype=jnp.int32)
    lane = jnp.arange(HD, dtype=jnp.int32)
    pair_id = jnp.where(lane < half_dim, lane, lane - half_dim)
    inv_freq = rope_base ** (-(pair_id.astype(jnp.float32) * 2.0 / HD))
    angles = positions.astype(jnp.float32)[:, None] * inv_freq[None, :]
    sine = jnp.sin(angles)
    return jnp.cos(angles), jnp.where(lane[None, :] < half_dim, -sine, sine)


def local(query, key, value, keep_rank, kept_count, out_weight):
    ctx_size = lax.axis_size("ctx")
    tp_size = lax.axis_size("tp")
    me = lax.axis_index("ctx")
    tp_me = lax.axis_index("tp")
    orig_rows = query.shape[0]
    heads = query.shape[1] // HD
    kv_heads = key.shape[1] // HD
    members = ctx_size // kv_heads
    classes = ctx_size // heads
    chunks = CHUNKS if classes == 1 else 1
    block = TOK_DEV // (chunks * classes)
    total = ctx_size * TOK_DEV
    reach = orig_rows // TOK_DEV
    cap = reach * block + TILE
    cap_kv = orig_rows + TILE
    columns = out_weight.shape[1] // tp_size

    kv_slots, q_slots = find_slots(
        me.reshape(1), kept_count, keep_rank, reach, chunks * classes, block, cap
    )
    cosine, sine = tables(orig_rows)

    across = [[z * members + m for z in range(kv_heads)] for m in range(members)]

    member = (me & (members - 1)).reshape(1)

    def pack_shared(rows, turned):
        (packed,) = pack(kv_slots, cosine, sine, rows, turned, 1, 1, cap_kv)
        return packed.reshape(kv_heads, cap_kv, HD)

    def send_across(packed):
        if kv_heads == 1:
            return packed
        return lax.all_to_all(
            packed, "ctx", split_axis=0, concat_axis=0, tiled=True, axis_index_groups=across
        )

    def swap(parts, bit):
        pairs = [(d, d ^ bit) for d in range(ctx_size)]
        return parts + [lax.ppermute(part, "ctx", pairs) for part in parts]

    bits = [members >> n for n in range(1, members.bit_length())]
    offsets = [0]
    for bit in bits:
        offsets = offsets + [offset ^ bit for offset in offsets]

    def send_query(packed):
        return lax.all_to_all(
            packed.reshape(ctx_size, cap, HD), "ctx", split_axis=0, concat_axis=0, tiled=True
        )

    traded = tp_size == 2 and classes == 1 and heads == 16 and chunks == 2
    both = [(0, 1), (1, 0)]

    def chip_swap(part, bit):
        return lax.ppermute(part, "ctx", [(d, d ^ bit) for d in range(ctx_size)])

    core, side = me & 1, (me >> 1) & 1
    sizes = [2, 2, 2]

    def weight_rows(p):
        low = sum(sizes[:p])
        first = jnp.where(side == 0, low, 8 - low - sizes[p]) + core * 8
        return lax.dynamic_slice(
            out_weight, (first * HD, (1 - tp_me) * columns), (sizes[p] * HD, columns)
        )

    def trade(part):
        return lax.ppermute(part, "tp", both)

    key_parts = [send_across(pack_shared(key, True))]
    slices = [weight_rows(p) for p in range(len(sizes))] if traded else []
    value_packed, key_parts, slices = lax.optimization_barrier(
        (pack_shared(value, False), key_parts, slices)
    )
    key_parts = swap(key_parts, bits[0])
    value_parts = [send_across(value_packed)]
    packed_q = list(pack(q_slots, cosine, sine, query, True, chunks, classes, cap))
    came = [trade(slices[0])] if traded else []
    packed_q[0], key_parts, value_parts, slices = lax.optimization_barrier(
        (packed_q[0], key_parts, value_parts, slices)
    )
    came = came + [trade(one) for one in slices[1:]]
    got_q = [send_query(packed_q[0])]
    value_parts = swap(value_parts, bits[0])
    for bit in bits[1:]:
        key_parts = swap(key_parts, bit)
    keys = compact(member, kept_count, key_parts, offsets, total, True)
    if chunks > 1:
        packed_q[1], value_parts, keys = lax.optimization_barrier(
            (packed_q[1], value_parts, keys)
        )
    for bit in bits[1:]:
        value_parts = swap(value_parts, bit)
    got_q = got_q + [send_query(packed) for packed in packed_q[1:]]
    values = compact(member, kept_count, value_parts, offsets, total, False)
    if traded:
        got_q[0], turned_part = lax.optimization_barrier((got_q[0], came[0]))
        came = came + [chip_swap(turned_part, 2)]

    got, done = [], None
    for j in range(chunks):
        cls_j = j * classes + (me & (classes - 1))
        if j > 0:
            got_q[j], done = lax.optimization_barrier((got_q[j], done))
            got.append(lax.all_to_all(done, "ctx", split_axis=0, concat_axis=0, tiled=True))
        done = attend(cls_j.reshape(1), kept_count, got_q[j], keys, values, block)
    if traded:
        done, came = lax.optimization_barrier((done, came))
    got.append(lax.all_to_all(done, "ctx", split_axis=0, concat_axis=0, tiled=True))
    if traded:
        theirs = [trade(one) for one in got]
        came = came + [chip_swap(part, 1) for part in came]
        own = project(tp_me * columns, got, out_weight, columns, classes)
        ups = [sum(sizes[:p]) for p in range(3)]
        order = [
            jnp.where(side == 0, up, 8 - up - size) for up, size in zip(ups, sizes)
        ] + [jnp.where(side == 0, 6, 0)]
        first_heads = jnp.stack([c * 8 + at for c in (core, 1 - core) for at in order])
        return join(first_heads.astype(jnp.int32), theirs, came, own)
    full = project(jnp.int32(0) * tp_me, got, out_weight, columns * tp_size, classes)
    split = jnp.transpose(full.reshape(full.shape[0], tp_size, columns), (1, 0, 2))
    swapped = lax.all_to_all(split, "tp", split_axis=0, concat_axis=0, tiled=True)
    return jnp.sum(swapped.astype(jnp.float32), axis=0).astype(jnp.bfloat16)


def solution(mesh):
    placed = (P("ctx", "tp"), P("ctx", "tp"), P("ctx", "tp"), P("ctx", None), P(), P("tp", None))
    return jax.shard_map(
        local, mesh=mesh, in_specs=placed, out_specs=P("ctx", "tp"), check_vma=False
    )
```

```python
import functools
import math

import jax
import jax.numpy as jnp
from jax import lax
from jax.experimental import pallas as pl
from jax.experimental.pallas import tpu as pltpu
from jax.sharding import PartitionSpec as P

HD = 128
TOK_DEV = 384
TILE = 16
PAD = 128
CHUNKS = 2

rope_base = 1000000.0
masked_score = -1e30
exp2_scale = math.log2(math.e) / math.sqrt(HD)
VMEM_BYTES = 58 * 1024 * 1024


def whole_vmem():
    return pl.BlockSpec(memory_space=pltpu.VMEM)


def whole_smem():
    return pl.BlockSpec(memory_space=pltpu.SMEM)


def params():
    return pltpu.CompilerParams(vmem_limit_bytes=VMEM_BYTES)


def small_cost():
    return pl.CostEstimate(flops=1024, bytes_accessed=1024, transcendentals=0)


def turn(rows, cosine, sine):
    as_float = rows.astype(jnp.float32)
    swapped = pltpu.roll(as_float, HD // 2, 1)
    return (as_float * cosine + swapped * sine).astype(jnp.bfloat16)


def rows_below(start, cls, block):
    whole = lax.div(start, TOK_DEV)
    return whole * block + jnp.clip(start - whole * TOK_DEV - cls * block, 0, block)


def slots_kernel(reach, groups, block, cap, me_ref, count_ref, rank_ref, kv_out, q_out):
    me = me_ref[0]
    rows = rank_ref.shape[1]
    start = jnp.int32(0)
    for s in range(count_ref.shape[0]):
        start = start + jnp.where(s < me, count_ref[s], 0)
    kept = rank_ref[...] < count_ref[me]
    upper = lax.broadcasted_iota(jnp.int32, (rows, rows), 0) <= lax.broadcasted_iota(
        jnp.int32, (rows, rows), 1
    )
    flags = jnp.broadcast_to(kept.astype(jnp.float32), (8, rows)).astype(jnp.bfloat16)
    order = (
        jnp.dot(
            flags, upper.astype(jnp.float32).astype(jnp.bfloat16), preferred_element_type=jnp.float32
        )[:1].astype(jnp.int32)
        - 1
    )
    kv_out[...] = jnp.where(kept, order + (start & (TILE - 1)), -1)
    place = start + order
    first = lax.div(start, TOK_DEV)
    device = first + jnp.zeros_like(place)
    for step in range(1, reach + 1):
        device = device + (place >= (first + step) * TOK_DEV).astype(jnp.int32)
    within = place - device * TOK_DEV
    cls = jnp.zeros_like(place)
    for step in range(1, groups):
        cls = cls + (within >= step * block).astype(jnp.int32)
    low = first * block + jnp.clip(start - first * TOK_DEV - cls * block, 0, block)
    slot = cls * cap + device * block + within - cls * block - low + (low & (TILE - 1))
    q_out[...] = jnp.where(kept, slot, -1)


def find_slots(me, counts, ranks, reach, groups, block, cap):
    shape = jax.ShapeDtypeStruct(ranks.shape, jnp.int32)
    return pl.pallas_call(
        functools.partial(slots_kernel, reach, groups, block, cap),
        in_specs=[whole_smem(), whole_smem(), whole_vmem()],
        out_specs=[whole_vmem()] * 2,
        out_shape=[shape, shape],
        compiler_params=params(),
        cost_estimate=small_cost(),
    )(me, counts, ranks)


def pack_kernel(turned, classes, cap, width, slot_ref, cos_ref, sin_ref, row_ref, *rest):
    out_refs, hot_ref = rest[:-1], rest[-1]

    @pl.when(pl.program_id(0) == 0)
    def _():
        ids = lax.broadcasted_iota(jnp.int32, hot_ref.shape, 0)
        hot_ref[...] = (ids == slot_ref[...]).astype(jnp.float32).astype(jnp.bfloat16)

    if turned:
        rows = jnp.concatenate(
            [
                turn(row_ref[:, h * HD : (h + 1) * HD], cos_ref[...], sin_ref[...])
                for h in range(width)
            ],
            axis=1,
        )
    else:
        rows = row_ref[...]
    for j, out_ref in enumerate(out_refs):
        for r in range(classes):
            first = (j * classes + r) * cap
            moved = jnp.dot(
                hot_ref[first : first + cap, :], rows, preferred_element_type=jnp.float32
            ).astype(jnp.bfloat16)
            for h in range(width):
                out_ref[h, r] = moved[:, h * HD : (h + 1) * HD]


def pack(slots, cosine, sine, rows, turned, chunks, classes, cap):
    count = rows.shape[0]
    heads = rows.shape[1] // HD
    width = min(2, heads)
    fixed = lambda i: (0, 0)
    total = chunks * classes * cap
    return pl.pallas_call(
        functools.partial(pack_kernel, turned, classes, cap, width),
        grid=(heads // width,),
        in_specs=[
            pl.BlockSpec((1, count), fixed),
            pl.BlockSpec((count, HD), fixed),
            pl.BlockSpec((count, HD), fixed),
            pl.BlockSpec((count, width * HD), lambda i: (0, i)),
        ],
        out_specs=[pl.BlockSpec((width, classes, cap, HD), lambda i: (i, 0, 0, 0))] * chunks,
        out_shape=[jax.ShapeDtypeStruct((heads, classes, cap, HD), jnp.bfloat16)] * chunks,
        scratch_shapes=[pltpu.VMEM((total, count), jnp.bfloat16)],
        compiler_params=params(),
        cost_estimate=small_cost(),
    )(slots, cosine, sine, rows)


def piece_rows(cap):
    return max(rows for rows in range(TILE, PAD + 1, TILE) if cap % rows == 0)


def merge_pieces(low, high, piece, source, add):
    shift = low & (TILE - 1)
    pieces = jnp.where(high > low, lax.div(high - low + shift + piece - 1, piece), 0)
    first = low - shift

    def one(i, carry):
        at = pl.multiple_of(first + i * piece, TILE)
        add(at, source(pl.multiple_of(i * piece, TILE)))
        return carry

    lax.fori_loop(0, pieces, one, 0)


def compact_kernel(offsets, per, total, as_keys, member_ref, count_ref, *rest):
    parts, out, all_rows, starts = rest[:-3], rest[-3], rest[-2], rest[-1]
    members = len(parts)
    piece = piece_rows(parts[0].shape[1])
    all_rows[...] = jnp.zeros_like(all_rows)
    start = jnp.int32(0)
    for s in range(count_ref.shape[0]):
        starts[s] = start
        start = start + count_ref[s]

    def add(at, rows):
        all_rows[pl.ds(at, piece), :] += rows

    for part, offset in zip(parts, offsets):
        for z in range(per):
            source = z * members + (member_ref[0] ^ offset)
            low = starts[source]
            merge_pieces(
                low,
                low + count_ref[source],
                piece,
                lambda at: part[z, pl.ds(at, piece), :],
                add,
            )
    if as_keys:
        for first in range(0, total, 2 * TOK_DEV):
            out[:, first : first + 2 * TOK_DEV] = jnp.transpose(
                all_rows[first : first + 2 * TOK_DEV, :]
            )
    else:
        out[:, :HD] = all_rows[:total, :]
        out[:, HD:] = jnp.ones((total, HD), jnp.bfloat16)


def compact(member, counts, parts, offsets, total, as_keys):
    per = parts[0].shape[0]
    return pl.pallas_call(
        functools.partial(compact_kernel, offsets, per, total, as_keys),
        in_specs=[whole_smem(), whole_smem()] + [whole_vmem()] * len(parts),
        out_specs=whole_vmem(),
        out_shape=jax.ShapeDtypeStruct(
            (HD, total) if as_keys else (total, 2 * HD), jnp.bfloat16
        ),
        scratch_shapes=[
            pltpu.VMEM((total + PAD, HD), jnp.bfloat16),
            pltpu.SMEM(counts.shape, jnp.int32),
        ],
        compiler_params=params(),
        cost_estimate=small_cost(),
    )(member, counts, *parts)


def attend_kernel(ctx_size, block, cls_ref, count_ref, got_ref, key_ref, value_ref, out_ref,
                  query_all, scores_a, scores_b, top_a, top_b, run_max, run_acc):
    span = 2 * TOK_DEV
    pair = 4 * block
    supers = ctx_size // 4
    steps = supers * (supers + 1)
    cls = cls_ref[0]
    piece = piece_rows(got_ref.shape[1])
    query_all[...] = jnp.zeros_like(query_all)

    def add(at, rows):
        query_all[pl.ds(at, piece), :] += rows

    start = jnp.int32(0)
    for s in range(ctx_size):
        end = start + count_ref[s]
        merge_pieces(
            rows_below(start, cls, block),
            rows_below(end, cls, block),
            piece,
            lambda at: got_ref[s, pl.ds(at, piece), :],
            add,
        )
        start = end

    def row_top(found):
        return jnp.broadcast_to(jnp.max(found, axis=1, keepdims=True), (pair, HD))

    def score(scores, top, i, k):
        rows = query_all[pl.ds(pl.multiple_of(jnp.minimum(i, supers - 1) * pair, TILE), pair), :]
        keys = key_ref[:, pl.ds(pl.multiple_of(k * span, HD), span)]
        found = jnp.dot(rows, keys, preferred_element_type=jnp.float32)
        scores[...] = found
        top[...] = row_top(found)

    def mask(scores, top, first):
        row_ids = lax.broadcasted_iota(jnp.int32, (pair, HD), 0)
        row = row_ids + cls * block - first
        for n in range(1, 4):
            row = row + jnp.where(row_ids >= n * block, TOK_DEV - block, 0)
        col = lax.broadcasted_iota(jnp.int32, (pair, span), 1)
        found = jnp.where(
            col <= jnp.concatenate([row] * (span // HD), axis=1), scores[...], masked_score
        )
        scores[...] = found
        top[...] = row_top(found)

    def absorb(scores, top, k):
        before = run_max[...]
        after = jnp.maximum(before, top[...])
        rescale = jnp.exp2((before - after) * exp2_scale)
        run_max[...] = after
        weights = jnp.exp2(
            (scores[...] - jnp.concatenate([after] * (span // HD), axis=1)) * exp2_scale
        )
        values = value_ref[pl.ds(pl.multiple_of(k * span, TILE), span), :]
        run_acc[...] = run_acc[...] * jnp.concatenate([rescale, rescale], axis=1) + jnp.dot(
            weights.astype(jnp.bfloat16), values, preferred_element_type=jnp.float32
        )

    def clear():
        run_max[...] = jnp.full_like(run_max, masked_score)
        run_acc[...] = jnp.zeros_like(run_acc)

    def one_step(now, later, i, k):
        last = k == 2 * i + 1
        next_i = jnp.where(last, i + 1, i)
        next_k = jnp.where(last, 0, k + 1)
        score(*later, next_i, next_k)
        absorb(*now, k)

        @pl.when(last)
        def _():
            result = (run_acc[:, :HD] / run_acc[:, HD:]).astype(jnp.bfloat16)
            for n in range(4):
                out_ref[4 * i + n] = result[n * block : (n + 1) * block]
            clear()

        @pl.when(next_k >= 2 * next_i)
        def _():
            mask(*later, (next_k - 2 * next_i) * span)

        return next_i, next_k

    buffers_a, buffers_b = (scores_a, top_a), (scores_b, top_b)
    clear()
    score(*buffers_a, 0, 0)
    mask(*buffers_a, 0)

    def two_steps(t, at):
        at = one_step(buffers_a, buffers_b, *at)
        return one_step(buffers_b, buffers_a, *at)

    lax.fori_loop(0, steps // 2, two_steps, (jnp.int32(0), jnp.int32(0)))


def attend(cls, counts, got, keys, values, block):
    ctx_size = got.shape[0]
    total = values.shape[0]
    pairs = total * ctx_size * block // 2
    return pl.pallas_call(
        functools.partial(attend_kernel, ctx_size, block),
        in_specs=[whole_smem()] * 2 + [whole_vmem()] * 3,
        out_specs=whole_vmem(),
        out_shape=jax.ShapeDtypeStruct((ctx_size, block, HD), jnp.bfloat16),
        scratch_shapes=[
            pltpu.VMEM((ctx_size * block + PAD, HD), jnp.bfloat16),
            pltpu.VMEM((4 * block, 2 * TOK_DEV), jnp.float32),
            pltpu.VMEM((4 * block, 2 * TOK_DEV), jnp.float32),
            pltpu.VMEM((4 * block, HD), jnp.float32),
            pltpu.VMEM((4 * block, HD), jnp.float32),
            pltpu.VMEM((4 * block, HD), jnp.float32),
            pltpu.VMEM((4 * block, 2 * HD), jnp.float32),
        ],
        compiler_params=params(),
        cost_estimate=small_cost(),
    )(cls, counts, got, keys, values)


def project_kernel(classes, chunks, column_ref, *rest):
    got_refs, (weight_ref, out_ref, rows_ref) = rest[:chunks], rest[chunks:]
    block = got_refs[0].shape[1]

    @pl.when(pl.program_id(0) == 0)
    def _():
        for j, got_ref in enumerate(got_refs):
            for d in range(got_ref.shape[0]):
                h, r = d // classes, d % classes
                first = (j * classes + r) * block
                rows_ref[first : first + block, h * HD : (h + 1) * HD] = got_ref[d]

    out_ref[...] = jnp.dot(
        rows_ref[...], weight_ref[...], preferred_element_type=jnp.float32
    ).astype(jnp.bfloat16)


def project(first_column, got, weight, columns, classes):
    ctx_size, block, _ = got[0].shape
    rows, depth = len(got) * classes * block, weight.shape[0]
    step = min(512, columns)
    return pl.pallas_call(
        functools.partial(project_kernel, classes, len(got)),
        grid_spec=pltpu.PrefetchScalarGridSpec(
            num_scalar_prefetch=1,
            grid=(columns // step,),
            in_specs=[pl.BlockSpec((ctx_size, block, HD), lambda i, first: (0, 0, 0))] * len(got)
            + [pl.BlockSpec((depth, step), lambda i, first: (0, first[0] + i))],
            out_specs=pl.BlockSpec((rows, step), lambda i, first: (0, i)),
            scratch_shapes=[pltpu.VMEM((rows, depth), jnp.bfloat16)],
        ),
        out_shape=jax.ShapeDtypeStruct((rows, columns), jnp.bfloat16),
        compiler_params=params(),
        cost_estimate=small_cost(),
    )((first_column // step).astype(jnp.int32).reshape(1), *got, weight)


def join_kernel(chunks, parts, head_ref, *rest):
    got_refs, weight_refs = rest[:chunks], rest[chunks : chunks + parts]
    own_ref, out_ref, rows_ref = rest[chunks + parts :]
    block = got_refs[0].shape[1]
    firsts = [sum(ref.shape[0] for ref in weight_refs[:p]) for p in range(parts)]

    @pl.when(pl.program_id(0) == 0)
    def _():
        for j, got_ref in enumerate(got_refs):
            for p in range(parts):
                for n in range(weight_refs[p].shape[0] // HD):
                    at = firsts[p] + n * HD
                    rows_ref[j * block : (j + 1) * block, at : at + HD] = got_ref[head_ref[p] + n]

    total = jnp.zeros(out_ref.shape, jnp.float32)
    for first, weight_ref in zip(firsts, weight_refs):
        total = total + jnp.dot(
            rows_ref[:, first : first + weight_ref.shape[0]],
            weight_ref[...],
            preferred_element_type=jnp.float32,
        )
    theirs = total.astype(jnp.bfloat16).astype(jnp.float32)
    out_ref[...] = (own_ref[...].astype(jnp.float32) + theirs).astype(jnp.bfloat16)


def join(first_heads, got, weights, own):
    ctx_size, block, _ = got[0].shape
    rows, columns = own.shape
    depth = sum(weight.shape[0] for weight in weights)
    step = min(512, columns)
    tile = pl.BlockSpec((rows, step), lambda i, first: (0, i))
    return pl.pallas_call(
        functools.partial(join_kernel, len(got), len(weights)),
        grid_spec=pltpu.PrefetchScalarGridSpec(
            num_scalar_prefetch=1,
            grid=(columns // step,),
            in_specs=[pl.BlockSpec((ctx_size, block, HD), lambda i, first: (0, 0, 0))] * len(got)
            + [pl.BlockSpec((weight.shape[0], step), lambda i, first: (0, i)) for weight in weights]
            + [tile],
            out_specs=tile,
            scratch_shapes=[pltpu.VMEM((rows, depth), jnp.bfloat16)],
        ),
        out_shape=jax.ShapeDtypeStruct((rows, columns), jnp.bfloat16),
        compiler_params=params(),
        cost_estimate=small_cost(),
    )(first_heads, *got, *weights, own)


def tables(query_rows):
    half_dim = HD // 2
    positions = lax.axis_index("ctx") * query_rows + jnp.arange(query_rows, dtype=jnp.int32)
    lane = jnp.arange(HD, dtype=jnp.int32)
    pair_id = jnp.where(lane < half_dim, lane, lane - half_dim)
    inv_freq = rope_base ** (-(pair_id.astype(jnp.float32) * 2.0 / HD))
    angles = positions.astype(jnp.float32)[:, None] * inv_freq[None, :]
    sine = jnp.sin(angles)
    return jnp.cos(angles), jnp.where(lane[None, :] < half_dim, -sine, sine)


def local(query, key, value, keep_rank, kept_count, out_weight):
    ctx_size = lax.axis_size("ctx")
    tp_size = lax.axis_size("tp")
    me = lax.axis_index("ctx")
    tp_me = lax.axis_index("tp")
    orig_rows = query.shape[0]
    heads = query.shape[1] // HD
    kv_heads = key.shape[1] // HD
    members = ctx_size // kv_heads
    classes = ctx_size // heads
    chunks = CHUNKS if classes == 1 else 1
    block = TOK_DEV // (chunks * classes)
    total = ctx_size * TOK_DEV
    reach = orig_rows // TOK_DEV
    cap = reach * block + TILE
    cap_kv = orig_rows + TILE
    columns = out_weight.shape[1] // tp_size

    kv_slots, q_slots = find_slots(
        me.reshape(1), kept_count, keep_rank, reach, chunks * classes, block, cap
    )
    cosine, sine = tables(orig_rows)

    across = [[z * members + m for z in range(kv_heads)] for m in range(members)]

    member = (me & (members - 1)).reshape(1)

    def pack_shared(rows, turned):
        (packed,) = pack(kv_slots, cosine, sine, rows, turned, 1, 1, cap_kv)
        return packed.reshape(kv_heads, cap_kv, HD)

    def send_across(packed):
        if kv_heads == 1:
            return packed
        return lax.all_to_all(
            packed, "ctx", split_axis=0, concat_axis=0, tiled=True, axis_index_groups=across
        )

    def swap(parts, bit):
        pairs = [(d, d ^ bit) for d in range(ctx_size)]
        return parts + [lax.ppermute(part, "ctx", pairs) for part in parts]

    bits = [members >> n for n in range(1, members.bit_length())]
    offsets = [0]
    for bit in bits:
        offsets = offsets + [offset ^ bit for offset in offsets]

    def send_query(packed):
        return lax.all_to_all(
            packed.reshape(ctx_size, cap, HD), "ctx", split_axis=0, concat_axis=0, tiled=True
        )

    traded = tp_size == 2 and classes == 1 and heads == 16 and chunks == 2
    both = [(0, 1), (1, 0)]

    def chip_swap(part, bit):
        return lax.ppermute(part, "ctx", [(d, d ^ bit) for d in range(ctx_size)])

    core, side = me & 1, (me >> 1) & 1
    sizes = [2, 4]

    def weight_rows(p):
        first = core * 8 + (jnp.where(side == 0, 0, 6) if p == 0 else 2)
        return lax.dynamic_slice(
            out_weight, (first * HD, (1 - tp_me) * columns), (sizes[p] * HD, columns)
        )

    def gather_weight(part):
        return lax.all_gather(part, "tp", axis=0)

    def trade(part):
        return lax.ppermute(part, "tp", both)

    key_parts = [send_across(pack_shared(key, True))]
    slices = [weight_rows(p) for p in range(len(sizes))] if traded else []
    value_packed, key_parts, slices = lax.optimization_barrier(
        (pack_shared(value, False), key_parts, slices)
    )
    key_parts = swap(key_parts, bits[0])
    value_parts = [send_across(value_packed)]
    packed_q = list(pack(q_slots, cosine, sine, query, True, chunks, classes, cap))
    gathered = [gather_weight(one) for one in slices]
    packed_q[0], key_parts, value_parts = lax.optimization_barrier(
        (packed_q[0], key_parts, value_parts)
    )
    got_q = [send_query(packed_q[0])]
    value_parts = swap(value_parts, bits[0])
    for bit in bits[1:]:
        key_parts = swap(key_parts, bit)
    keys = compact(member, kept_count, key_parts, offsets, total, True)
    if chunks > 1:
        packed_q[1], value_parts, keys = lax.optimization_barrier(
            (packed_q[1], value_parts, keys)
        )
    for bit in bits[1:]:
        value_parts = swap(value_parts, bit)
    got_q = got_q + [send_query(packed) for packed in packed_q[1:]]
    values = compact(member, kept_count, value_parts, offsets, total, False)
    if traded:
        got_q[0], gathered[0] = lax.optimization_barrier((got_q[0], gathered[0]))
        first_part = lax.dynamic_index_in_dim(gathered[0], 1 - tp_me, 0, keepdims=False)
        came = [first_part, chip_swap(first_part, 2)]

    got, done = [], None
    for j in range(chunks):
        cls_j = j * classes + (me & (classes - 1))
        if j > 0:
            got_q[j], done = lax.optimization_barrier((got_q[j], done))
            got.append(lax.all_to_all(done, "ctx", split_axis=0, concat_axis=0, tiled=True))
        done = attend(cls_j.reshape(1), kept_count, got_q[j], keys, values, block)
    if traded:
        done, came, gathered = lax.optimization_barrier((done, came, gathered))
        came = came + [lax.dynamic_index_in_dim(gathered[1], 1 - tp_me, 0, keepdims=False)]
    got.append(lax.all_to_all(done, "ctx", split_axis=0, concat_axis=0, tiled=True))
    if traded:
        theirs = [trade(one) for one in got]
        came = came + [chip_swap(part, 1) for part in came]
        own = project(tp_me * columns, got, out_weight, columns, classes)
        order = [jnp.where(side == 0, 0, 6), jnp.where(side == 0, 6, 0), jnp.int32(2)]
        first_heads = jnp.stack([c * 8 + at for c in (core, 1 - core) for at in order])
        return join(first_heads.astype(jnp.int32), theirs, came, own)
    full = project(jnp.int32(0) * tp_me, got, out_weight, columns * tp_size, classes)
    split = jnp.transpose(full.reshape(full.shape[0], tp_size, columns), (1, 0, 2))
    swapped = lax.all_to_all(split, "tp", split_axis=0, concat_axis=0, tiled=True)
    return jnp.sum(swapped.astype(jnp.float32), axis=0).astype(jnp.bfloat16)


def solution(mesh):
    placed = (P("ctx", "tp"), P("ctx", "tp"), P("ctx", "tp"), P("ctx", None), P(), P("tp", None))
    return jax.shard_map(
        local, mesh=mesh, in_specs=placed, out_specs=P("ctx", "tp"), check_vma=False
    )
```

```python
import functools
import math

import jax
import jax.numpy as jnp
from jax import lax
from jax.experimental import pallas as pl
from jax.experimental.pallas import tpu as pltpu
from jax.sharding import PartitionSpec as P

HD = 128
TOK_DEV = 384
TILE = 16
PAD = 128
CHUNKS = 2

rope_base = 1000000.0
masked_score = -1e30
exp2_scale = math.log2(math.e) / math.sqrt(HD)
VMEM_BYTES = 58 * 1024 * 1024


def whole_vmem():
    return pl.BlockSpec(memory_space=pltpu.VMEM)


def whole_smem():
    return pl.BlockSpec(memory_space=pltpu.SMEM)


def params():
    return pltpu.CompilerParams(vmem_limit_bytes=VMEM_BYTES)


def small_cost():
    return pl.CostEstimate(flops=1024, bytes_accessed=1024, transcendentals=0)


def turn(rows, cosine, sine):
    as_float = rows.astype(jnp.float32)
    swapped = pltpu.roll(as_float, HD // 2, 1)
    return (as_float * cosine + swapped * sine).astype(jnp.bfloat16)


def rows_below(start, cls, block):
    whole = lax.div(start, TOK_DEV)
    return whole * block + jnp.clip(start - whole * TOK_DEV - cls * block, 0, block)


def slots_kernel(reach, groups, block, cap, me_ref, count_ref, rank_ref, kv_out, q_out):
    me = me_ref[0]
    rows = rank_ref.shape[1]
    start = jnp.int32(0)
    for s in range(count_ref.shape[0]):
        start = start + jnp.where(s < me, count_ref[s], 0)
    kept = rank_ref[...] < count_ref[me]
    upper = lax.broadcasted_iota(jnp.int32, (rows, rows), 0) <= lax.broadcasted_iota(
        jnp.int32, (rows, rows), 1
    )
    flags = jnp.broadcast_to(kept.astype(jnp.float32), (8, rows)).astype(jnp.bfloat16)
    order = (
        jnp.dot(
            flags, upper.astype(jnp.float32).astype(jnp.bfloat16), preferred_element_type=jnp.float32
        )[:1].astype(jnp.int32)
        - 1
    )
    kv_out[...] = jnp.where(kept, order + (start & (TILE - 1)), -1)
    place = start + order
    first = lax.div(start, TOK_DEV)
    device = first + jnp.zeros_like(place)
    for step in range(1, reach + 1):
        device = device + (place >= (first + step) * TOK_DEV).astype(jnp.int32)
    within = place - device * TOK_DEV
    cls = jnp.zeros_like(place)
    for step in range(1, groups):
        cls = cls + (within >= step * block).astype(jnp.int32)
    low = first * block + jnp.clip(start - first * TOK_DEV - cls * block, 0, block)
    slot = cls * cap + device * block + within - cls * block - low + (low & (TILE - 1))
    q_out[...] = jnp.where(kept, slot, -1)


def find_slots(me, counts, ranks, reach, groups, block, cap):
    shape = jax.ShapeDtypeStruct(ranks.shape, jnp.int32)
    return pl.pallas_call(
        functools.partial(slots_kernel, reach, groups, block, cap),
        in_specs=[whole_smem(), whole_smem(), whole_vmem()],
        out_specs=[whole_vmem()] * 2,
        out_shape=[shape, shape],
        compiler_params=params(),
        cost_estimate=small_cost(),
    )(me, counts, ranks)


def pack_kernel(turned, classes, cap, width, slot_ref, cos_ref, sin_ref, row_ref, *rest):
    out_refs, hot_ref = rest[:-1], rest[-1]

    @pl.when(pl.program_id(0) == 0)
    def _():
        ids = lax.broadcasted_iota(jnp.int32, hot_ref.shape, 0)
        hot_ref[...] = (ids == slot_ref[...]).astype(jnp.float32).astype(jnp.bfloat16)

    if turned:
        rows = jnp.concatenate(
            [
                turn(row_ref[:, h * HD : (h + 1) * HD], cos_ref[...], sin_ref[...])
                for h in range(width)
            ],
            axis=1,
        )
    else:
        rows = row_ref[...]
    for j, out_ref in enumerate(out_refs):
        for r in range(classes):
            first = (j * classes + r) * cap
            moved = jnp.dot(
                hot_ref[first : first + cap, :], rows, preferred_element_type=jnp.float32
            ).astype(jnp.bfloat16)
            for h in range(width):
                out_ref[h, r] = moved[:, h * HD : (h + 1) * HD]


def pack(slots, cosine, sine, rows, turned, chunks, classes, cap):
    count = rows.shape[0]
    heads = rows.shape[1] // HD
    width = min(2, heads)
    fixed = lambda i: (0, 0)
    total = chunks * classes * cap
    return pl.pallas_call(
        functools.partial(pack_kernel, turned, classes, cap, width),
        grid=(heads // width,),
        in_specs=[
            pl.BlockSpec((1, count), fixed),
            pl.BlockSpec((count, HD), fixed),
            pl.BlockSpec((count, HD), fixed),
            pl.BlockSpec((count, width * HD), lambda i: (0, i)),
        ],
        out_specs=[pl.BlockSpec((width, classes, cap, HD), lambda i: (i, 0, 0, 0))] * chunks,
        out_shape=[jax.ShapeDtypeStruct((heads, classes, cap, HD), jnp.bfloat16)] * chunks,
        scratch_shapes=[pltpu.VMEM((total, count), jnp.bfloat16)],
        compiler_params=params(),
        cost_estimate=small_cost(),
    )(slots, cosine, sine, rows)


def piece_rows(cap):
    return max(rows for rows in range(TILE, PAD + 1, TILE) if cap % rows == 0)


def merge_pieces(low, high, piece, source, add):
    shift = low & (TILE - 1)
    pieces = jnp.where(high > low, lax.div(high - low + shift + piece - 1, piece), 0)
    first = low - shift

    def one(i, carry):
        at = pl.multiple_of(first + i * piece, TILE)
        add(at, source(pl.multiple_of(i * piece, TILE)))
        return carry

    lax.fori_loop(0, pieces, one, 0)


def compact_kernel(offsets, per, total, as_keys, member_ref, count_ref, *rest):
    parts, out, all_rows, starts = rest[:-3], rest[-3], rest[-2], rest[-1]
    members = len(parts)
    piece = piece_rows(parts[0].shape[1])
    all_rows[...] = jnp.zeros_like(all_rows)
    start = jnp.int32(0)
    for s in range(count_ref.shape[0]):
        starts[s] = start
        start = start + count_ref[s]

    def add(at, rows):
        all_rows[pl.ds(at, piece), :] += rows

    for part, offset in zip(parts, offsets):
        for z in range(per):
            source = z * members + (member_ref[0] ^ offset)
            low = starts[source]
            merge_pieces(
                low,
                low + count_ref[source],
                piece,
                lambda at: part[z, pl.ds(at, piece), :],
                add,
            )
    if as_keys:
        for first in range(0, total, 2 * TOK_DEV):
            out[:, first : first + 2 * TOK_DEV] = jnp.transpose(
                all_rows[first : first + 2 * TOK_DEV, :]
            )
    else:
        out[:, :HD] = all_rows[:total, :]
        out[:, HD:] = jnp.ones((total, HD), jnp.bfloat16)


def compact(member, counts, parts, offsets, total, as_keys):
    per = parts[0].shape[0]
    return pl.pallas_call(
        functools.partial(compact_kernel, offsets, per, total, as_keys),
        in_specs=[whole_smem(), whole_smem()] + [whole_vmem()] * len(parts),
        out_specs=whole_vmem(),
        out_shape=jax.ShapeDtypeStruct(
            (HD, total) if as_keys else (total, 2 * HD), jnp.bfloat16
        ),
        scratch_shapes=[
            pltpu.VMEM((total + PAD, HD), jnp.bfloat16),
            pltpu.SMEM(counts.shape, jnp.int32),
        ],
        compiler_params=params(),
        cost_estimate=small_cost(),
    )(member, counts, *parts)


def attend_kernel(ctx_size, block, cls_ref, count_ref, got_ref, key_ref, value_ref, out_ref,
                  query_all, scores_a, scores_b, top_a, top_b, run_max, run_acc):
    span = 2 * TOK_DEV
    pair = 4 * block
    supers = ctx_size // 4
    steps = supers * (supers + 1)
    cls = cls_ref[0]
    piece = piece_rows(got_ref.shape[1])
    query_all[...] = jnp.zeros_like(query_all)

    def add(at, rows):
        query_all[pl.ds(at, piece), :] += rows

    start = jnp.int32(0)
    for s in range(ctx_size):
        end = start + count_ref[s]
        merge_pieces(
            rows_below(start, cls, block),
            rows_below(end, cls, block),
            piece,
            lambda at: got_ref[s, pl.ds(at, piece), :],
            add,
        )
        start = end

    def row_top(found):
        return jnp.broadcast_to(jnp.max(found, axis=1, keepdims=True), (pair, HD))

    def score(scores, top, i, k):
        rows = query_all[pl.ds(pl.multiple_of(jnp.minimum(i, supers - 1) * pair, TILE), pair), :]
        keys = key_ref[:, pl.ds(pl.multiple_of(k * span, HD), span)]
        found = jnp.dot(rows, keys, preferred_element_type=jnp.float32)
        scores[...] = found
        top[...] = row_top(found)

    def mask(scores, top, first):
        row_ids = lax.broadcasted_iota(jnp.int32, (pair, HD), 0)
        row = row_ids + cls * block - first
        for n in range(1, 4):
            row = row + jnp.where(row_ids >= n * block, TOK_DEV - block, 0)
        col = lax.broadcasted_iota(jnp.int32, (pair, span), 1)
        found = jnp.where(
            col <= jnp.concatenate([row] * (span // HD), axis=1), scores[...], masked_score
        )
        scores[...] = found
        top[...] = row_top(found)

    def absorb(scores, top, k):
        before = run_max[...]
        after = jnp.maximum(before, top[...])
        rescale = jnp.exp2((before - after) * exp2_scale)
        run_max[...] = after
        weights = jnp.exp2(
            (scores[...] - jnp.concatenate([after] * (span // HD), axis=1)) * exp2_scale
        )
        values = value_ref[pl.ds(pl.multiple_of(k * span, TILE), span), :]
        run_acc[...] = run_acc[...] * jnp.concatenate([rescale, rescale], axis=1) + jnp.dot(
            weights.astype(jnp.bfloat16), values, preferred_element_type=jnp.float32
        )

    def clear():
        run_max[...] = jnp.full_like(run_max, masked_score)
        run_acc[...] = jnp.zeros_like(run_acc)

    def one_step(now, later, i, k):
        last = k == 2 * i + 1
        next_i = jnp.where(last, i + 1, i)
        next_k = jnp.where(last, 0, k + 1)
        score(*later, next_i, next_k)
        absorb(*now, k)

        @pl.when(last)
        def _():
            result = (run_acc[:, :HD] / run_acc[:, HD:]).astype(jnp.bfloat16)
            for n in range(4):
                out_ref[4 * i + n] = result[n * block : (n + 1) * block]
            clear()

        @pl.when(next_k >= 2 * next_i)
        def _():
            mask(*later, (next_k - 2 * next_i) * span)

        return next_i, next_k

    buffers_a, buffers_b = (scores_a, top_a), (scores_b, top_b)
    clear()
    score(*buffers_a, 0, 0)
    mask(*buffers_a, 0)

    def two_steps(t, at):
        at = one_step(buffers_a, buffers_b, *at)
        return one_step(buffers_b, buffers_a, *at)

    lax.fori_loop(0, steps // 2, two_steps, (jnp.int32(0), jnp.int32(0)))


def attend(cls, counts, got, keys, values, block):
    ctx_size = got.shape[0]
    total = values.shape[0]
    pairs = total * ctx_size * block // 2
    return pl.pallas_call(
        functools.partial(attend_kernel, ctx_size, block),
        in_specs=[whole_smem()] * 2 + [whole_vmem()] * 3,
        out_specs=whole_vmem(),
        out_shape=jax.ShapeDtypeStruct((ctx_size, block, HD), jnp.bfloat16),
        scratch_shapes=[
            pltpu.VMEM((ctx_size * block + PAD, HD), jnp.bfloat16),
            pltpu.VMEM((4 * block, 2 * TOK_DEV), jnp.float32),
            pltpu.VMEM((4 * block, 2 * TOK_DEV), jnp.float32),
            pltpu.VMEM((4 * block, HD), jnp.float32),
            pltpu.VMEM((4 * block, HD), jnp.float32),
            pltpu.VMEM((4 * block, HD), jnp.float32),
            pltpu.VMEM((4 * block, 2 * HD), jnp.float32),
        ],
        compiler_params=params(),
        cost_estimate=pl.CostEstimate(
            flops=pairs * 16 * HD, bytes_accessed=total * HD * 8, transcendentals=pairs
        ),
    )(cls, counts, got, keys, values)


def project_kernel(classes, chunks, column_ref, *rest):
    got_refs, (weight_ref, out_ref, rows_ref) = rest[:chunks], rest[chunks:]
    block = got_refs[0].shape[1]

    @pl.when(pl.program_id(0) == 0)
    def _():
        for j, got_ref in enumerate(got_refs):
            for d in range(got_ref.shape[0]):
                h, r = d // classes, d % classes
                first = (j * classes + r) * block
                rows_ref[first : first + block, h * HD : (h + 1) * HD] = got_ref[d]

    out_ref[...] = jnp.dot(
        rows_ref[...], weight_ref[...], preferred_element_type=jnp.float32
    ).astype(jnp.bfloat16)


def project(first_column, got, weight, columns, classes):
    ctx_size, block, _ = got[0].shape
    rows, depth = len(got) * classes * block, weight.shape[0]
    step = min(512, columns)
    return pl.pallas_call(
        functools.partial(project_kernel, classes, len(got)),
        grid_spec=pltpu.PrefetchScalarGridSpec(
            num_scalar_prefetch=1,
            grid=(columns // step,),
            in_specs=[pl.BlockSpec((ctx_size, block, HD), lambda i, first: (0, 0, 0))] * len(got)
            + [pl.BlockSpec((depth, step), lambda i, first: (0, first[0] + i))],
            out_specs=pl.BlockSpec((rows, step), lambda i, first: (0, i)),
            scratch_shapes=[pltpu.VMEM((rows, depth), jnp.bfloat16)],
        ),
        out_shape=jax.ShapeDtypeStruct((rows, columns), jnp.bfloat16),
        compiler_params=params(),
        cost_estimate=small_cost(),
    )((first_column // step).astype(jnp.int32).reshape(1), *got, weight)


def join_kernel(chunks, parts, head_ref, *rest):
    got_refs, weight_refs = rest[:chunks], rest[chunks : chunks + parts]
    own_ref, out_ref, rows_ref = rest[chunks + parts :]
    block = got_refs[0].shape[1]
    firsts = [sum(ref.shape[0] for ref in weight_refs[:p]) for p in range(parts)]

    @pl.when(pl.program_id(0) == 0)
    def _():
        for j, got_ref in enumerate(got_refs):
            for p in range(parts):
                for n in range(weight_refs[p].shape[0] // HD):
                    at = firsts[p] + n * HD
                    rows_ref[j * block : (j + 1) * block, at : at + HD] = got_ref[head_ref[p] + n]

    total = jnp.zeros(out_ref.shape, jnp.float32)
    for first, weight_ref in zip(firsts, weight_refs):
        total = total + jnp.dot(
            rows_ref[:, first : first + weight_ref.shape[0]],
            weight_ref[...],
            preferred_element_type=jnp.float32,
        )
    theirs = total.astype(jnp.bfloat16).astype(jnp.float32)
    out_ref[...] = (own_ref[...].astype(jnp.float32) + theirs).astype(jnp.bfloat16)


def join(first_heads, got, weights, own):
    ctx_size, block, _ = got[0].shape
    rows, columns = own.shape
    depth = sum(weight.shape[0] for weight in weights)
    step = min(512, columns)
    tile = pl.BlockSpec((rows, step), lambda i, first: (0, i))
    return pl.pallas_call(
        functools.partial(join_kernel, len(got), len(weights)),
        grid_spec=pltpu.PrefetchScalarGridSpec(
            num_scalar_prefetch=1,
            grid=(columns // step,),
            in_specs=[pl.BlockSpec((ctx_size, block, HD), lambda i, first: (0, 0, 0))] * len(got)
            + [pl.BlockSpec((weight.shape[0], step), lambda i, first: (0, i)) for weight in weights]
            + [tile],
            out_specs=tile,
            scratch_shapes=[pltpu.VMEM((rows, depth), jnp.bfloat16)],
        ),
        out_shape=jax.ShapeDtypeStruct((rows, columns), jnp.bfloat16),
        compiler_params=params(),
        cost_estimate=small_cost(),
    )(first_heads, *got, *weights, own)


def tables(query_rows):
    half_dim = HD // 2
    positions = lax.axis_index("ctx") * query_rows + jnp.arange(query_rows, dtype=jnp.int32)
    lane = jnp.arange(HD, dtype=jnp.int32)
    pair_id = jnp.where(lane < half_dim, lane, lane - half_dim)
    inv_freq = rope_base ** (-(pair_id.astype(jnp.float32) * 2.0 / HD))
    angles = positions.astype(jnp.float32)[:, None] * inv_freq[None, :]
    sine = jnp.sin(angles)
    return jnp.cos(angles), jnp.where(lane[None, :] < half_dim, -sine, sine)


def local(query, key, value, keep_rank, kept_count, out_weight):
    ctx_size = lax.axis_size("ctx")
    tp_size = lax.axis_size("tp")
    me = lax.axis_index("ctx")
    tp_me = lax.axis_index("tp")
    orig_rows = query.shape[0]
    heads = query.shape[1] // HD
    kv_heads = key.shape[1] // HD
    members = ctx_size // kv_heads
    classes = ctx_size // heads
    chunks = CHUNKS if classes == 1 else 1
    block = TOK_DEV // (chunks * classes)
    total = ctx_size * TOK_DEV
    reach = orig_rows // TOK_DEV
    cap = reach * block + TILE
    cap_kv = orig_rows + TILE
    columns = out_weight.shape[1] // tp_size

    kv_slots, q_slots = find_slots(
        me.reshape(1), kept_count, keep_rank, reach, chunks * classes, block, cap
    )
    cosine, sine = tables(orig_rows)

    across = [[z * members + m for z in range(kv_heads)] for m in range(members)]

    member = (me & (members - 1)).reshape(1)

    def pack_shared(rows, turned):
        (packed,) = pack(kv_slots, cosine, sine, rows, turned, 1, 1, cap_kv)
        return packed.reshape(kv_heads, cap_kv, HD)

    def send_across(packed):
        if kv_heads == 1:
            return packed
        return lax.all_to_all(
            packed, "ctx", split_axis=0, concat_axis=0, tiled=True, axis_index_groups=across
        )

    def swap(parts, bit):
        pairs = [(d, d ^ bit) for d in range(ctx_size)]
        return parts + [lax.ppermute(part, "ctx", pairs) for part in parts]

    bits = [members >> n for n in range(1, members.bit_length())]
    offsets = [0]
    for bit in bits:
        offsets = offsets + [offset ^ bit for offset in offsets]

    def send_query(packed):
        return lax.all_to_all(
            packed.reshape(ctx_size, cap, HD), "ctx", split_axis=0, concat_axis=0, tiled=True
        )

    traded = tp_size == 2 and classes == 1 and heads == 16 and chunks == 2
    both = [(0, 1), (1, 0)]

    def chip_swap(part, bit):
        return lax.ppermute(part, "ctx", [(d, d ^ bit) for d in range(ctx_size)])

    core, side = me & 1, (me >> 1) & 1
    sizes = [2, 4]

    def weight_rows(p):
        first = core * 8 + (jnp.where(side == 0, 0, 6) if p == 0 else 2)
        return lax.dynamic_slice(
            out_weight, (first * HD, (1 - tp_me) * columns), (sizes[p] * HD, columns)
        )

    def gather_weight(part):
        return lax.all_gather(part, "tp", axis=0)

    def trade(part):
        return lax.ppermute(part, "tp", both)

    key_packed = pack_shared(key, True)
    slices = []
    if traded:
        key_packed, out_weight = lax.optimization_barrier((key_packed, out_weight))
        first_slice, value = lax.optimization_barrier((weight_rows(0), value))
        slices = [first_slice, weight_rows(1)]
    key_parts = [send_across(key_packed)]
    value_packed, key_parts, slices = lax.optimization_barrier(
        (pack_shared(value, False), key_parts, slices)
    )
    key_parts = swap(key_parts, bits[0])
    value_parts = [send_across(value_packed)]
    packed_q = list(pack(q_slots, cosine, sine, query, True, chunks, classes, cap))
    gathered = [gather_weight(one) for one in slices]
    packed_q[0], key_parts, value_parts = lax.optimization_barrier(
        (packed_q[0], key_parts, value_parts)
    )
    got_q = [send_query(packed_q[0])]
    value_parts = swap(value_parts, bits[0])
    for bit in bits[1:]:
        key_parts = swap(key_parts, bit)
    keys = compact(member, kept_count, key_parts, offsets, total, True)
    if chunks > 1:
        packed_q[1], value_parts, keys = lax.optimization_barrier(
            (packed_q[1], value_parts, keys)
        )
    for bit in bits[1:]:
        value_parts = swap(value_parts, bit)
    got_q = got_q + [send_query(packed) for packed in packed_q[1:]]
    values = compact(member, kept_count, value_parts, offsets, total, False)
    if traded:
        got_q[0], gathered[0] = lax.optimization_barrier((got_q[0], gathered[0]))
        first_part = lax.dynamic_index_in_dim(gathered[0], 1 - tp_me, 0, keepdims=False)
        came = [first_part, chip_swap(first_part, 2)]

    got, done = [], None
    for j in range(chunks):
        cls_j = j * classes + (me & (classes - 1))
        if j > 0:
            got_q[j], done = lax.optimization_barrier((got_q[j], done))
            got.append(lax.all_to_all(done, "ctx", split_axis=0, concat_axis=0, tiled=True))
        done = attend(cls_j.reshape(1), kept_count, got_q[j], keys, values, block)
    if chunks > 1:
        done, got[0] = lax.optimization_barrier((done, got[0]))
    if traded:
        _, came, second = lax.optimization_barrier((done, came, gathered[1]))
        came = came + [lax.dynamic_index_in_dim(second, 1 - tp_me, 0, keepdims=False)]
    got.append(lax.all_to_all(done, "ctx", split_axis=0, concat_axis=0, tiled=True))
    if traded:
        theirs = [trade(one) for one in got]
        came = came + [chip_swap(part, 1) for part in came]
        own = project(tp_me * columns, got, out_weight, columns, classes)
        order = [jnp.where(side == 0, 0, 6), jnp.where(side == 0, 6, 0), jnp.int32(2)]
        first_heads = jnp.stack([c * 8 + at for c in (core, 1 - core) for at in order])
        return join(first_heads.astype(jnp.int32), theirs, came, own)
    full = project(jnp.int32(0) * tp_me, got, out_weight, columns * tp_size, classes)
    split = jnp.transpose(full.reshape(full.shape[0], tp_size, columns), (1, 0, 2))
    swapped = lax.all_to_all(split, "tp", split_axis=0, concat_axis=0, tiled=True)
    return jnp.sum(swapped.astype(jnp.float32), axis=0).astype(jnp.bfloat16)


def solution(mesh):
    placed = (P("ctx", "tp"), P("ctx", "tp"), P("ctx", "tp"), P("ctx", None), P(), P("tp", None))
    return jax.shard_map(
        local, mesh=mesh, in_specs=placed, out_specs=P("ctx", "tp"), check_vma=False
    )
```

```python
import functools
import math

import jax
import jax.numpy as jnp
from jax import lax
from jax.experimental import pallas as pl
from jax.experimental.pallas import tpu as pltpu
from jax.sharding import PartitionSpec as P

HD = 128
TOK_DEV = 384
TILE = 16
PAD = 128
CHUNKS = 2

rope_base = 1000000.0
masked_score = -1e30
exp2_scale = math.log2(math.e) / math.sqrt(HD)
VMEM_BYTES = 58 * 1024 * 1024


def whole_vmem():
    return pl.BlockSpec(memory_space=pltpu.VMEM)


def whole_smem():
    return pl.BlockSpec(memory_space=pltpu.SMEM)


def params():
    return pltpu.CompilerParams(vmem_limit_bytes=VMEM_BYTES)


def turn(rows, cosine, sine):
    as_float = rows.astype(jnp.float32)
    swapped = pltpu.roll(as_float, HD // 2, 1)
    return (as_float * cosine + swapped * sine).astype(jnp.bfloat16)


def rows_below(start, cls, block):
    whole = lax.div(start, TOK_DEV)
    return whole * block + jnp.clip(start - whole * TOK_DEV - cls * block, 0, block)


def slots_kernel(reach, groups, block, cap, me_ref, count_ref, rank_ref, kv_out, q_out):
    me = me_ref[0]
    rows = rank_ref.shape[1]
    start = jnp.int32(0)
    for s in range(count_ref.shape[0]):
        start = start + jnp.where(s < me, count_ref[s], 0)
    kept = rank_ref[...] < count_ref[me]
    upper = lax.broadcasted_iota(jnp.int32, (rows, rows), 0) <= lax.broadcasted_iota(
        jnp.int32, (rows, rows), 1
    )
    flags = jnp.broadcast_to(kept.astype(jnp.float32), (8, rows)).astype(jnp.bfloat16)
    order = (
        jnp.dot(
            flags, upper.astype(jnp.float32).astype(jnp.bfloat16), preferred_element_type=jnp.float32
        )[:1].astype(jnp.int32)
        - 1
    )
    kv_out[...] = jnp.where(kept, order + (start & (TILE - 1)), -1)
    place = start + order
    first = lax.div(start, TOK_DEV)
    device = first + jnp.zeros_like(place)
    for step in range(1, reach + 1):
        device = device + (place >= (first + step) * TOK_DEV).astype(jnp.int32)
    within = place - device * TOK_DEV
    cls = jnp.zeros_like(place)
    for step in range(1, groups):
        cls = cls + (within >= step * block).astype(jnp.int32)
    low = first * block + jnp.clip(start - first * TOK_DEV - cls * block, 0, block)
    slot = cls * cap + device * block + within - cls * block - low + (low & (TILE - 1))
    q_out[...] = jnp.where(kept, slot, -1)


def find_slots(me, counts, ranks, reach, groups, block, cap):
    shape = jax.ShapeDtypeStruct(ranks.shape, jnp.int32)
    return pl.pallas_call(
        functools.partial(slots_kernel, reach, groups, block, cap),
        in_specs=[whole_smem(), whole_smem(), whole_vmem()],
        out_specs=[whole_vmem()] * 2,
        out_shape=[shape, shape],
        compiler_params=params(),
        cost_estimate=pl.CostEstimate(flops=2**20, bytes_accessed=2**14, transcendentals=0),
    )(me, counts, ranks)


def pack_kernel(turned, classes, cap, width, slot_ref, cos_ref, sin_ref, row_ref, *rest):
    out_refs, hot_ref = rest[:-1], rest[-1]

    @pl.when(pl.program_id(0) == 0)
    def _():
        ids = lax.broadcasted_iota(jnp.int32, hot_ref.shape, 0)
        hot_ref[...] = (ids == slot_ref[...]).astype(jnp.float32).astype(jnp.bfloat16)

    if turned:
        rows = jnp.concatenate(
            [
                turn(row_ref[:, h * HD : (h + 1) * HD], cos_ref[...], sin_ref[...])
                for h in range(width)
            ],
            axis=1,
        )
    else:
        rows = row_ref[...]
    for j, out_ref in enumerate(out_refs):
        for r in range(classes):
            first = (j * classes + r) * cap
            moved = jnp.dot(
                hot_ref[first : first + cap, :], rows, preferred_element_type=jnp.float32
            ).astype(jnp.bfloat16)
            for h in range(width):
                out_ref[h, r] = moved[:, h * HD : (h + 1) * HD]


def pack(slots, cosine, sine, rows, turned, chunks, classes, cap):
    count = rows.shape[0]
    heads = rows.shape[1] // HD
    width = min(2, heads)
    fixed = lambda i: (0, 0)
    total = chunks * classes * cap
    return pl.pallas_call(
        functools.partial(pack_kernel, turned, classes, cap, width),
        grid=(heads // width,),
        in_specs=[
            pl.BlockSpec((1, count), fixed),
            pl.BlockSpec((count, HD), fixed),
            pl.BlockSpec((count, HD), fixed),
            pl.BlockSpec((count, width * HD), lambda i: (0, i)),
        ],
        out_specs=[pl.BlockSpec((width, classes, cap, HD), lambda i: (i, 0, 0, 0))] * chunks,
        out_shape=[jax.ShapeDtypeStruct((heads, classes, cap, HD), jnp.bfloat16)] * chunks,
        scratch_shapes=[pltpu.VMEM((total, count), jnp.bfloat16)],
        compiler_params=params(),
        cost_estimate=pl.CostEstimate(
            flops=2 * heads * total * count * HD, bytes_accessed=count * heads * HD * 4, transcendentals=0
        ),
    )(slots, cosine, sine, rows)


def piece_rows(cap):
    return max(rows for rows in range(TILE, PAD + 1, TILE) if cap % rows == 0)


def merge_pieces(low, high, piece, source, add):
    shift = low & (TILE - 1)
    pieces = jnp.where(high > low, lax.div(high - low + shift + piece - 1, piece), 0)
    first = low - shift

    def one(i, carry):
        at = pl.multiple_of(first + i * piece, TILE)
        add(at, source(pl.multiple_of(i * piece, TILE)))
        return carry

    lax.fori_loop(0, pieces, one, 0)


def compact_kernel(offsets, per, total, as_keys, member_ref, count_ref, *rest):
    parts, out, all_rows, starts = rest[:-3], rest[-3], rest[-2], rest[-1]
    members = len(parts)
    piece = piece_rows(parts[0].shape[1])
    all_rows[...] = jnp.zeros_like(all_rows)
    start = jnp.int32(0)
    for s in range(count_ref.shape[0]):
        starts[s] = start
        start = start + count_ref[s]

    def add(at, rows):
        all_rows[pl.ds(at, piece), :] += rows

    for part, offset in zip(parts, offsets):
        for z in range(per):
            source = z * members + (member_ref[0] ^ offset)
            low = starts[source]
            merge_pieces(
                low,
                low + count_ref[source],
                piece,
                lambda at: part[z, pl.ds(at, piece), :],
                add,
            )
    if as_keys:
        for first in range(0, total, 2 * TOK_DEV):
            out[:, first : first + 2 * TOK_DEV] = jnp.transpose(
                all_rows[first : first + 2 * TOK_DEV, :]
            )
    else:
        out[:, :HD] = all_rows[:total, :]
        out[:, HD:] = jnp.ones((total, HD), jnp.bfloat16)


def compact(member, counts, parts, offsets, total, as_keys):
    per = parts[0].shape[0]
    return pl.pallas_call(
        functools.partial(compact_kernel, offsets, per, total, as_keys),
        in_specs=[whole_smem(), whole_smem()] + [whole_vmem()] * len(parts),
        out_specs=whole_vmem(),
        out_shape=jax.ShapeDtypeStruct(
            (HD, total) if as_keys else (total, 2 * HD), jnp.bfloat16
        ),
        scratch_shapes=[
            pltpu.VMEM((total + PAD, HD), jnp.bfloat16),
            pltpu.SMEM(counts.shape, jnp.int32),
        ],
        compiler_params=params(),
        cost_estimate=pl.CostEstimate(flops=total * HD * 8, bytes_accessed=total * HD * 8, transcendentals=0),
    )(member, counts, *parts)


def attend_kernel(ctx_size, block, cls_ref, count_ref, got_ref, key_ref, value_ref, out_ref,
                  query_all, scores_a, scores_b, top_a, top_b, run_max, run_acc):
    span = 2 * TOK_DEV
    pair = 4 * block
    supers = ctx_size // 4
    steps = supers * (supers + 1)
    cls = cls_ref[0]
    piece = piece_rows(got_ref.shape[1])
    query_all[...] = jnp.zeros_like(query_all)

    def add(at, rows):
        query_all[pl.ds(at, piece), :] += rows

    start = jnp.int32(0)
    for s in range(ctx_size):
        end = start + count_ref[s]
        merge_pieces(
            rows_below(start, cls, block),
            rows_below(end, cls, block),
            piece,
            lambda at: got_ref[s, pl.ds(at, piece), :],
            add,
        )
        start = end

    def row_top(found):
        return jnp.broadcast_to(jnp.max(found, axis=1, keepdims=True), (pair, HD))

    def score(scores, top, i, k):
        rows = query_all[pl.ds(pl.multiple_of(jnp.minimum(i, supers - 1) * pair, TILE), pair), :]
        keys = key_ref[:, pl.ds(pl.multiple_of(k * span, HD), span)]
        found = jnp.dot(rows, keys, preferred_element_type=jnp.float32)
        scores[...] = found
        top[...] = row_top(found)

    def mask(scores, top, first):
        row_ids = lax.broadcasted_iota(jnp.int32, (pair, HD), 0)
        row = row_ids + cls * block - first
        for n in range(1, 4):
            row = row + jnp.where(row_ids >= n * block, TOK_DEV - block, 0)
        col = lax.broadcasted_iota(jnp.int32, (pair, span), 1)
        found = jnp.where(
            col <= jnp.concatenate([row] * (span // HD), axis=1), scores[...], masked_score
        )
        scores[...] = found
        top[...] = row_top(found)

    def absorb(scores, top, k):
        before = run_max[...]
        after = jnp.maximum(before, top[...])
        rescale = jnp.exp2((before - after) * exp2_scale)
        run_max[...] = after
        weights = jnp.exp2(
            (scores[...] - jnp.concatenate([after] * (span // HD), axis=1)) * exp2_scale
        )
        values = value_ref[pl.ds(pl.multiple_of(k * span, TILE), span), :]
        run_acc[...] = run_acc[...] * jnp.concatenate([rescale, rescale], axis=1) + jnp.dot(
            weights.astype(jnp.bfloat16), values, preferred_element_type=jnp.float32
        )

    def clear():
        run_max[...] = jnp.full_like(run_max, masked_score)
        run_acc[...] = jnp.zeros_like(run_acc)

    def one_step(now, later, i, k):
        last = k == 2 * i + 1
        next_i = jnp.where(last, i + 1, i)
        next_k = jnp.where(last, 0, k + 1)
        score(*later, next_i, next_k)
        absorb(*now, k)

        @pl.when(last)
        def _():
            result = (run_acc[:, :HD] / run_acc[:, HD:]).astype(jnp.bfloat16)
            for n in range(4):
                out_ref[4 * i + n] = result[n * block : (n + 1) * block]
            clear()

        @pl.when(next_k >= 2 * next_i)
        def _():
            mask(*later, (next_k - 2 * next_i) * span)

        return next_i, next_k

    buffers_a, buffers_b = (scores_a, top_a), (scores_b, top_b)
    clear()
    score(*buffers_a, 0, 0)
    mask(*buffers_a, 0)

    def two_steps(t, at):
        at = one_step(buffers_a, buffers_b, *at)
        return one_step(buffers_b, buffers_a, *at)

    lax.fori_loop(0, steps // 2, two_steps, (jnp.int32(0), jnp.int32(0)))


def attend(cls, counts, got, keys, values, block):
    ctx_size = got.shape[0]
    total = values.shape[0]
    pairs = total * ctx_size * block // 2
    return pl.pallas_call(
        functools.partial(attend_kernel, ctx_size, block),
        in_specs=[whole_smem()] * 2 + [whole_vmem()] * 3,
        out_specs=whole_vmem(),
        out_shape=jax.ShapeDtypeStruct((ctx_size, block, HD), jnp.bfloat16),
        scratch_shapes=[
            pltpu.VMEM((ctx_size * block + PAD, HD), jnp.bfloat16),
            pltpu.VMEM((4 * block, 2 * TOK_DEV), jnp.float32),
            pltpu.VMEM((4 * block, 2 * TOK_DEV), jnp.float32),
            pltpu.VMEM((4 * block, HD), jnp.float32),
            pltpu.VMEM((4 * block, HD), jnp.float32),
            pltpu.VMEM((4 * block, HD), jnp.float32),
            pltpu.VMEM((4 * block, 2 * HD), jnp.float32),
        ],
        compiler_params=params(),
        cost_estimate=pl.CostEstimate(
            flops=pairs * 2 * HD, bytes_accessed=total * HD * 8, transcendentals=pairs
        ),
    )(cls, counts, got, keys, values)


def project_kernel(classes, chunks, column_ref, *rest):
    got_refs, (weight_ref, out_ref, rows_ref) = rest[:chunks], rest[chunks:]
    block = got_refs[0].shape[1]

    @pl.when(pl.program_id(0) == 0)
    def _():
        for j, got_ref in enumerate(got_refs):
            for d in range(got_ref.shape[0]):
                h, r = d // classes, d % classes
                first = (j * classes + r) * block
                rows_ref[first : first + block, h * HD : (h + 1) * HD] = got_ref[d]

    out_ref[...] = jnp.dot(
        rows_ref[...], weight_ref[...], preferred_element_type=jnp.float32
    ).astype(jnp.bfloat16)


def project(first_column, got, weight, columns, classes):
    ctx_size, block, _ = got[0].shape
    rows, depth = len(got) * classes * block, weight.shape[0]
    step = min(512, columns)
    return pl.pallas_call(
        functools.partial(project_kernel, classes, len(got)),
        grid_spec=pltpu.PrefetchScalarGridSpec(
            num_scalar_prefetch=1,
            grid=(columns // step,),
            in_specs=[pl.BlockSpec((ctx_size, block, HD), lambda i, first: (0, 0, 0))] * len(got)
            + [pl.BlockSpec((depth, step), lambda i, first: (0, first[0] + i))],
            out_specs=pl.BlockSpec((rows, step), lambda i, first: (0, i)),
            scratch_shapes=[pltpu.VMEM((rows, depth), jnp.bfloat16)],
        ),
        out_shape=jax.ShapeDtypeStruct((rows, columns), jnp.bfloat16),
        compiler_params=params(),
        cost_estimate=pl.CostEstimate(
            flops=2 * rows * depth * columns, bytes_accessed=2 * depth * columns, transcendentals=0
        ),
    )((first_column // step).astype(jnp.int32).reshape(1), *got, weight)


def join_kernel(chunks, parts, head_ref, *rest):
    got_refs, weight_refs = rest[:chunks], rest[chunks : chunks + parts]
    own_ref, out_ref, rows_ref = rest[chunks + parts :]
    block = got_refs[0].shape[1]
    firsts = [sum(ref.shape[0] for ref in weight_refs[:p]) for p in range(parts)]

    @pl.when(pl.program_id(0) == 0)
    def _():
        for j, got_ref in enumerate(got_refs):
            for p in range(parts):
                for n in range(weight_refs[p].shape[0] // HD):
                    at = firsts[p] + n * HD
                    rows_ref[j * block : (j + 1) * block, at : at + HD] = got_ref[head_ref[p] + n]

    total = jnp.zeros(out_ref.shape, jnp.float32)
    for first, weight_ref in zip(firsts, weight_refs):
        total = total + jnp.dot(
            rows_ref[:, first : first + weight_ref.shape[0]],
            weight_ref[...],
            preferred_element_type=jnp.float32,
        )
    theirs = total.astype(jnp.bfloat16).astype(jnp.float32)
    out_ref[...] = (own_ref[...].astype(jnp.float32) + theirs).astype(jnp.bfloat16)


def join(first_heads, got, weights, own):
    ctx_size, block, _ = got[0].shape
    rows, columns = own.shape
    depth = sum(weight.shape[0] for weight in weights)
    step = min(512, columns)
    tile = pl.BlockSpec((rows, step), lambda i, first: (0, i))
    return pl.pallas_call(
        functools.partial(join_kernel, len(got), len(weights)),
        grid_spec=pltpu.PrefetchScalarGridSpec(
            num_scalar_prefetch=1,
            grid=(columns // step,),
            in_specs=[pl.BlockSpec((ctx_size, block, HD), lambda i, first: (0, 0, 0))] * len(got)
            + [pl.BlockSpec((weight.shape[0], step), lambda i, first: (0, i)) for weight in weights]
            + [tile],
            out_specs=tile,
            scratch_shapes=[pltpu.VMEM((rows, depth), jnp.bfloat16)],
        ),
        out_shape=jax.ShapeDtypeStruct((rows, columns), jnp.bfloat16),
        compiler_params=params(),
        cost_estimate=pl.CostEstimate(
            flops=2 * rows * depth * columns,
            bytes_accessed=2 * depth * columns,
            transcendentals=0,
        ),
    )(first_heads, *got, *weights, own)


def tables(query_rows):
    half_dim = HD // 2
    positions = lax.axis_index("ctx") * query_rows + jnp.arange(query_rows, dtype=jnp.int32)
    lane = jnp.arange(HD, dtype=jnp.int32)
    pair_id = jnp.where(lane < half_dim, lane, lane - half_dim)
    inv_freq = rope_base ** (-(pair_id.astype(jnp.float32) * 2.0 / HD))
    angles = positions.astype(jnp.float32)[:, None] * inv_freq[None, :]
    sine = jnp.sin(angles)
    return jnp.cos(angles), jnp.where(lane[None, :] < half_dim, -sine, sine)


def local(query, key, value, keep_rank, kept_count, out_weight):
    ctx_size = lax.axis_size("ctx")
    tp_size = lax.axis_size("tp")
    me = lax.axis_index("ctx")
    tp_me = lax.axis_index("tp")
    orig_rows = query.shape[0]
    heads = query.shape[1] // HD
    kv_heads = key.shape[1] // HD
    members = ctx_size // kv_heads
    classes = ctx_size // heads
    chunks = CHUNKS if classes == 1 else 1
    block = TOK_DEV // (chunks * classes)
    total = ctx_size * TOK_DEV
    reach = orig_rows // TOK_DEV
    cap = reach * block + TILE
    cap_kv = orig_rows + TILE
    columns = out_weight.shape[1] // tp_size

    kv_slots, q_slots = find_slots(
        me.reshape(1), kept_count, keep_rank, reach, chunks * classes, block, cap
    )
    cosine, sine = tables(orig_rows)

    across = [[z * members + m for z in range(kv_heads)] for m in range(members)]

    member = (me & (members - 1)).reshape(1)

    def pack_shared(rows, turned):
        (packed,) = pack(kv_slots, cosine, sine, rows, turned, 1, 1, cap_kv)
        return packed.reshape(kv_heads, cap_kv, HD)

    def send_across(packed):
        if kv_heads == 1:
            return packed
        return lax.all_to_all(
            packed, "ctx", split_axis=0, concat_axis=0, tiled=True, axis_index_groups=across
        )

    def swap(parts, bit):
        pairs = [(d, d ^ bit) for d in range(ctx_size)]
        return parts + [lax.ppermute(part, "ctx", pairs) for part in parts]

    bits = [members >> n for n in range(1, members.bit_length())]
    offsets = [0]
    for bit in bits:
        offsets = offsets + [offset ^ bit for offset in offsets]

    def send_query(packed):
        return lax.all_to_all(
            packed.reshape(ctx_size, cap, HD), "ctx", split_axis=0, concat_axis=0, tiled=True
        )

    traded = tp_size == 2 and classes == 1 and heads == 16 and chunks == 2
    both = [(0, 1), (1, 0)]

    def chip_swap(part, bit):
        return lax.ppermute(part, "ctx", [(d, d ^ bit) for d in range(ctx_size)])

    core, side = me & 1, (me >> 1) & 1
    sizes = [1, 1, 1, 3]

    def at_side(left, right):
        return jnp.where(side == 0, left, right)

    lows = [at_side(0, 6), at_side(1, 7), at_side(2, 5), at_side(3, 2)]

    def weight_rows(p):
        return lax.dynamic_slice(
            out_weight,
            ((core * 8 + lows[p]) * HD, (1 - tp_me) * columns),
            (sizes[p] * HD, columns),
        )

    def trade(part):
        return lax.ppermute(part, "tp", both)

    key_packed = pack_shared(key, True)
    slices = []
    if traded:
        key_packed, out_weight = lax.optimization_barrier((key_packed, out_weight))
        first_slice, value = lax.optimization_barrier((weight_rows(0), value))
        slices = [first_slice] + [weight_rows(p) for p in range(1, 4)]
    key_parts = [send_across(key_packed)]
    value_packed, key_parts, slices = lax.optimization_barrier(
        (pack_shared(value, False), key_parts, slices)
    )
    key_parts = swap(key_parts, bits[0])
    value_parts = [send_across(value_packed)]
    came = []
    if traded:
        q_slots, came, slices = lax.optimization_barrier((q_slots, [trade(slices[0])], slices))
        came = came + [trade(slices[1])]
    packed_q = list(pack(q_slots, cosine, sine, query, True, chunks, classes, cap))
    packed_q[0], key_parts, value_parts = lax.optimization_barrier(
        (packed_q[0], key_parts, value_parts)
    )
    got_q = [send_query(packed_q[0])]
    value_parts = swap(value_parts, bits[0])
    for bit in bits[1:]:
        key_parts = swap(key_parts, bit)
    if traded:
        key_parts, came, slices = lax.optimization_barrier((key_parts, came, slices))
        came = came + [trade(slices[2])]
    keys = compact(member, kept_count, key_parts, offsets, total, True)
    if chunks > 1:
        packed_q[1], value_parts, keys = lax.optimization_barrier((packed_q[1], value_parts, keys))
    for bit in bits[1:]:
        value_parts = swap(value_parts, bit)
    got_q = got_q + [send_query(packed) for packed in packed_q[1:]]
    if traded:
        value_parts, came, slices = lax.optimization_barrier((value_parts, came, slices))
        joined = jnp.concatenate(came[:2], axis=0)
        came = [joined, came[2], trade(slices[3]), chip_swap(joined, 2)]
    values = compact(member, kept_count, value_parts, offsets, total, False)

    got, done = [], None
    for j in range(chunks):
        cls_j = j * classes + (me & (classes - 1))
        if j > 0:
            got_q[j], done = lax.optimization_barrier((got_q[j], done))
            got.append(lax.all_to_all(done, "ctx", split_axis=0, concat_axis=0, tiled=True))
        done = attend(cls_j.reshape(1), kept_count, got_q[j], keys, values, block)
    if chunks > 1:
        done, got, came = lax.optimization_barrier((done, got, came))
    got.append(lax.all_to_all(done, "ctx", split_axis=0, concat_axis=0, tiled=True))
    if traded:
        theirs = [trade(one) for one in got]
        came = came + [chip_swap(part, 1) for part in came]
        own = project(tp_me * columns, got, out_weight, columns, classes)
        order = [lows[0], lows[2], lows[3], at_side(6, 0)]
        first_heads = jnp.stack([c * 8 + at for c in (core, 1 - core) for at in order])
        return join(first_heads.astype(jnp.int32), theirs, came, own)
    full = project(jnp.int32(0) * tp_me, got, out_weight, columns * tp_size, classes)
    split = jnp.transpose(full.reshape(full.shape[0], tp_size, columns), (1, 0, 2))
    swapped = lax.all_to_all(split, "tp", split_axis=0, concat_axis=0, tiled=True)
    return jnp.sum(swapped.astype(jnp.float32), axis=0).astype(jnp.bfloat16)


def solution(mesh):
    placed = (P("ctx", "tp"), P("ctx", "tp"), P("ctx", "tp"), P("ctx", None), P(), P("tp", None))
    return jax.shard_map(
        local, mesh=mesh, in_specs=placed, out_specs=P("ctx", "tp"), check_vma=False
    )
```

```python
import functools
import math

import jax
import jax.numpy as jnp
from jax import lax
from jax.experimental import pallas as pl
from jax.experimental.pallas import tpu as pltpu
from jax.sharding import PartitionSpec as P

HD = 128
TOK_DEV = 384
TILE = 16
PAD = 128
CHUNKS = 2

rope_base = 1000000.0
masked_score = -1e30
exp2_scale = math.log2(math.e) / math.sqrt(HD)
VMEM_BYTES = 58 * 1024 * 1024


def whole_vmem():
    return pl.BlockSpec(memory_space=pltpu.VMEM)


def whole_smem():
    return pl.BlockSpec(memory_space=pltpu.SMEM)


def params():
    return pltpu.CompilerParams(vmem_limit_bytes=VMEM_BYTES)


def turn(rows, cosine, sine):
    as_float = rows.astype(jnp.float32)
    swapped = pltpu.roll(as_float, HD // 2, 1)
    return (as_float * cosine + swapped * sine).astype(jnp.bfloat16)


def rows_below(start, cls, block):
    whole = lax.div(start, TOK_DEV)
    return whole * block + jnp.clip(start - whole * TOK_DEV - cls * block, 0, block)


def slots_kernel(reach, groups, block, cap, me_ref, count_ref, rank_ref, kv_out, q_out):
    me = me_ref[0]
    rows = rank_ref.shape[1]
    start = jnp.int32(0)
    for s in range(count_ref.shape[0]):
        start = start + jnp.where(s < me, count_ref[s], 0)
    kept = rank_ref[...] < count_ref[me]
    upper = lax.broadcasted_iota(jnp.int32, (rows, rows), 0) <= lax.broadcasted_iota(
        jnp.int32, (rows, rows), 1
    )
    flags = jnp.broadcast_to(kept.astype(jnp.float32), (8, rows)).astype(jnp.bfloat16)
    order = (
        jnp.dot(
            flags, upper.astype(jnp.float32).astype(jnp.bfloat16), preferred_element_type=jnp.float32
        )[:1].astype(jnp.int32)
        - 1
    )
    kv_out[...] = jnp.where(kept, order + (start & (TILE - 1)), -1)
    place = start + order
    first = lax.div(start, TOK_DEV)
    device = first + jnp.zeros_like(place)
    for step in range(1, reach + 1):
        device = device + (place >= (first + step) * TOK_DEV).astype(jnp.int32)
    within = place - device * TOK_DEV
    cls = jnp.zeros_like(place)
    for step in range(1, groups):
        cls = cls + (within >= step * block).astype(jnp.int32)
    low = first * block + jnp.clip(start - first * TOK_DEV - cls * block, 0, block)
    slot = cls * cap + device * block + within - cls * block - low + (low & (TILE - 1))
    q_out[...] = jnp.where(kept, slot, -1)


def find_slots(me, counts, ranks, reach, groups, block, cap):
    shape = jax.ShapeDtypeStruct(ranks.shape, jnp.int32)
    return pl.pallas_call(
        functools.partial(slots_kernel, reach, groups, block, cap),
        in_specs=[whole_smem(), whole_smem(), whole_vmem()],
        out_specs=[whole_vmem()] * 2,
        out_shape=[shape, shape],
        compiler_params=params(),
        cost_estimate=pl.CostEstimate(flops=2**20, bytes_accessed=2**14, transcendentals=0),
    )(me, counts, ranks)


def pack_kernel(turned, classes, cap, width, slot_ref, cos_ref, sin_ref, row_ref, *rest):
    out_refs, hot_ref = rest[:-1], rest[-1]

    @pl.when(pl.program_id(0) == 0)
    def _():
        ids = lax.broadcasted_iota(jnp.int32, hot_ref.shape, 0)
        hot_ref[...] = (ids == slot_ref[...]).astype(jnp.float32).astype(jnp.bfloat16)

    if turned:
        rows = jnp.concatenate(
            [
                turn(row_ref[:, h * HD : (h + 1) * HD], cos_ref[...], sin_ref[...])
                for h in range(width)
            ],
            axis=1,
        )
    else:
        rows = row_ref[...]
    for j, out_ref in enumerate(out_refs):
        for r in range(classes):
            first = (j * classes + r) * cap
            moved = jnp.dot(
                hot_ref[first : first + cap, :], rows, preferred_element_type=jnp.float32
            ).astype(jnp.bfloat16)
            for h in range(width):
                out_ref[h, r] = moved[:, h * HD : (h + 1) * HD]


def pack(slots, cosine, sine, rows, turned, chunks, classes, cap):
    count = rows.shape[0]
    heads = rows.shape[1] // HD
    width = min(2, heads)
    fixed = lambda i: (0, 0)
    total = chunks * classes * cap
    return pl.pallas_call(
        functools.partial(pack_kernel, turned, classes, cap, width),
        grid=(heads // width,),
        in_specs=[
            pl.BlockSpec((1, count), fixed),
            pl.BlockSpec((count, HD), fixed),
            pl.BlockSpec((count, HD), fixed),
            pl.BlockSpec((count, width * HD), lambda i: (0, i)),
        ],
        out_specs=[pl.BlockSpec((width, classes, cap, HD), lambda i: (i, 0, 0, 0))] * chunks,
        out_shape=[jax.ShapeDtypeStruct((heads, classes, cap, HD), jnp.bfloat16)] * chunks,
        scratch_shapes=[pltpu.VMEM((total, count), jnp.bfloat16)],
        compiler_params=params(),
        cost_estimate=pl.CostEstimate(
            flops=2 * heads * total * count * HD, bytes_accessed=count * heads * HD * 4, transcendentals=0
        ),
    )(slots, cosine, sine, rows)


def piece_rows(cap):
    return max(rows for rows in range(TILE, PAD + 1, TILE) if cap % rows == 0)


def merge_pieces(low, high, piece, source, add):
    shift = low & (TILE - 1)
    pieces = jnp.where(high > low, lax.div(high - low + shift + piece - 1, piece), 0)
    first = low - shift

    def one(i, carry):
        at = pl.multiple_of(first + i * piece, TILE)
        add(at, source(pl.multiple_of(i * piece, TILE)))
        return carry

    lax.fori_loop(0, pieces, one, 0)


def compact_kernel(offsets, per, total, as_keys, member_ref, count_ref, *rest):
    parts, out, all_rows, starts = rest[:-3], rest[-3], rest[-2], rest[-1]
    members = len(parts)
    piece = piece_rows(parts[0].shape[1])
    all_rows[...] = jnp.zeros_like(all_rows)
    start = jnp.int32(0)
    for s in range(count_ref.shape[0]):
        starts[s] = start
        start = start + count_ref[s]

    def add(at, rows):
        all_rows[pl.ds(at, piece), :] += rows

    for part, offset in zip(parts, offsets):
        for z in range(per):
            source = z * members + (member_ref[0] ^ offset)
            low = starts[source]
            merge_pieces(
                low,
                low + count_ref[source],
                piece,
                lambda at: part[z, pl.ds(at, piece), :],
                add,
            )
    if as_keys:
        for first in range(0, total, 2 * TOK_DEV):
            out[:, first : first + 2 * TOK_DEV] = jnp.transpose(
                all_rows[first : first + 2 * TOK_DEV, :]
            )
    else:
        out[:, :HD] = all_rows[:total, :]
        out[:, HD:] = jnp.ones((total, HD), jnp.bfloat16)


def compact(member, counts, parts, offsets, total, as_keys):
    per = parts[0].shape[0]
    return pl.pallas_call(
        functools.partial(compact_kernel, offsets, per, total, as_keys),
        in_specs=[whole_smem(), whole_smem()] + [whole_vmem()] * len(parts),
        out_specs=whole_vmem(),
        out_shape=jax.ShapeDtypeStruct(
            (HD, total) if as_keys else (total, 2 * HD), jnp.bfloat16
        ),
        scratch_shapes=[
            pltpu.VMEM((total + PAD, HD), jnp.bfloat16),
            pltpu.SMEM(counts.shape, jnp.int32),
        ],
        compiler_params=params(),
        cost_estimate=pl.CostEstimate(flops=total * HD * 8, bytes_accessed=total * HD * 8, transcendentals=0),
    )(member, counts, *parts)


def attend_kernel(ctx_size, block, cls_ref, count_ref, got_ref, key_ref, value_ref, out_ref,
                  query_all, scores_a, scores_b, top_a, top_b, run_max, run_acc):
    span = 2 * TOK_DEV
    pair = 4 * block
    supers = ctx_size // 4
    steps = supers * (supers + 1)
    cls = cls_ref[0]
    piece = piece_rows(got_ref.shape[1])
    query_all[...] = jnp.zeros_like(query_all)

    def add(at, rows):
        query_all[pl.ds(at, piece), :] += rows

    start = jnp.int32(0)
    for s in range(ctx_size):
        end = start + count_ref[s]
        merge_pieces(
            rows_below(start, cls, block),
            rows_below(end, cls, block),
            piece,
            lambda at: got_ref[s, pl.ds(at, piece), :],
            add,
        )
        start = end

    def row_top(found):
        return jnp.broadcast_to(jnp.max(found, axis=1, keepdims=True), (pair, HD))

    def score(scores, top, i, k):
        rows = query_all[pl.ds(pl.multiple_of(jnp.minimum(i, supers - 1) * pair, TILE), pair), :]
        keys = key_ref[:, pl.ds(pl.multiple_of(k * span, HD), span)]
        found = jnp.dot(rows, keys, preferred_element_type=jnp.float32)
        scores[...] = found
        top[...] = row_top(found)

    def mask(scores, top, first):
        row_ids = lax.broadcasted_iota(jnp.int32, (pair, HD), 0)
        row = row_ids + cls * block - first
        for n in range(1, 4):
            row = row + jnp.where(row_ids >= n * block, TOK_DEV - block, 0)
        col = lax.broadcasted_iota(jnp.int32, (pair, span), 1)
        found = jnp.where(
            col <= jnp.concatenate([row] * (span // HD), axis=1), scores[...], masked_score
        )
        scores[...] = found
        top[...] = row_top(found)

    def absorb(scores, top, k):
        before = run_max[...]
        after = jnp.maximum(before, top[...])
        rescale = jnp.exp2((before - after) * exp2_scale)
        run_max[...] = after
        weights = jnp.exp2(
            (scores[...] - jnp.concatenate([after] * (span // HD), axis=1)) * exp2_scale
        )
        values = value_ref[pl.ds(pl.multiple_of(k * span, TILE), span), :]
        run_acc[...] = run_acc[...] * jnp.concatenate([rescale, rescale], axis=1) + jnp.dot(
            weights.astype(jnp.bfloat16), values, preferred_element_type=jnp.float32
        )

    def clear():
        run_max[...] = jnp.full_like(run_max, masked_score)
        run_acc[...] = jnp.zeros_like(run_acc)

    def one_step(now, later, i, k):
        last = k == 2 * i + 1
        next_i = jnp.where(last, i + 1, i)
        next_k = jnp.where(last, 0, k + 1)
        score(*later, next_i, next_k)
        absorb(*now, k)

        @pl.when(last)
        def _():
            result = (run_acc[:, :HD] / run_acc[:, HD:]).astype(jnp.bfloat16)
            for n in range(4):
                out_ref[4 * i + n] = result[n * block : (n + 1) * block]
            clear()

        @pl.when(next_k >= 2 * next_i)
        def _():
            mask(*later, (next_k - 2 * next_i) * span)

        return next_i, next_k

    buffers_a, buffers_b = (scores_a, top_a), (scores_b, top_b)
    clear()
    score(*buffers_a, 0, 0)
    mask(*buffers_a, 0)

    def two_steps(t, at):
        at = one_step(buffers_a, buffers_b, *at)
        return one_step(buffers_b, buffers_a, *at)

    lax.fori_loop(0, steps // 2, two_steps, (jnp.int32(0), jnp.int32(0)))


def attend(cls, counts, got, keys, values, block):
    ctx_size = got.shape[0]
    total = values.shape[0]
    pairs = total * ctx_size * block // 2
    return pl.pallas_call(
        functools.partial(attend_kernel, ctx_size, block),
        in_specs=[whole_smem()] * 2 + [whole_vmem()] * 3,
        out_specs=whole_vmem(),
        out_shape=jax.ShapeDtypeStruct((ctx_size, block, HD), jnp.bfloat16),
        scratch_shapes=[
            pltpu.VMEM((ctx_size * block + PAD, HD), jnp.bfloat16),
            pltpu.VMEM((4 * block, 2 * TOK_DEV), jnp.float32),
            pltpu.VMEM((4 * block, 2 * TOK_DEV), jnp.float32),
            pltpu.VMEM((4 * block, HD), jnp.float32),
            pltpu.VMEM((4 * block, HD), jnp.float32),
            pltpu.VMEM((4 * block, HD), jnp.float32),
            pltpu.VMEM((4 * block, 2 * HD), jnp.float32),
        ],
        compiler_params=params(),
        cost_estimate=pl.CostEstimate(
            flops=pairs * 8 * HD, bytes_accessed=total * HD * 8, transcendentals=pairs
        ),
    )(cls, counts, got, keys, values)


def project_kernel(classes, chunks, column_ref, *rest):
    got_refs, (weight_ref, out_ref, rows_ref) = rest[:chunks], rest[chunks:]
    block = got_refs[0].shape[1]

    @pl.when(pl.program_id(0) == 0)
    def _():
        for j, got_ref in enumerate(got_refs):
            for d in range(got_ref.shape[0]):
                h, r = d // classes, d % classes
                first = (j * classes + r) * block
                rows_ref[first : first + block, h * HD : (h + 1) * HD] = got_ref[d]

    out_ref[...] = jnp.dot(
        rows_ref[...], weight_ref[...], preferred_element_type=jnp.float32
    ).astype(jnp.bfloat16)


def project(first_column, got, weight, columns, classes):
    ctx_size, block, _ = got[0].shape
    rows, depth = len(got) * classes * block, weight.shape[0]
    step = min(512, columns)
    return pl.pallas_call(
        functools.partial(project_kernel, classes, len(got)),
        grid_spec=pltpu.PrefetchScalarGridSpec(
            num_scalar_prefetch=1,
            grid=(columns // step,),
            in_specs=[pl.BlockSpec((ctx_size, block, HD), lambda i, first: (0, 0, 0))] * len(got)
            + [pl.BlockSpec((depth, step), lambda i, first: (0, first[0] + i))],
            out_specs=pl.BlockSpec((rows, step), lambda i, first: (0, i)),
            scratch_shapes=[pltpu.VMEM((rows, depth), jnp.bfloat16)],
        ),
        out_shape=jax.ShapeDtypeStruct((rows, columns), jnp.bfloat16),
        compiler_params=params(),
        cost_estimate=pl.CostEstimate(
            flops=2 * rows * depth * columns, bytes_accessed=2 * depth * columns, transcendentals=0
        ),
    )((first_column // step).astype(jnp.int32).reshape(1), *got, weight)


def join_kernel(chunks, parts, head_ref, *rest):
    got_refs, weight_refs = rest[:chunks], rest[chunks : chunks + parts]
    own_ref, out_ref, rows_ref = rest[chunks + parts :]
    block = got_refs[0].shape[1]
    firsts = [sum(ref.shape[0] for ref in weight_refs[:p]) for p in range(parts)]

    @pl.when(pl.program_id(0) == 0)
    def _():
        for j, got_ref in enumerate(got_refs):
            for p in range(parts):
                for n in range(weight_refs[p].shape[0] // HD):
                    at = firsts[p] + n * HD
                    rows_ref[j * block : (j + 1) * block, at : at + HD] = got_ref[head_ref[p] + n]

    total = jnp.zeros(out_ref.shape, jnp.float32)
    for first, weight_ref in zip(firsts, weight_refs):
        total = total + jnp.dot(
            rows_ref[:, first : first + weight_ref.shape[0]],
            weight_ref[...],
            preferred_element_type=jnp.float32,
        )
    theirs = total.astype(jnp.bfloat16).astype(jnp.float32)
    out_ref[...] = (own_ref[...].astype(jnp.float32) + theirs).astype(jnp.bfloat16)


def join(first_heads, got, weights, own):
    ctx_size, block, _ = got[0].shape
    rows, columns = own.shape
    depth = sum(weight.shape[0] for weight in weights)
    step = min(512, columns)
    tile = pl.BlockSpec((rows, step), lambda i, first: (0, i))
    return pl.pallas_call(
        functools.partial(join_kernel, len(got), len(weights)),
        grid_spec=pltpu.PrefetchScalarGridSpec(
            num_scalar_prefetch=1,
            grid=(columns // step,),
            in_specs=[pl.BlockSpec((ctx_size, block, HD), lambda i, first: (0, 0, 0))] * len(got)
            + [pl.BlockSpec((weight.shape[0], step), lambda i, first: (0, i)) for weight in weights]
            + [tile],
            out_specs=tile,
            scratch_shapes=[pltpu.VMEM((rows, depth), jnp.bfloat16)],
        ),
        out_shape=jax.ShapeDtypeStruct((rows, columns), jnp.bfloat16),
        compiler_params=params(),
        cost_estimate=pl.CostEstimate(
            flops=2 * rows * depth * columns,
            bytes_accessed=2 * depth * columns,
            transcendentals=0,
        ),
    )(first_heads, *got, *weights, own)


def tables(query_rows):
    half_dim = HD // 2
    positions = lax.axis_index("ctx") * query_rows + jnp.arange(query_rows, dtype=jnp.int32)
    lane = jnp.arange(HD, dtype=jnp.int32)
    pair_id = jnp.where(lane < half_dim, lane, lane - half_dim)
    inv_freq = rope_base ** (-(pair_id.astype(jnp.float32) * 2.0 / HD))
    angles = positions.astype(jnp.float32)[:, None] * inv_freq[None, :]
    sine = jnp.sin(angles)
    return jnp.cos(angles), jnp.where(lane[None, :] < half_dim, -sine, sine)


def local(query, key, value, keep_rank, kept_count, out_weight):
    ctx_size = lax.axis_size("ctx")
    tp_size = lax.axis_size("tp")
    me = lax.axis_index("ctx")
    tp_me = lax.axis_index("tp")
    orig_rows = query.shape[0]
    heads = query.shape[1] // HD
    kv_heads = key.shape[1] // HD
    members = ctx_size // kv_heads
    classes = ctx_size // heads
    chunks = CHUNKS if classes == 1 else 1
    block = TOK_DEV // (chunks * classes)
    total = ctx_size * TOK_DEV
    reach = orig_rows // TOK_DEV
    cap = reach * block + TILE
    cap_kv = orig_rows + TILE
    columns = out_weight.shape[1] // tp_size

    kv_slots, q_slots = find_slots(
        me.reshape(1), kept_count, keep_rank, reach, chunks * classes, block, cap
    )
    cosine, sine = tables(orig_rows)

    across = [[z * members + m for z in range(kv_heads)] for m in range(members)]

    member = (me & (members - 1)).reshape(1)

    def pack_shared(rows, turned):
        (packed,) = pack(kv_slots, cosine, sine, rows, turned, 1, 1, cap_kv)
        return packed.reshape(kv_heads, cap_kv, HD)

    def send_across(packed):
        if kv_heads == 1:
            return packed
        return lax.all_to_all(
            packed, "ctx", split_axis=0, concat_axis=0, tiled=True, axis_index_groups=across
        )

    def swap(parts, bit):
        pairs = [(d, d ^ bit) for d in range(ctx_size)]
        return parts + [lax.ppermute(part, "ctx", pairs) for part in parts]

    bits = [members >> n for n in range(1, members.bit_length())]
    offsets = [0]
    for bit in bits:
        offsets = offsets + [offset ^ bit for offset in offsets]

    def send_query(packed):
        return lax.all_to_all(
            packed.reshape(ctx_size, cap, HD), "ctx", split_axis=0, concat_axis=0, tiled=True
        )

    traded = tp_size == 2 and classes == 1 and heads == 16 and chunks == 2
    both = [(0, 1), (1, 0)]

    def chip_swap(part, bit):
        return lax.ppermute(part, "ctx", [(d, d ^ bit) for d in range(ctx_size)])

    core, side = me & 1, (me >> 1) & 1
    sizes = [2, 2, 2]

    def at_side(left, right):
        return jnp.where(side == 0, left, right)

    lows = [at_side(0, 6), at_side(2, 4), at_side(4, 2)]

    def weight_rows(p):
        return lax.dynamic_slice(
            out_weight,
            ((core * 8 + lows[p]) * HD, (1 - tp_me) * columns),
            (sizes[p] * HD, columns),
        )

    def trade(part):
        return lax.ppermute(part, "tp", both)

    key_packed = pack_shared(key, True)
    slices = []
    if traded:
        key_packed, out_weight = lax.optimization_barrier((key_packed, out_weight))
        first_slice, value = lax.optimization_barrier((weight_rows(0), value))
        slices = [first_slice] + [weight_rows(p) for p in range(1, 3)]
    key_parts = [send_across(key_packed)]
    value_packed, key_parts, slices = lax.optimization_barrier(
        (pack_shared(value, False), key_parts, slices)
    )
    key_parts = swap(key_parts, bits[0])
    value_parts = [send_across(value_packed)]
    came = [trade(slices[0])] if traded else []
    packed_q = list(pack(q_slots, cosine, sine, query, True, chunks, classes, cap))
    packed_q[0], key_parts, value_parts, came, slices = lax.optimization_barrier(
        (packed_q[0], key_parts, value_parts, came, slices)
    )
    came = came + [trade(one) for one in slices[1:2]]
    got_q = [send_query(packed_q[0])]
    value_parts = swap(value_parts, bits[0])
    for bit in bits[1:]:
        key_parts = swap(key_parts, bit)
    keys = compact(member, kept_count, key_parts, offsets, total, True)
    if chunks > 1:
        packed_q[1], value_parts, keys = lax.optimization_barrier((packed_q[1], value_parts, keys))
    for bit in bits[1:]:
        value_parts = swap(value_parts, bit)
    got_q = got_q + [send_query(packed) for packed in packed_q[1:]]
    if traded:
        value_parts, came, slices = lax.optimization_barrier((value_parts, came, slices))
        crossed = [chip_swap(part, 1) for part in came]
        came = came + [trade(slices[2]), chip_swap(came[0], 2)]
    values = compact(member, kept_count, value_parts, offsets, total, False)

    got, done = [], None
    for j in range(chunks):
        cls_j = j * classes + (me & (classes - 1))
        if j > 0:
            got_q[j], done = lax.optimization_barrier((got_q[j], done))
            got.append(lax.all_to_all(done, "ctx", split_axis=0, concat_axis=0, tiled=True))
        done = attend(cls_j.reshape(1), kept_count, got_q[j], keys, values, block)
    if chunks > 1:
        done, got, came = lax.optimization_barrier((done, got, came))
    got.append(lax.all_to_all(done, "ctx", split_axis=0, concat_axis=0, tiled=True))
    if traded:
        theirs = [trade(one) for one in got]
        came = came + crossed + [chip_swap(part, 1) for part in came[2:]]
        own = project(tp_me * columns, got, out_weight, columns, classes)
        order = lows + [at_side(6, 0)]
        first_heads = jnp.stack([c * 8 + at for c in (core, 1 - core) for at in order])
        return join(first_heads.astype(jnp.int32), theirs, came, own)
    full = project(jnp.int32(0) * tp_me, got, out_weight, columns * tp_size, classes)
    split = jnp.transpose(full.reshape(full.shape[0], tp_size, columns), (1, 0, 2))
    swapped = lax.all_to_all(split, "tp", split_axis=0, concat_axis=0, tiled=True)
    return jnp.sum(swapped.astype(jnp.float32), axis=0).astype(jnp.bfloat16)


def solution(mesh):
    placed = (P("ctx", "tp"), P("ctx", "tp"), P("ctx", "tp"), P("ctx", None), P(), P("tp", None))
    return jax.shard_map(
        local, mesh=mesh, in_specs=placed, out_specs=P("ctx", "tp"), check_vma=False
    )
```

```python
import functools
import math

import jax
import jax.numpy as jnp
from jax import lax
from jax.experimental import pallas as pl
from jax.experimental.pallas import tpu as pltpu
from jax.sharding import PartitionSpec as P

HD = 128
TOK_DEV = 384
TILE = 16
PAD = 288
CHUNKS = 3

rope_base = 1000000.0
masked_score = -1e30
exp2_scale = math.log2(math.e) / math.sqrt(HD)
VMEM_BYTES = 58 * 1024 * 1024


def whole_vmem():
    return pl.BlockSpec(memory_space=pltpu.VMEM)


def whole_smem():
    return pl.BlockSpec(memory_space=pltpu.SMEM)


def params():
    return pltpu.CompilerParams(vmem_limit_bytes=VMEM_BYTES)


def turn(rows, cosine, sine):
    as_float = rows.astype(jnp.float32)
    swapped = pltpu.roll(as_float, HD // 2, 1)
    return (as_float * cosine + swapped * sine).astype(jnp.bfloat16)


def rows_below(start, cls, block):
    whole = lax.div(start, TOK_DEV)
    return whole * block + jnp.clip(start - whole * TOK_DEV - cls * block, 0, block)


def slots_kernel(reach, groups, block, cap, me_ref, count_ref, rank_ref, kv_out, q_out):
    me = me_ref[0]
    rows = rank_ref.shape[1]
    start = jnp.int32(0)
    for s in range(count_ref.shape[0]):
        start = start + jnp.where(s < me, count_ref[s], 0)
    kept = rank_ref[...] < count_ref[me]
    upper = lax.broadcasted_iota(jnp.int32, (rows, rows), 0) <= lax.broadcasted_iota(
        jnp.int32, (rows, rows), 1
    )
    flags = jnp.broadcast_to(kept.astype(jnp.float32), (8, rows)).astype(jnp.bfloat16)
    order = (
        jnp.dot(
            flags, upper.astype(jnp.float32).astype(jnp.bfloat16), preferred_element_type=jnp.float32
        )[:1].astype(jnp.int32)
        - 1
    )
    kv_out[...] = jnp.where(kept, order + (start & (TILE - 1)), -1)
    place = start + order
    first = lax.div(start, TOK_DEV)
    device = first + jnp.zeros_like(place)
    for step in range(1, reach + 1):
        device = device + (place >= (first + step) * TOK_DEV).astype(jnp.int32)
    within = place - device * TOK_DEV
    cls = jnp.zeros_like(place)
    for step in range(1, groups):
        cls = cls + (within >= step * block).astype(jnp.int32)
    low = first * block + jnp.clip(start - first * TOK_DEV - cls * block, 0, block)
    slot = cls * cap + device * block + within - cls * block - low + (low & (TILE - 1))
    q_out[...] = jnp.where(kept, slot, -1)


def find_slots(me, counts, ranks, reach, groups, block, cap):
    shape = jax.ShapeDtypeStruct(ranks.shape, jnp.int32)
    return pl.pallas_call(
        functools.partial(slots_kernel, reach, groups, block, cap),
        in_specs=[whole_smem(), whole_smem(), whole_vmem()],
        out_specs=[whole_vmem()] * 2,
        out_shape=[shape, shape],
        compiler_params=params(),
        cost_estimate=pl.CostEstimate(flops=2**20, bytes_accessed=2**14, transcendentals=0),
    )(me, counts, ranks)


def pack_kernel(turned, classes, cap, width, slot_ref, cos_ref, sin_ref, row_ref, *rest):
    out_refs, hot_ref = rest[:-1], rest[-1]

    @pl.when(pl.program_id(0) == 0)
    def _():
        ids = lax.broadcasted_iota(jnp.int32, hot_ref.shape, 0)
        hot_ref[...] = (ids == slot_ref[...]).astype(jnp.float32).astype(jnp.bfloat16)

    if turned:
        rows = jnp.concatenate(
            [
                turn(row_ref[:, h * HD : (h + 1) * HD], cos_ref[...], sin_ref[...])
                for h in range(width)
            ],
            axis=1,
        )
    else:
        rows = row_ref[...]
    for j, out_ref in enumerate(out_refs):
        for r in range(classes):
            first = (j * classes + r) * cap
            moved = jnp.dot(
                hot_ref[first : first + cap, :], rows, preferred_element_type=jnp.float32
            ).astype(jnp.bfloat16)
            for h in range(width):
                out_ref[h, r] = moved[:, h * HD : (h + 1) * HD]


def pack(slots, cosine, sine, rows, turned, chunks, classes, cap):
    count = rows.shape[0]
    heads = rows.shape[1] // HD
    width = min(2, heads)
    fixed = lambda i: (0, 0)
    total = chunks * classes * cap
    return pl.pallas_call(
        functools.partial(pack_kernel, turned, classes, cap, width),
        grid=(heads // width,),
        in_specs=[
            pl.BlockSpec((1, count), fixed),
            pl.BlockSpec((count, HD), fixed),
            pl.BlockSpec((count, HD), fixed),
            pl.BlockSpec((count, width * HD), lambda i: (0, i)),
        ],
        out_specs=[pl.BlockSpec((width, classes, cap, HD), lambda i: (i, 0, 0, 0))] * chunks,
        out_shape=[jax.ShapeDtypeStruct((heads, classes, cap, HD), jnp.bfloat16)] * chunks,
        scratch_shapes=[pltpu.VMEM((total, count), jnp.bfloat16)],
        compiler_params=params(),
        cost_estimate=pl.CostEstimate(
            flops=2 * heads * total * count * HD, bytes_accessed=count * heads * HD * 4, transcendentals=0
        ),
    )(slots, cosine, sine, rows)


def piece_rows(cap):
    return max(rows for rows in range(TILE, PAD + 1, TILE) if cap % rows == 0)


def merge_pieces(low, high, piece, source, add):
    shift = low & (TILE - 1)
    pieces = jnp.where(high > low, lax.div(high - low + shift + piece - 1, piece), 0)
    first = low - shift

    def one(i, carry):
        at = pl.multiple_of(first + i * piece, TILE)
        add(at, source(pl.multiple_of(i * piece, TILE)))
        return carry

    lax.fori_loop(0, pieces, one, 0)


def compact_kernel(offsets, per, total, as_keys, member_ref, count_ref, *rest):
    parts, out, all_rows, starts = rest[:-3], rest[-3], rest[-2], rest[-1]
    members = len(parts)
    piece = piece_rows(parts[0].shape[1])
    all_rows[...] = jnp.zeros_like(all_rows)
    start = jnp.int32(0)
    for s in range(count_ref.shape[0]):
        starts[s] = start
        start = start + count_ref[s]

    def add(at, rows):
        all_rows[pl.ds(at, piece), :] += rows

    for part, offset in zip(parts, offsets):
        for z in range(per):
            source = z * members + (member_ref[0] ^ offset)
            low = starts[source]
            merge_pieces(
                low,
                low + count_ref[source],
                piece,
                lambda at: part[z, pl.ds(at, piece), :],
                add,
            )
    if as_keys:
        for first in range(0, total, 2 * TOK_DEV):
            out[:, first : first + 2 * TOK_DEV] = jnp.transpose(
                all_rows[first : first + 2 * TOK_DEV, :]
            )
    else:
        out[:, :HD] = all_rows[:total, :]
        out[:, HD:] = jnp.ones((total, HD), jnp.bfloat16)


def compact(member, counts, parts, offsets, total, as_keys):
    per = parts[0].shape[0]
    return pl.pallas_call(
        functools.partial(compact_kernel, offsets, per, total, as_keys),
        in_specs=[whole_smem(), whole_smem()] + [whole_vmem()] * len(parts),
        out_specs=whole_vmem(),
        out_shape=jax.ShapeDtypeStruct(
            (HD, total) if as_keys else (total, 2 * HD), jnp.bfloat16
        ),
        scratch_shapes=[
            pltpu.VMEM((total + PAD, HD), jnp.bfloat16),
            pltpu.SMEM(counts.shape, jnp.int32),
        ],
        compiler_params=params(),
        cost_estimate=pl.CostEstimate(flops=total * HD * 8, bytes_accessed=total * HD * 8, transcendentals=0),
    )(member, counts, *parts)


def attend_kernel(ctx_size, block, cls_ref, count_ref, got_ref, key_ref, value_ref, out_ref,
                  query_all, scores_a, scores_b, top_a, top_b, run_max, run_acc):
    span = 2 * TOK_DEV
    pair = 4 * block
    supers = ctx_size // 4
    steps = supers * (supers + 1)
    cls = cls_ref[0]
    piece = piece_rows(got_ref.shape[1])
    query_all[...] = jnp.zeros_like(query_all)

    def add(at, rows):
        query_all[pl.ds(at, piece), :] += rows

    start = jnp.int32(0)
    for s in range(ctx_size):
        end = start + count_ref[s]
        merge_pieces(
            rows_below(start, cls, block),
            rows_below(end, cls, block),
            piece,
            lambda at: got_ref[s, pl.ds(at, piece), :],
            add,
        )
        start = end

    def row_top(found):
        return jnp.broadcast_to(jnp.max(found, axis=1, keepdims=True), (pair, HD))

    def score(scores, top, i, k):
        rows = query_all[pl.ds(pl.multiple_of(jnp.minimum(i, supers - 1) * pair, TILE), pair), :]
        keys = key_ref[:, pl.ds(pl.multiple_of(k * span, HD), span)]
        found = jnp.dot(rows, keys, preferred_element_type=jnp.float32)
        scores[...] = found
        top[...] = row_top(found)

    def mask(scores, top, first):
        row_ids = lax.broadcasted_iota(jnp.int32, (pair, HD), 0)
        row = row_ids + cls * block - first
        for n in range(1, 4):
            row = row + jnp.where(row_ids >= n * block, TOK_DEV - block, 0)
        col = lax.broadcasted_iota(jnp.int32, (pair, span), 1)
        found = jnp.where(
            col <= jnp.concatenate([row] * (span // HD), axis=1), scores[...], masked_score
        )
        scores[...] = found
        top[...] = row_top(found)

    def absorb(scores, top, k):
        before = run_max[...]
        after = jnp.maximum(before, top[...])
        rescale = jnp.exp2((before - after) * exp2_scale)
        run_max[...] = after
        weights = jnp.exp2(
            (scores[...] - jnp.concatenate([after] * (span // HD), axis=1)) * exp2_scale
        )
        values = value_ref[pl.ds(pl.multiple_of(k * span, TILE), span), :]
        run_acc[...] = run_acc[...] * jnp.concatenate([rescale, rescale], axis=1) + jnp.dot(
            weights.astype(jnp.bfloat16), values, preferred_element_type=jnp.float32
        )

    def clear():
        run_max[...] = jnp.full_like(run_max, masked_score)
        run_acc[...] = jnp.zeros_like(run_acc)

    def one_step(now, later, i, k):
        last = k == 2 * i + 1
        next_i = jnp.where(last, i + 1, i)
        next_k = jnp.where(last, 0, k + 1)
        score(*later, next_i, next_k)
        absorb(*now, k)

        @pl.when(last)
        def _():
            result = (run_acc[:, :HD] / run_acc[:, HD:]).astype(jnp.bfloat16)
            for n in range(4):
                out_ref[4 * i + n] = result[n * block : (n + 1) * block]
            clear()

        @pl.when(next_k >= 2 * next_i)
        def _():
            mask(*later, (next_k - 2 * next_i) * span)

        return next_i, next_k

    buffers_a, buffers_b = (scores_a, top_a), (scores_b, top_b)
    clear()
    score(*buffers_a, 0, 0)
    mask(*buffers_a, 0)

    def two_steps(t, at):
        at = one_step(buffers_a, buffers_b, *at)
        return one_step(buffers_b, buffers_a, *at)

    lax.fori_loop(0, steps // 2, two_steps, (jnp.int32(0), jnp.int32(0)))


def attend(cls, counts, got, keys, values, block):
    ctx_size = got.shape[0]
    total = values.shape[0]
    pairs = total * ctx_size * block // 2
    return pl.pallas_call(
        functools.partial(attend_kernel, ctx_size, block),
        in_specs=[whole_smem()] * 2 + [whole_vmem()] * 3,
        out_specs=whole_vmem(),
        out_shape=jax.ShapeDtypeStruct((ctx_size, block, HD), jnp.bfloat16),
        scratch_shapes=[
            pltpu.VMEM((ctx_size * block + PAD, HD), jnp.bfloat16),
            pltpu.VMEM((4 * block, 2 * TOK_DEV), jnp.float32),
            pltpu.VMEM((4 * block, 2 * TOK_DEV), jnp.float32),
            pltpu.VMEM((4 * block, HD), jnp.float32),
            pltpu.VMEM((4 * block, HD), jnp.float32),
            pltpu.VMEM((4 * block, HD), jnp.float32),
            pltpu.VMEM((4 * block, 2 * HD), jnp.float32),
        ],
        compiler_params=params(),
        cost_estimate=pl.CostEstimate(
            flops=pairs * 8 * HD, bytes_accessed=total * HD * 8, transcendentals=pairs
        ),
    )(cls, counts, got, keys, values)


def project_kernel(classes, chunks, column_ref, *rest):
    got_refs, (weight_ref, out_ref, rows_ref) = rest[:chunks], rest[chunks:]
    block = got_refs[0].shape[1]

    @pl.when(pl.program_id(0) == 0)
    def _():
        for j, got_ref in enumerate(got_refs):
            for d in range(got_ref.shape[0]):
                h, r = d // classes, d % classes
                first = (j * classes + r) * block
                rows_ref[first : first + block, h * HD : (h + 1) * HD] = got_ref[d]

    out_ref[...] = jnp.dot(
        rows_ref[...], weight_ref[...], preferred_element_type=jnp.float32
    ).astype(jnp.bfloat16)


def project(first_column, got, weight, columns, classes):
    ctx_size, block, _ = got[0].shape
    rows, depth = len(got) * classes * block, weight.shape[0]
    step = min(512, columns)
    return pl.pallas_call(
        functools.partial(project_kernel, classes, len(got)),
        grid_spec=pltpu.PrefetchScalarGridSpec(
            num_scalar_prefetch=1,
            grid=(columns // step,),
            in_specs=[pl.BlockSpec((ctx_size, block, HD), lambda i, first: (0, 0, 0))] * len(got)
            + [pl.BlockSpec((depth, step), lambda i, first: (0, first[0] + i))],
            out_specs=pl.BlockSpec((rows, step), lambda i, first: (0, i)),
            scratch_shapes=[pltpu.VMEM((rows, depth), jnp.bfloat16)],
        ),
        out_shape=jax.ShapeDtypeStruct((rows, columns), jnp.bfloat16),
        compiler_params=params(),
        cost_estimate=pl.CostEstimate(
            flops=2 * rows * depth * columns, bytes_accessed=2 * depth * columns, transcendentals=0
        ),
    )((first_column // step).astype(jnp.int32).reshape(1), *got, weight)


def tables(query_rows):
    half_dim = HD // 2
    positions = lax.axis_index("ctx") * query_rows + jnp.arange(query_rows, dtype=jnp.int32)
    lane = jnp.arange(HD, dtype=jnp.int32)
    pair_id = jnp.where(lane < half_dim, lane, lane - half_dim)
    inv_freq = rope_base ** (-(pair_id.astype(jnp.float32) * 2.0 / HD))
    angles = positions.astype(jnp.float32)[:, None] * inv_freq[None, :]
    sine = jnp.sin(angles)
    return jnp.cos(angles), jnp.where(lane[None, :] < half_dim, -sine, sine)


def local(query, key, value, keep_rank, kept_count, out_weight):
    ctx_size = lax.axis_size("ctx")
    tp_size = lax.axis_size("tp")
    me = lax.axis_index("ctx")
    tp_me = lax.axis_index("tp")
    orig_rows = query.shape[0]
    heads = query.shape[1] // HD
    kv_heads = key.shape[1] // HD
    members = ctx_size // kv_heads
    classes = ctx_size // heads
    chunks = CHUNKS if classes == 1 else 1
    block = TOK_DEV // (chunks * classes)
    total = ctx_size * TOK_DEV
    reach = orig_rows // TOK_DEV
    cap = reach * block + TILE
    cap_kv = orig_rows + TILE
    columns = out_weight.shape[1] // tp_size

    kv_slots, q_slots = find_slots(
        me.reshape(1), kept_count, keep_rank, reach, chunks * classes, block, cap
    )
    cosine, sine = tables(orig_rows)

    across = [[z * members + m for z in range(kv_heads)] for m in range(members)]

    member = (me & (members - 1)).reshape(1)

    def pack_shared(rows, turned):
        (packed,) = pack(kv_slots, cosine, sine, rows, turned, 1, 1, cap_kv)
        return packed.reshape(kv_heads, cap_kv, HD)

    def send_across(packed):
        if kv_heads == 1:
            return packed
        return lax.all_to_all(
            packed, "ctx", split_axis=0, concat_axis=0, tiled=True, axis_index_groups=across
        )

    def swap(parts, bit):
        pairs = [(d, d ^ bit) for d in range(ctx_size)]
        return parts + [lax.ppermute(part, "ctx", pairs) for part in parts]

    bits = [members >> n for n in range(1, members.bit_length())]
    offsets = [0]
    for bit in bits:
        offsets = offsets + [offset ^ bit for offset in offsets]

    def send_query(packed):
        return lax.all_to_all(
            packed.reshape(ctx_size, cap, HD), "ctx", split_axis=0, concat_axis=0, tiled=True
        )

    both = [(0, 1), (1, 0)]
    key_parts = [send_across(pack_shared(key, True))]
    value_packed, key_parts = lax.optimization_barrier((pack_shared(value, False), key_parts))
    key_parts = swap(key_parts, bits[0])
    value_parts = [send_across(value_packed)]
    packed_q = list(pack(q_slots, cosine, sine, query, True, chunks, classes, cap))
    packed_q[0], key_parts, value_parts = lax.optimization_barrier(
        (packed_q[0], key_parts, value_parts)
    )
    got_q = [send_query(packed_q[0])]
    value_parts = swap(value_parts, bits[0])
    for bit in bits[1:]:
        key_parts = swap(key_parts, bit)
    keys = compact(member, kept_count, key_parts, offsets, total, True)
    if chunks > 1:
        packed_q[1], value_parts, keys = lax.optimization_barrier((packed_q[1], value_parts, keys))
    for bit in bits[1:]:
        value_parts = swap(value_parts, bit)
    if chunks > 1:
        got_q.append(send_query(packed_q[1]))
    values = compact(member, kept_count, value_parts, offsets, total, False)

    got, done = [], None
    for j in range(chunks):
        cls_j = j * classes + (me & (classes - 1))
        if j > 0:
            got_q[j], done = lax.optimization_barrier((got_q[j], done))
            got.append(lax.all_to_all(done, "ctx", split_axis=0, concat_axis=0, tiled=True))
        done = attend(cls_j.reshape(1), kept_count, got_q[j], keys, values, block)
        if j > 1:
            done, got[j - 2] = lax.optimization_barrier((done, got[j - 2]))
        if j + 2 < chunks:
            packed_q[j + 2], done = lax.optimization_barrier((packed_q[j + 2], done))
            got_q.append(send_query(packed_q[j + 2]))
    got.append(lax.all_to_all(done, "ctx", split_axis=0, concat_axis=0, tiled=True))
    if tp_size == 2:
        half = columns // 2
        came = [
            [
                lax.ppermute(
                    project((1 - tp_me) * columns + n * half, [one], out_weight, half, classes),
                    "tp",
                    both,
                )
                for n in range(2)
            ]
            for one in got
        ]
        own = project(tp_me * columns, got, out_weight, columns, classes).astype(jnp.float32)
        rows = own.shape[0] // chunks
        return jnp.concatenate(
            [
                jnp.concatenate(
                    [
                        (own[j * rows : (j + 1) * rows, n * half : (n + 1) * half]
                            + part.astype(jnp.float32)
                        ).astype(
                            jnp.bfloat16
                        )
                        for n, part in enumerate(parts)
                    ],
                    axis=1,
                )
                for j, parts in enumerate(came)
            ],
            axis=0,
        )
    full = project(jnp.int32(0) * tp_me, got, out_weight, columns * tp_size, classes)
    split = jnp.transpose(full.reshape(full.shape[0], tp_size, columns), (1, 0, 2))
    swapped = lax.all_to_all(split, "tp", split_axis=0, concat_axis=0, tiled=True)
    return jnp.sum(swapped.astype(jnp.float32), axis=0).astype(jnp.bfloat16)


def solution(mesh):
    placed = (P("ctx", "tp"), P("ctx", "tp"), P("ctx", "tp"), P("ctx", None), P(), P("tp", None))
    return jax.shard_map(
        local, mesh=mesh, in_specs=placed, out_specs=P("ctx", "tp"), check_vma=False
    )
```

```python
import functools
import math

import jax
import jax.numpy as jnp
from jax import lax
from jax.experimental import pallas as pl
from jax.experimental.pallas import tpu as pltpu
from jax.sharding import PartitionSpec as P

HD = 128
TOK_DEV = 384
TILE = 16
PAD = 288
CHUNKS = 2

rope_base = 1000000.0
masked_score = -1e30
exp2_scale = math.log2(math.e) / math.sqrt(HD)
VMEM_BYTES = 58 * 1024 * 1024


def whole_vmem():
    return pl.BlockSpec(memory_space=pltpu.VMEM)


def whole_smem():
    return pl.BlockSpec(memory_space=pltpu.SMEM)


def params():
    return pltpu.CompilerParams(vmem_limit_bytes=VMEM_BYTES)


def turn(rows, cosine, sine):
    as_float = rows.astype(jnp.float32)
    swapped = pltpu.roll(as_float, HD // 2, 1)
    return (as_float * cosine + swapped * sine).astype(jnp.bfloat16)


def rows_below(start, cls, block):
    whole = lax.div(start, TOK_DEV)
    return whole * block + jnp.clip(start - whole * TOK_DEV - cls * block, 0, block)


def slots_kernel(reach, groups, block, cap, me_ref, count_ref, rank_ref, kv_out, q_out):
    me = me_ref[0]
    rows = rank_ref.shape[1]
    start = jnp.int32(0)
    for s in range(count_ref.shape[0]):
        start = start + jnp.where(s < me, count_ref[s], 0)
    kept = rank_ref[...] < count_ref[me]
    upper = lax.broadcasted_iota(jnp.int32, (rows, rows), 0) <= lax.broadcasted_iota(
        jnp.int32, (rows, rows), 1
    )
    flags = jnp.broadcast_to(kept.astype(jnp.float32), (8, rows)).astype(jnp.bfloat16)
    order = (
        jnp.dot(
            flags, upper.astype(jnp.float32).astype(jnp.bfloat16), preferred_element_type=jnp.float32
        )[:1].astype(jnp.int32)
        - 1
    )
    kv_out[...] = jnp.where(kept, order + (start & (TILE - 1)), -1)
    place = start + order
    first = lax.div(start, TOK_DEV)
    device = first + jnp.zeros_like(place)
    for step in range(1, reach + 1):
        device = device + (place >= (first + step) * TOK_DEV).astype(jnp.int32)
    within = place - device * TOK_DEV
    cls = jnp.zeros_like(place)
    for step in range(1, groups):
        cls = cls + (within >= step * block).astype(jnp.int32)
    low = first * block + jnp.clip(start - first * TOK_DEV - cls * block, 0, block)
    slot = cls * cap + device * block + within - cls * block - low + (low & (TILE - 1))
    q_out[...] = jnp.where(kept, slot, -1)


def find_slots(me, counts, ranks, reach, groups, block, cap):
    shape = jax.ShapeDtypeStruct(ranks.shape, jnp.int32)
    return pl.pallas_call(
        functools.partial(slots_kernel, reach, groups, block, cap),
        in_specs=[whole_smem(), whole_smem(), whole_vmem()],
        out_specs=[whole_vmem()] * 2,
        out_shape=[shape, shape],
        compiler_params=params(),
        cost_estimate=pl.CostEstimate(flops=2**20, bytes_accessed=2**14, transcendentals=0),
    )(me, counts, ranks)


def pack_kernel(turned, classes, cap, width, slot_ref, cos_ref, sin_ref, row_ref, *rest):
    out_refs, hot_ref = rest[:-1], rest[-1]

    @pl.when(pl.program_id(0) == 0)
    def _():
        ids = lax.broadcasted_iota(jnp.int32, hot_ref.shape, 0)
        hot_ref[...] = (ids == slot_ref[...]).astype(jnp.float32).astype(jnp.bfloat16)

    if turned:
        rows = jnp.concatenate(
            [
                turn(row_ref[:, h * HD : (h + 1) * HD], cos_ref[...], sin_ref[...])
                for h in range(width)
            ],
            axis=1,
        )
    else:
        rows = row_ref[...]
    for j, out_ref in enumerate(out_refs):
        for r in range(classes):
            first = (j * classes + r) * cap
            moved = jnp.dot(
                hot_ref[first : first + cap, :], rows, preferred_element_type=jnp.float32
            ).astype(jnp.bfloat16)
            for h in range(width):
                out_ref[h, r] = moved[:, h * HD : (h + 1) * HD]


def pack(slots, cosine, sine, rows, turned, chunks, classes, cap):
    count = rows.shape[0]
    heads = rows.shape[1] // HD
    width = min(2, heads)
    fixed = lambda i: (0, 0)
    total = chunks * classes * cap
    return pl.pallas_call(
        functools.partial(pack_kernel, turned, classes, cap, width),
        grid=(heads // width,),
        in_specs=[
            pl.BlockSpec((1, count), fixed),
            pl.BlockSpec((count, HD), fixed),
            pl.BlockSpec((count, HD), fixed),
            pl.BlockSpec((count, width * HD), lambda i: (0, i)),
        ],
        out_specs=[pl.BlockSpec((width, classes, cap, HD), lambda i: (i, 0, 0, 0))] * chunks,
        out_shape=[jax.ShapeDtypeStruct((heads, classes, cap, HD), jnp.bfloat16)] * chunks,
        scratch_shapes=[pltpu.VMEM((total, count), jnp.bfloat16)],
        compiler_params=params(),
        cost_estimate=pl.CostEstimate(
            flops=2 * heads * total * count * HD, bytes_accessed=count * heads * HD * 4, transcendentals=0
        ),
    )(slots, cosine, sine, rows)


def piece_rows(cap):
    return max(rows for rows in range(TILE, PAD + 1, TILE) if cap % rows == 0)


def merge_pieces(low, high, piece, source, add):
    shift = low & (TILE - 1)
    pieces = jnp.where(high > low, lax.div(high - low + shift + piece - 1, piece), 0)
    first = low - shift

    def one(i, carry):
        at = pl.multiple_of(first + i * piece, TILE)
        add(at, source(pl.multiple_of(i * piece, TILE)))
        return carry

    lax.fori_loop(0, pieces, one, 0)


def compact_kernel(offsets, per, total, as_keys, member_ref, count_ref, *rest):
    parts, out, all_rows, starts = rest[:-3], rest[-3], rest[-2], rest[-1]
    members = len(parts)
    piece = piece_rows(parts[0].shape[1])
    all_rows[...] = jnp.zeros_like(all_rows)
    start = jnp.int32(0)
    for s in range(count_ref.shape[0]):
        starts[s] = start
        start = start + count_ref[s]

    def add(at, rows):
        all_rows[pl.ds(at, piece), :] += rows

    for part, offset in zip(parts, offsets):
        for z in range(per):
            source = z * members + (member_ref[0] ^ offset)
            low = starts[source]
            merge_pieces(
                low,
                low + count_ref[source],
                piece,
                lambda at: part[z, pl.ds(at, piece), :],
                add,
            )
    if as_keys:
        for first in range(0, total, 2 * TOK_DEV):
            out[:, first : first + 2 * TOK_DEV] = jnp.transpose(
                all_rows[first : first + 2 * TOK_DEV, :]
            )
    else:
        out[:, :HD] = all_rows[:total, :]
        out[:, HD:] = jnp.ones((total, HD), jnp.bfloat16)


def compact(member, counts, parts, offsets, total, as_keys):
    per = parts[0].shape[0]
    return pl.pallas_call(
        functools.partial(compact_kernel, offsets, per, total, as_keys),
        in_specs=[whole_smem(), whole_smem()] + [whole_vmem()] * len(parts),
        out_specs=whole_vmem(),
        out_shape=jax.ShapeDtypeStruct(
            (HD, total) if as_keys else (total, 2 * HD), jnp.bfloat16
        ),
        scratch_shapes=[
            pltpu.VMEM((total + PAD, HD), jnp.bfloat16),
            pltpu.SMEM(counts.shape, jnp.int32),
        ],
        compiler_params=params(),
        cost_estimate=pl.CostEstimate(flops=total * HD * 8, bytes_accessed=total * HD * 8, transcendentals=0),
    )(member, counts, *parts)


def attend_kernel(ctx_size, block, cls_ref, count_ref, got_ref, key_ref, value_ref, out_ref,
                  query_all, scores_a, scores_b, top_a, top_b, run_max, run_acc):
    span = 2 * TOK_DEV
    pair = 4 * block
    supers = ctx_size // 4
    steps = supers * (supers + 1)
    cls = cls_ref[0]
    piece = piece_rows(got_ref.shape[1])
    query_all[...] = jnp.zeros_like(query_all)

    def add(at, rows):
        query_all[pl.ds(at, piece), :] += rows

    start = jnp.int32(0)
    for s in range(ctx_size):
        end = start + count_ref[s]
        merge_pieces(
            rows_below(start, cls, block),
            rows_below(end, cls, block),
            piece,
            lambda at: got_ref[s, pl.ds(at, piece), :],
            add,
        )
        start = end

    def row_top(found):
        return jnp.broadcast_to(jnp.max(found, axis=1, keepdims=True), (pair, HD))

    def score(scores, top, i, k):
        rows = query_all[pl.ds(pl.multiple_of(jnp.minimum(i, supers - 1) * pair, TILE), pair), :]
        keys = key_ref[:, pl.ds(pl.multiple_of(k * span, HD), span)]
        found = jnp.dot(rows, keys, preferred_element_type=jnp.float32)
        scores[...] = found
        top[...] = row_top(found)

    def mask(scores, top, first):
        row_ids = lax.broadcasted_iota(jnp.int32, (pair, HD), 0)
        row = row_ids + cls * block - first
        for n in range(1, 4):
            row = row + jnp.where(row_ids >= n * block, TOK_DEV - block, 0)
        col = lax.broadcasted_iota(jnp.int32, (pair, span), 1)
        found = jnp.where(
            col <= jnp.concatenate([row] * (span // HD), axis=1), scores[...], masked_score
        )
        scores[...] = found
        top[...] = row_top(found)

    def absorb(scores, top, k):
        before = run_max[...]
        after = jnp.maximum(before, top[...])
        rescale = jnp.exp2((before - after) * exp2_scale)
        run_max[...] = after
        weights = jnp.exp2(
            (scores[...] - jnp.concatenate([after] * (span // HD), axis=1)) * exp2_scale
        )
        values = value_ref[pl.ds(pl.multiple_of(k * span, TILE), span), :]
        run_acc[...] = run_acc[...] * jnp.concatenate([rescale, rescale], axis=1) + jnp.dot(
            weights.astype(jnp.bfloat16), values, preferred_element_type=jnp.float32
        )

    def clear():
        run_max[...] = jnp.full_like(run_max, masked_score)
        run_acc[...] = jnp.zeros_like(run_acc)

    def one_step(now, later, i, k):
        last = k == 2 * i + 1
        next_i = jnp.where(last, i + 1, i)
        next_k = jnp.where(last, 0, k + 1)
        score(*later, next_i, next_k)
        absorb(*now, k)

        @pl.when(last)
        def _():
            result = (run_acc[:, :HD] / run_acc[:, HD:]).astype(jnp.bfloat16)
            for n in range(4):
                out_ref[4 * i + n] = result[n * block : (n + 1) * block]
            clear()

        @pl.when(next_k >= 2 * next_i)
        def _():
            mask(*later, (next_k - 2 * next_i) * span)

        return next_i, next_k

    buffers_a, buffers_b = (scores_a, top_a), (scores_b, top_b)
    clear()
    score(*buffers_a, 0, 0)
    mask(*buffers_a, 0)

    def two_steps(t, at):
        at = one_step(buffers_a, buffers_b, *at)
        return one_step(buffers_b, buffers_a, *at)

    lax.fori_loop(0, steps // 2, two_steps, (jnp.int32(0), jnp.int32(0)))


def attend(cls, counts, got, keys, values, block):
    ctx_size = got.shape[0]
    total = values.shape[0]
    pairs = total * ctx_size * block // 2
    return pl.pallas_call(
        functools.partial(attend_kernel, ctx_size, block),
        in_specs=[whole_smem()] * 2 + [whole_vmem()] * 3,
        out_specs=whole_vmem(),
        out_shape=jax.ShapeDtypeStruct((ctx_size, block, HD), jnp.bfloat16),
        scratch_shapes=[
            pltpu.VMEM((ctx_size * block + PAD, HD), jnp.bfloat16),
            pltpu.VMEM((4 * block, 2 * TOK_DEV), jnp.float32),
            pltpu.VMEM((4 * block, 2 * TOK_DEV), jnp.float32),
            pltpu.VMEM((4 * block, HD), jnp.float32),
            pltpu.VMEM((4 * block, HD), jnp.float32),
            pltpu.VMEM((4 * block, HD), jnp.float32),
            pltpu.VMEM((4 * block, 2 * HD), jnp.float32),
        ],
        compiler_params=params(),
        cost_estimate=pl.CostEstimate(
            flops=pairs * 8 * HD, bytes_accessed=total * HD * 8, transcendentals=pairs
        ),
    )(cls, counts, got, keys, values)


def project_kernel(classes, chunks, column_ref, *rest):
    got_refs, (weight_ref, out_ref, rows_ref) = rest[:chunks], rest[chunks:]
    block = got_refs[0].shape[1]

    @pl.when(pl.program_id(0) == 0)
    def _():
        for j, got_ref in enumerate(got_refs):
            for d in range(got_ref.shape[0]):
                h, r = d // classes, d % classes
                first = (j * classes + r) * block
                rows_ref[first : first + block, h * HD : (h + 1) * HD] = got_ref[d]

    out_ref[...] = jnp.dot(
        rows_ref[...], weight_ref[...], preferred_element_type=jnp.float32
    ).astype(jnp.bfloat16)


def project(first_column, got, weight, columns, classes):
    ctx_size, block, _ = got[0].shape
    rows, depth = len(got) * classes * block, weight.shape[0]
    step = min(512, columns)
    return pl.pallas_call(
        functools.partial(project_kernel, classes, len(got)),
        grid_spec=pltpu.PrefetchScalarGridSpec(
            num_scalar_prefetch=1,
            grid=(columns // step,),
            in_specs=[pl.BlockSpec((ctx_size, block, HD), lambda i, first: (0, 0, 0))] * len(got)
            + [pl.BlockSpec((depth, step), lambda i, first: (0, first[0] + i))],
            out_specs=pl.BlockSpec((rows, step), lambda i, first: (0, i)),
            scratch_shapes=[pltpu.VMEM((rows, depth), jnp.bfloat16)],
        ),
        out_shape=jax.ShapeDtypeStruct((rows, columns), jnp.bfloat16),
        compiler_params=params(),
        cost_estimate=pl.CostEstimate(
            flops=2 * rows * depth * columns, bytes_accessed=2 * depth * columns, transcendentals=0
        ),
    )((first_column // step).astype(jnp.int32).reshape(1), *got, weight)


def tables(query_rows):
    half_dim = HD // 2
    positions = lax.axis_index("ctx") * query_rows + jnp.arange(query_rows, dtype=jnp.int32)
    lane = jnp.arange(HD, dtype=jnp.int32)
    pair_id = jnp.where(lane < half_dim, lane, lane - half_dim)
    inv_freq = rope_base ** (-(pair_id.astype(jnp.float32) * 2.0 / HD))
    angles = positions.astype(jnp.float32)[:, None] * inv_freq[None, :]
    sine = jnp.sin(angles)
    return jnp.cos(angles), jnp.where(lane[None, :] < half_dim, -sine, sine)


def local(query, key, value, keep_rank, kept_count, out_weight):
    ctx_size = lax.axis_size("ctx")
    tp_size = lax.axis_size("tp")
    me = lax.axis_index("ctx")
    tp_me = lax.axis_index("tp")
    orig_rows = query.shape[0]
    heads = query.shape[1] // HD
    kv_heads = key.shape[1] // HD
    members = ctx_size // kv_heads
    classes = ctx_size // heads
    chunks = CHUNKS if classes == 1 else 1
    block = TOK_DEV // (chunks * classes)
    total = ctx_size * TOK_DEV
    reach = orig_rows // TOK_DEV
    cap = reach * block + TILE
    cap_kv = orig_rows + TILE
    columns = out_weight.shape[1] // tp_size

    kv_slots, q_slots = find_slots(
        me.reshape(1), kept_count, keep_rank, reach, chunks * classes, block, cap
    )
    cosine, sine = tables(orig_rows)

    across = [[z * members + m for z in range(kv_heads)] for m in range(members)]

    member = (me & (members - 1)).reshape(1)

    def pack_shared(rows, turned):
        (packed,) = pack(kv_slots, cosine, sine, rows, turned, 1, 1, cap_kv)
        return packed.reshape(kv_heads, cap_kv, HD)

    def send_across(packed):
        if kv_heads == 1:
            return packed
        return lax.all_to_all(
            packed, "ctx", split_axis=0, concat_axis=0, tiled=True, axis_index_groups=across
        )

    def swap(parts, bit):
        pairs = [(d, d ^ bit) for d in range(ctx_size)]
        return parts + [lax.ppermute(part, "ctx", pairs) for part in parts]

    bits = [members >> n for n in range(1, members.bit_length())]
    offsets = [0]
    for bit in bits:
        offsets = offsets + [offset ^ bit for offset in offsets]

    def send_query(packed):
        return lax.all_to_all(
            packed.reshape(ctx_size, cap, HD), "ctx", split_axis=0, concat_axis=0, tiled=True
        )

    both = [(0, 1), (1, 0)]
    key_parts = [send_across(pack_shared(key, True))]
    value_packed, key_parts = lax.optimization_barrier((pack_shared(value, False), key_parts))
    key_parts = swap(key_parts, bits[0])
    value_parts = [send_across(value_packed)]
    packed_q = list(pack(q_slots, cosine, sine, query, True, chunks, classes, cap))
    packed_q[0], key_parts, value_parts = lax.optimization_barrier(
        (packed_q[0], key_parts, value_parts)
    )
    got_q = [send_query(packed_q[0])]
    value_parts = swap(value_parts, bits[0])
    for bit in bits[1:]:
        key_parts = swap(key_parts, bit)
    keys = compact(member, kept_count, key_parts, offsets, total, True)
    if chunks > 1:
        packed_q[1], value_parts, keys = lax.optimization_barrier((packed_q[1], value_parts, keys))
    for bit in bits[1:]:
        value_parts = swap(value_parts, bit)
    if chunks > 1:
        got_q.append(send_query(packed_q[1]))
    values = compact(member, kept_count, value_parts, offsets, total, False)

    got, done = [], None
    for j in range(chunks):
        cls_j = j * classes + (me & (classes - 1))
        if j > 0:
            got_q[j], done = lax.optimization_barrier((got_q[j], done))
            got.append(lax.all_to_all(done, "ctx", split_axis=0, concat_axis=0, tiled=True))
        done = attend(cls_j.reshape(1), kept_count, got_q[j], keys, values, block)
        if j > 1:
            done, got[j - 2] = lax.optimization_barrier((done, got[j - 2]))
        if j + 2 < chunks:
            packed_q[j + 2], done = lax.optimization_barrier((packed_q[j + 2], done))
            got_q.append(send_query(packed_q[j + 2]))
    got.append(lax.all_to_all(done, "ctx", split_axis=0, concat_axis=0, tiled=True))
    if tp_size == 2:
        half = columns // 2
        came = [
            [
                lax.ppermute(
                    project((1 - tp_me) * columns + n * half, [one], out_weight, half, classes),
                    "tp",
                    both,
                )
                for n in range(2)
            ]
            for one in got
        ]
        own = project(tp_me * columns, got, out_weight, columns, classes).astype(jnp.float32)
        rows = own.shape[0] // chunks
        return jnp.concatenate(
            [
                jnp.concatenate(
                    [
                        (own[j * rows : (j + 1) * rows, n * half : (n + 1) * half]
                            + part.astype(jnp.float32)
                        ).astype(
                            jnp.bfloat16
                        )
                        for n, part in enumerate(parts)
                    ],
                    axis=1,
                )
                for j, parts in enumerate(came)
            ],
            axis=0,
        )
    full = project(jnp.int32(0) * tp_me, got, out_weight, columns * tp_size, classes)
    split = jnp.transpose(full.reshape(full.shape[0], tp_size, columns), (1, 0, 2))
    swapped = lax.all_to_all(split, "tp", split_axis=0, concat_axis=0, tiled=True)
    return jnp.sum(swapped.astype(jnp.float32), axis=0).astype(jnp.bfloat16)


def solution(mesh):
    placed = (P("ctx", "tp"), P("ctx", "tp"), P("ctx", "tp"), P("ctx", None), P(), P("tp", None))
    return jax.shard_map(
        local, mesh=mesh, in_specs=placed, out_specs=P("ctx", "tp"), check_vma=False
    )
```

```python
import functools
import math

import jax
import jax.numpy as jnp
from jax import lax
from jax.experimental import pallas as pl
from jax.experimental.pallas import tpu as pltpu
from jax.sharding import PartitionSpec as P

HD = 128
TOK_DEV = 384
TILE = 16
PAD = 288
CHUNKS = 2

rope_base = 1000000.0
masked_score = -1e30
exp2_scale = math.log2(math.e) / math.sqrt(HD)
VMEM_BYTES = 58 * 1024 * 1024


def whole_vmem():
    return pl.BlockSpec(memory_space=pltpu.VMEM)


def whole_smem():
    return pl.BlockSpec(memory_space=pltpu.SMEM)


def params():
    return pltpu.CompilerParams(vmem_limit_bytes=VMEM_BYTES)


def turn(rows, cosine, sine):
    as_float = rows.astype(jnp.float32)
    swapped = pltpu.roll(as_float, HD // 2, 1)
    return (as_float * cosine + swapped * sine).astype(jnp.bfloat16)


def rows_below(start, cls, block):
    whole = lax.div(start, TOK_DEV)
    return whole * block + jnp.clip(start - whole * TOK_DEV - cls * block, 0, block)


def slots_kernel(reach, groups, block, cap, me_ref, count_ref, rank_ref, kv_out, q_out):
    me = me_ref[0]
    rows = rank_ref.shape[1]
    start = jnp.int32(0)
    for s in range(count_ref.shape[0]):
        start = start + jnp.where(s < me, count_ref[s], 0)
    kept = rank_ref[...] < count_ref[me]
    upper = lax.broadcasted_iota(jnp.int32, (rows, rows), 0) <= lax.broadcasted_iota(
        jnp.int32, (rows, rows), 1
    )
    flags = jnp.broadcast_to(kept.astype(jnp.float32), (8, rows)).astype(jnp.bfloat16)
    order = (
        jnp.dot(
            flags, upper.astype(jnp.float32).astype(jnp.bfloat16), preferred_element_type=jnp.float32
        )[:1].astype(jnp.int32)
        - 1
    )
    kv_out[...] = jnp.where(kept, order + (start & (TILE - 1)), -1)
    place = start + order
    first = lax.div(start, TOK_DEV)
    device = first + jnp.zeros_like(place)
    for step in range(1, reach + 1):
        device = device + (place >= (first + step) * TOK_DEV).astype(jnp.int32)
    within = place - device * TOK_DEV
    cls = jnp.zeros_like(place)
    for step in range(1, groups):
        cls = cls + (within >= step * block).astype(jnp.int32)
    low = first * block + jnp.clip(start - first * TOK_DEV - cls * block, 0, block)
    slot = cls * cap + device * block + within - cls * block - low + (low & (TILE - 1))
    q_out[...] = jnp.where(kept, slot, -1)


def find_slots(me, counts, ranks, reach, groups, block, cap):
    shape = jax.ShapeDtypeStruct(ranks.shape, jnp.int32)
    return pl.pallas_call(
        functools.partial(slots_kernel, reach, groups, block, cap),
        in_specs=[whole_smem(), whole_smem(), whole_vmem()],
        out_specs=[whole_vmem()] * 2,
        out_shape=[shape, shape],
        compiler_params=params(),
        cost_estimate=pl.CostEstimate(flops=2**20, bytes_accessed=2**14, transcendentals=0),
    )(me, counts, ranks)


def pack_kernel(turned, classes, cap, width, slot_ref, cos_ref, sin_ref, row_ref, *rest):
    out_refs, hot_ref = rest[:-1], rest[-1]

    @pl.when(pl.program_id(0) == 0)
    def _():
        ids = lax.broadcasted_iota(jnp.int32, hot_ref.shape, 0)
        hot_ref[...] = (ids == slot_ref[...]).astype(jnp.float32).astype(jnp.bfloat16)

    if turned:
        rows = jnp.concatenate(
            [
                turn(row_ref[:, h * HD : (h + 1) * HD], cos_ref[...], sin_ref[...])
                for h in range(width)
            ],
            axis=1,
        )
    else:
        rows = row_ref[...]
    for j, out_ref in enumerate(out_refs):
        for r in range(classes):
            first = (j * classes + r) * cap
            moved = jnp.dot(
                hot_ref[first : first + cap, :], rows, preferred_element_type=jnp.float32
            ).astype(jnp.bfloat16)
            for h in range(width):
                out_ref[h, r] = moved[:, h * HD : (h + 1) * HD]


def pack(slots, cosine, sine, rows, turned, chunks, classes, cap):
    count = rows.shape[0]
    heads = rows.shape[1] // HD
    width = min(2, heads)
    fixed = lambda i: (0, 0)
    total = chunks * classes * cap
    return pl.pallas_call(
        functools.partial(pack_kernel, turned, classes, cap, width),
        grid=(heads // width,),
        in_specs=[
            pl.BlockSpec((1, count), fixed),
            pl.BlockSpec((count, HD), fixed),
            pl.BlockSpec((count, HD), fixed),
            pl.BlockSpec((count, width * HD), lambda i: (0, i)),
        ],
        out_specs=[pl.BlockSpec((width, classes, cap, HD), lambda i: (i, 0, 0, 0))] * chunks,
        out_shape=[jax.ShapeDtypeStruct((heads, classes, cap, HD), jnp.bfloat16)] * chunks,
        scratch_shapes=[pltpu.VMEM((total, count), jnp.bfloat16)],
        compiler_params=params(),
        cost_estimate=pl.CostEstimate(
            flops=2 * heads * total * count * HD, bytes_accessed=count * heads * HD * 4, transcendentals=0
        ),
    )(slots, cosine, sine, rows)


def piece_rows(cap):
    return max(rows for rows in range(TILE, PAD + 1, TILE) if cap % rows == 0)


def merge_pieces(low, high, piece, source, add):
    shift = low & (TILE - 1)
    pieces = jnp.where(high > low, lax.div(high - low + shift + piece - 1, piece), 0)
    first = low - shift

    def one(i, carry):
        at = pl.multiple_of(first + i * piece, TILE)
        add(at, source(pl.multiple_of(i * piece, TILE)))
        return carry

    lax.fori_loop(0, pieces, one, 0)


def compact_kernel(offsets, per, total, as_keys, member_ref, count_ref, *rest):
    parts, out, all_rows, starts = rest[:-3], rest[-3], rest[-2], rest[-1]
    members = len(parts)
    piece = piece_rows(parts[0].shape[1])
    all_rows[...] = jnp.zeros_like(all_rows)
    start = jnp.int32(0)
    for s in range(count_ref.shape[0]):
        starts[s] = start
        start = start + count_ref[s]

    def add(at, rows):
        all_rows[pl.ds(at, piece), :] += rows

    for part, offset in zip(parts, offsets):
        for z in range(per):
            source = z * members + (member_ref[0] ^ offset)
            low = starts[source]
            merge_pieces(
                low,
                low + count_ref[source],
                piece,
                lambda at: part[z, pl.ds(at, piece), :],
                add,
            )
    if as_keys:
        for first in range(0, total, 2 * TOK_DEV):
            out[:, first : first + 2 * TOK_DEV] = jnp.transpose(
                all_rows[first : first + 2 * TOK_DEV, :]
            )
    else:
        out[:, :HD] = all_rows[:total, :]
        out[:, HD:] = jnp.ones((total, HD), jnp.bfloat16)


def compact(member, counts, parts, offsets, total, as_keys):
    per = parts[0].shape[0]
    return pl.pallas_call(
        functools.partial(compact_kernel, offsets, per, total, as_keys),
        in_specs=[whole_smem(), whole_smem()] + [whole_vmem()] * len(parts),
        out_specs=whole_vmem(),
        out_shape=jax.ShapeDtypeStruct(
            (HD, total) if as_keys else (total, 2 * HD), jnp.bfloat16
        ),
        scratch_shapes=[
            pltpu.VMEM((total + PAD, HD), jnp.bfloat16),
            pltpu.SMEM(counts.shape, jnp.int32),
        ],
        compiler_params=params(),
        cost_estimate=pl.CostEstimate(flops=total * HD * 8, bytes_accessed=total * HD * 8, transcendentals=0),
    )(member, counts, *parts)


def attend_kernel(ctx_size, block, cls_ref, count_ref, got_ref, key_ref, value_ref, out_ref,
                  query_all, scores_a, scores_b, top_a, top_b, run_max, run_acc):
    span = 2 * TOK_DEV
    pair = 4 * block
    supers = ctx_size // 4
    steps = supers * (supers + 1)
    cls = cls_ref[0]
    piece = piece_rows(got_ref.shape[1])
    query_all[...] = jnp.zeros_like(query_all)

    def add(at, rows):
        query_all[pl.ds(at, piece), :] += rows

    start = jnp.int32(0)
    for s in range(ctx_size):
        end = start + count_ref[s]
        merge_pieces(
            rows_below(start, cls, block),
            rows_below(end, cls, block),
            piece,
            lambda at: got_ref[s, pl.ds(at, piece), :],
            add,
        )
        start = end

    def row_top(found):
        return jnp.broadcast_to(jnp.max(found, axis=1, keepdims=True), (pair, HD))

    def score(scores, top, i, k):
        rows = query_all[pl.ds(pl.multiple_of(jnp.minimum(i, supers - 1) * pair, TILE), pair), :]
        keys = key_ref[:, pl.ds(pl.multiple_of(k * span, HD), span)]
        found = jnp.dot(rows, keys, preferred_element_type=jnp.float32)
        scores[...] = found
        top[...] = row_top(found)

    def mask(scores, top, first):
        row_ids = lax.broadcasted_iota(jnp.int32, (pair, HD), 0)
        row = row_ids + cls * block - first
        for n in range(1, 4):
            row = row + jnp.where(row_ids >= n * block, TOK_DEV - block, 0)
        col = lax.broadcasted_iota(jnp.int32, (pair, span), 1)
        found = jnp.where(
            col <= jnp.concatenate([row] * (span // HD), axis=1), scores[...], masked_score
        )
        scores[...] = found
        top[...] = row_top(found)

    def absorb(scores, top, k):
        before = run_max[...]
        after = jnp.maximum(before, top[...])
        rescale = jnp.exp2((before - after) * exp2_scale)
        run_max[...] = after
        weights = jnp.exp2(
            (scores[...] - jnp.concatenate([after] * (span // HD), axis=1)) * exp2_scale
        )
        values = value_ref[pl.ds(pl.multiple_of(k * span, TILE), span), :]
        run_acc[...] = run_acc[...] * jnp.concatenate([rescale, rescale], axis=1) + jnp.dot(
            weights.astype(jnp.bfloat16), values, preferred_element_type=jnp.float32
        )

    def clear():
        run_max[...] = jnp.full_like(run_max, masked_score)
        run_acc[...] = jnp.zeros_like(run_acc)

    def one_step(now, later, i, k):
        last = k == 2 * i + 1
        next_i = jnp.where(last, i + 1, i)
        next_k = jnp.where(last, 0, k + 1)
        score(*later, next_i, next_k)
        absorb(*now, k)

        @pl.when(last)
        def _():
            result = (run_acc[:, :HD] / run_acc[:, HD:]).astype(jnp.bfloat16)
            for n in range(4):
                out_ref[4 * i + n] = result[n * block : (n + 1) * block]
            clear()

        @pl.when(next_k >= 2 * next_i)
        def _():
            mask(*later, (next_k - 2 * next_i) * span)

        return next_i, next_k

    buffers_a, buffers_b = (scores_a, top_a), (scores_b, top_b)
    clear()
    score(*buffers_a, 0, 0)
    mask(*buffers_a, 0)

    def two_steps(t, at):
        at = one_step(buffers_a, buffers_b, *at)
        return one_step(buffers_b, buffers_a, *at)

    lax.fori_loop(0, steps // 2, two_steps, (jnp.int32(0), jnp.int32(0)))


def attend(cls, counts, got, keys, values, block):
    ctx_size = got.shape[0]
    total = values.shape[0]
    pairs = total * ctx_size * block // 2
    return pl.pallas_call(
        functools.partial(attend_kernel, ctx_size, block),
        in_specs=[whole_smem()] * 2 + [whole_vmem()] * 3,
        out_specs=whole_vmem(),
        out_shape=jax.ShapeDtypeStruct((ctx_size, block, HD), jnp.bfloat16),
        scratch_shapes=[
            pltpu.VMEM((ctx_size * block + PAD, HD), jnp.bfloat16),
            pltpu.VMEM((4 * block, 2 * TOK_DEV), jnp.float32),
            pltpu.VMEM((4 * block, 2 * TOK_DEV), jnp.float32),
            pltpu.VMEM((4 * block, HD), jnp.float32),
            pltpu.VMEM((4 * block, HD), jnp.float32),
            pltpu.VMEM((4 * block, HD), jnp.float32),
            pltpu.VMEM((4 * block, 2 * HD), jnp.float32),
        ],
        compiler_params=params(),
        cost_estimate=pl.CostEstimate(
            flops=pairs * 8 * HD, bytes_accessed=total * HD * 8, transcendentals=pairs
        ),
    )(cls, counts, got, keys, values)


def project_kernel(classes, chunks, column_ref, *rest):
    got_refs, (weight_ref, out_ref, rows_ref) = rest[:chunks], rest[chunks:]
    block = got_refs[0].shape[1]

    @pl.when(pl.program_id(0) == 0)
    def _():
        for j, got_ref in enumerate(got_refs):
            for d in range(got_ref.shape[0]):
                h, r = d // classes, d % classes
                first = (j * classes + r) * block
                rows_ref[first : first + block, h * HD : (h + 1) * HD] = got_ref[d]

    out_ref[...] = jnp.dot(
        rows_ref[...], weight_ref[...], preferred_element_type=jnp.float32
    ).astype(jnp.bfloat16)


def project(first_column, got, weight, columns, classes):
    ctx_size, block, _ = got[0].shape
    rows, depth = len(got) * classes * block, weight.shape[0]
    step = min(512, columns)
    return pl.pallas_call(
        functools.partial(project_kernel, classes, len(got)),
        grid_spec=pltpu.PrefetchScalarGridSpec(
            num_scalar_prefetch=1,
            grid=(columns // step,),
            in_specs=[pl.BlockSpec((ctx_size, block, HD), lambda i, first: (0, 0, 0))] * len(got)
            + [pl.BlockSpec((depth, step), lambda i, first: (0, first[0] + i))],
            out_specs=pl.BlockSpec((rows, step), lambda i, first: (0, i)),
            scratch_shapes=[pltpu.VMEM((rows, depth), jnp.bfloat16)],
        ),
        out_shape=jax.ShapeDtypeStruct((rows, columns), jnp.bfloat16),
        compiler_params=params(),
        cost_estimate=pl.CostEstimate(
            flops=2 * rows * depth * columns, bytes_accessed=2 * depth * columns, transcendentals=0
        ),
    )((first_column // step).astype(jnp.int32).reshape(1), *got, weight)


def add_piece_kernel(sum_ref, part_ref, out_ref):
    out_ref[...] = (
        sum_ref[...].astype(jnp.float32) + part_ref[...].astype(jnp.float32)
    ).astype(jnp.bfloat16)


def add_piece(total_sum, part, j, n):
    rows, width = part.shape
    step = min(1024, width)
    steps = width // step
    here = pl.BlockSpec((rows, step), lambda i: (j, n * steps + i))
    return pl.pallas_call(
        add_piece_kernel,
        grid=(steps,),
        in_specs=[here, pl.BlockSpec((rows, step), lambda i: (0, i))],
        out_specs=here,
        out_shape=jax.ShapeDtypeStruct(total_sum.shape, total_sum.dtype),
        input_output_aliases={0: 0},
        compiler_params=params(),
        cost_estimate=pl.CostEstimate(
            flops=rows * width, bytes_accessed=6 * rows * width, transcendentals=0
        ),
    )(total_sum, part)


def tables(query_rows):
    half_dim = HD // 2
    positions = lax.axis_index("ctx") * query_rows + jnp.arange(query_rows, dtype=jnp.int32)
    lane = jnp.arange(HD, dtype=jnp.int32)
    pair_id = jnp.where(lane < half_dim, lane, lane - half_dim)
    inv_freq = rope_base ** (-(pair_id.astype(jnp.float32) * 2.0 / HD))
    angles = positions.astype(jnp.float32)[:, None] * inv_freq[None, :]
    sine = jnp.sin(angles)
    return jnp.cos(angles), jnp.where(lane[None, :] < half_dim, -sine, sine)


def local(query, key, value, keep_rank, kept_count, out_weight):
    ctx_size = lax.axis_size("ctx")
    tp_size = lax.axis_size("tp")
    me = lax.axis_index("ctx")
    tp_me = lax.axis_index("tp")
    orig_rows = query.shape[0]
    heads = query.shape[1] // HD
    kv_heads = key.shape[1] // HD
    members = ctx_size // kv_heads
    classes = ctx_size // heads
    chunks = CHUNKS if classes == 1 else 1
    block = TOK_DEV // (chunks * classes)
    total = ctx_size * TOK_DEV
    reach = orig_rows // TOK_DEV
    cap = reach * block + TILE
    cap_kv = orig_rows + TILE
    columns = out_weight.shape[1] // tp_size

    kv_slots, q_slots = find_slots(
        me.reshape(1), kept_count, keep_rank, reach, chunks * classes, block, cap
    )
    cosine, sine = tables(orig_rows)

    across = [[z * members + m for z in range(kv_heads)] for m in range(members)]

    member = (me & (members - 1)).reshape(1)

    def pack_shared(rows, turned):
        (packed,) = pack(kv_slots, cosine, sine, rows, turned, 1, 1, cap_kv)
        return packed.reshape(kv_heads, cap_kv, HD)

    def send_across(packed):
        if kv_heads == 1:
            return packed
        return lax.all_to_all(
            packed, "ctx", split_axis=0, concat_axis=0, tiled=True, axis_index_groups=across
        )

    def swap(parts, bit):
        pairs = [(d, d ^ bit) for d in range(ctx_size)]
        return parts + [lax.ppermute(part, "ctx", pairs) for part in parts]

    bits = [members >> n for n in range(1, members.bit_length())]
    offsets = [0]
    for bit in bits:
        offsets = offsets + [offset ^ bit for offset in offsets]

    def send_query(packed):
        return lax.all_to_all(
            packed.reshape(ctx_size, cap, HD), "ctx", split_axis=0, concat_axis=0, tiled=True
        )

    both = [(0, 1), (1, 0)]
    key_parts = [send_across(pack_shared(key, True))]
    value_packed, key_parts = lax.optimization_barrier((pack_shared(value, False), key_parts))
    key_parts = swap(key_parts, bits[0])
    value_parts = [send_across(value_packed)]
    packed_q = list(pack(q_slots, cosine, sine, query, True, chunks, classes, cap))
    packed_q[0], key_parts, value_parts = lax.optimization_barrier(
        (packed_q[0], key_parts, value_parts)
    )
    got_q = [send_query(packed_q[0])]
    value_parts = swap(value_parts, bits[0])
    for bit in bits[1:]:
        key_parts = swap(key_parts, bit)
    keys = compact(member, kept_count, key_parts, offsets, total, True)
    if chunks > 1:
        packed_q[1], value_parts, keys = lax.optimization_barrier((packed_q[1], value_parts, keys))
    for bit in bits[1:]:
        value_parts = swap(value_parts, bit)
    if chunks > 1:
        got_q.append(send_query(packed_q[1]))
    values = compact(member, kept_count, value_parts, offsets, total, False)

    got, done = [], None
    for j in range(chunks):
        cls_j = j * classes + (me & (classes - 1))
        if j > 0:
            got_q[j], done = lax.optimization_barrier((got_q[j], done))
            got.append(lax.all_to_all(done, "ctx", split_axis=0, concat_axis=0, tiled=True))
        done = attend(cls_j.reshape(1), kept_count, got_q[j], keys, values, block)
        if j > 1:
            done, got[j - 2] = lax.optimization_barrier((done, got[j - 2]))
        if j + 2 < chunks:
            packed_q[j + 2], done = lax.optimization_barrier((packed_q[j + 2], done))
            got_q.append(send_query(packed_q[j + 2]))
    half = columns // 2

    def for_peer(one):
        return [
            project((1 - tp_me) * columns + n * half, [one], out_weight, half, classes)
            for n in range(2)
        ]

    def trade(parts):
        return [lax.ppermute(part, "tp", [(0, 1), (1, 0)]) for part in parts]

    paired = tp_size == 2 and chunks == 2
    if paired:
        first = for_peer(got[0])
        done, first[0] = lax.optimization_barrier((done, first[0]))
    last = lax.all_to_all(done, "ctx", split_axis=0, concat_axis=0, tiled=True)
    if paired:
        last, first[1] = lax.optimization_barrier((last, first[1]))
        came = [trade(first), trade(for_peer(last))]
        total_sum = project(tp_me * columns, got + [last], out_weight, columns, classes)
        for j, parts in enumerate(came):
            for n, part in enumerate(parts):
                total_sum = add_piece(total_sum, part, j, n)
        return total_sum
    got.append(last)
    full = project(jnp.int32(0) * tp_me, got, out_weight, columns * tp_size, classes)
    split = jnp.transpose(full.reshape(full.shape[0], tp_size, columns), (1, 0, 2))
    swapped = lax.all_to_all(split, "tp", split_axis=0, concat_axis=0, tiled=True)
    return jnp.sum(swapped.astype(jnp.float32), axis=0).astype(jnp.bfloat16)


def solution(mesh):
    placed = (P("ctx", "tp"), P("ctx", "tp"), P("ctx", "tp"), P("ctx", None), P(), P("tp", None))
    return jax.shard_map(
        local, mesh=mesh, in_specs=placed, out_specs=P("ctx", "tp"), check_vma=False
    )
```

```python
import functools
import math

import jax
import jax.numpy as jnp
from jax import lax
from jax.experimental import pallas as pl
from jax.experimental.pallas import tpu as pltpu
from jax.sharding import PartitionSpec as P

HD = 128
TOK_DEV = 384
TILE = 16
PAD = 288
CHUNKS = 2

rope_base = 1000000.0
masked_score = -1e30
exp2_scale = math.log2(math.e) / math.sqrt(HD)
VMEM_BYTES = 58 * 1024 * 1024


def whole_vmem():
    return pl.BlockSpec(memory_space=pltpu.VMEM)


def whole_smem():
    return pl.BlockSpec(memory_space=pltpu.SMEM)


def params():
    return pltpu.CompilerParams(vmem_limit_bytes=VMEM_BYTES)


def turn(rows, cosine, sine):
    as_float = rows.astype(jnp.float32)
    swapped = pltpu.roll(as_float, HD // 2, 1)
    return (as_float * cosine + swapped * sine).astype(jnp.bfloat16)


def rows_below(start, cls, block):
    whole = lax.div(start, TOK_DEV)
    return whole * block + jnp.clip(start - whole * TOK_DEV - cls * block, 0, block)


def slots_kernel(reach, groups, block, cap, me_ref, count_ref, rank_ref, kv_out, q_out):
    me = me_ref[0]
    rows = rank_ref.shape[1]
    start = jnp.int32(0)
    for s in range(count_ref.shape[0]):
        start = start + jnp.where(s < me, count_ref[s], 0)
    kept = rank_ref[...] < count_ref[me]
    upper = lax.broadcasted_iota(jnp.int32, (rows, rows), 0) <= lax.broadcasted_iota(
        jnp.int32, (rows, rows), 1
    )
    flags = jnp.broadcast_to(kept.astype(jnp.float32), (8, rows)).astype(jnp.bfloat16)
    order = (
        jnp.dot(
            flags, upper.astype(jnp.float32).astype(jnp.bfloat16), preferred_element_type=jnp.float32
        )[:1].astype(jnp.int32)
        - 1
    )
    kv_out[...] = jnp.where(kept, order + (start & (TILE - 1)), -1)
    place = start + order
    first = lax.div(start, TOK_DEV)
    device = first + jnp.zeros_like(place)
    for step in range(1, reach + 1):
        device = device + (place >= (first + step) * TOK_DEV).astype(jnp.int32)
    within = place - device * TOK_DEV
    cls = jnp.zeros_like(place)
    for step in range(1, groups):
        cls = cls + (within >= step * block).astype(jnp.int32)
    low = first * block + jnp.clip(start - first * TOK_DEV - cls * block, 0, block)
    slot = cls * cap + device * block + within - cls * block - low + (low & (TILE - 1))
    q_out[...] = jnp.where(kept, slot, -1)


def find_slots(me, counts, ranks, reach, groups, block, cap):
    shape = jax.ShapeDtypeStruct(ranks.shape, jnp.int32)
    return pl.pallas_call(
        functools.partial(slots_kernel, reach, groups, block, cap),
        in_specs=[whole_smem(), whole_smem(), whole_vmem()],
        out_specs=[whole_vmem()] * 2,
        out_shape=[shape, shape],
        compiler_params=params(),
        cost_estimate=pl.CostEstimate(flops=2**20, bytes_accessed=2**14, transcendentals=0),
    )(me, counts, ranks)


def pack_kernel(turned, classes, cap, width, slot_ref, cos_ref, sin_ref, row_ref, *rest):
    out_refs, hot_ref = rest[:-1], rest[-1]

    @pl.when(pl.program_id(0) == 0)
    def _():
        ids = lax.broadcasted_iota(jnp.int32, hot_ref.shape, 0)
        hot_ref[...] = (ids == slot_ref[...]).astype(jnp.float32).astype(jnp.bfloat16)

    if turned:
        rows = jnp.concatenate(
            [
                turn(row_ref[:, h * HD : (h + 1) * HD], cos_ref[...], sin_ref[...])
                for h in range(width)
            ],
            axis=1,
        )
    else:
        rows = row_ref[...]
    for j, out_ref in enumerate(out_refs):
        for r in range(classes):
            first = (j * classes + r) * cap
            moved = jnp.dot(
                hot_ref[first : first + cap, :], rows, preferred_element_type=jnp.float32
            ).astype(jnp.bfloat16)
            for h in range(width):
                out_ref[h, r] = moved[:, h * HD : (h + 1) * HD]


def pack(slots, cosine, sine, rows, turned, chunks, classes, cap):
    count = rows.shape[0]
    heads = rows.shape[1] // HD
    width = min(2, heads)
    fixed = lambda i: (0, 0)
    total = chunks * classes * cap
    return pl.pallas_call(
        functools.partial(pack_kernel, turned, classes, cap, width),
        grid=(heads // width,),
        in_specs=[
            pl.BlockSpec((1, count), fixed),
            pl.BlockSpec((count, HD), fixed),
            pl.BlockSpec((count, HD), fixed),
            pl.BlockSpec((count, width * HD), lambda i: (0, i)),
        ],
        out_specs=[pl.BlockSpec((width, classes, cap, HD), lambda i: (i, 0, 0, 0))] * chunks,
        out_shape=[jax.ShapeDtypeStruct((heads, classes, cap, HD), jnp.bfloat16)] * chunks,
        scratch_shapes=[pltpu.VMEM((total, count), jnp.bfloat16)],
        compiler_params=params(),
        cost_estimate=pl.CostEstimate(
            flops=2 * heads * total * count * HD, bytes_accessed=count * heads * HD * 4, transcendentals=0
        ),
    )(slots, cosine, sine, rows)


def piece_rows(cap):
    return max(rows for rows in range(TILE, PAD + 1, TILE) if cap % rows == 0)


def merge_pieces(low, high, piece, source, add):
    shift = low & (TILE - 1)
    pieces = jnp.where(high > low, lax.div(high - low + shift + piece - 1, piece), 0)
    first = low - shift

    def one(i, carry):
        at = pl.multiple_of(first + i * piece, TILE)
        add(at, source(pl.multiple_of(i * piece, TILE)))
        return carry

    lax.fori_loop(0, pieces, one, 0)


def compact_kernel(offsets, per, total, as_keys, member_ref, count_ref, *rest):
    parts, out, all_rows, starts = rest[:-3], rest[-3], rest[-2], rest[-1]
    members = len(parts)
    piece = piece_rows(parts[0].shape[1])
    all_rows[...] = jnp.zeros_like(all_rows)
    start = jnp.int32(0)
    for s in range(count_ref.shape[0]):
        starts[s] = start
        start = start + count_ref[s]

    def add(at, rows):
        all_rows[pl.ds(at, piece), :] += rows

    for part, offset in zip(parts, offsets):
        for z in range(per):
            source = z * members + (member_ref[0] ^ offset)
            low = starts[source]
            merge_pieces(
                low,
                low + count_ref[source],
                piece,
                lambda at: part[z, pl.ds(at, piece), :],
                add,
            )
    if as_keys:
        for first in range(0, total, 2 * TOK_DEV):
            out[:, first : first + 2 * TOK_DEV] = jnp.transpose(
                all_rows[first : first + 2 * TOK_DEV, :]
            )
    else:
        out[:, :HD] = all_rows[:total, :]
        out[:, HD:] = jnp.ones((total, HD), jnp.bfloat16)


def compact(member, counts, parts, offsets, total, as_keys):
    per = parts[0].shape[0]
    return pl.pallas_call(
        functools.partial(compact_kernel, offsets, per, total, as_keys),
        in_specs=[whole_smem(), whole_smem()] + [whole_vmem()] * len(parts),
        out_specs=whole_vmem(),
        out_shape=jax.ShapeDtypeStruct(
            (HD, total) if as_keys else (total, 2 * HD), jnp.bfloat16
        ),
        scratch_shapes=[
            pltpu.VMEM((total + PAD, HD), jnp.bfloat16),
            pltpu.SMEM(counts.shape, jnp.int32),
        ],
        compiler_params=params(),
        cost_estimate=pl.CostEstimate(flops=total * HD * 8, bytes_accessed=total * HD * 8, transcendentals=0),
    )(member, counts, *parts)


def attend_kernel(ctx_size, block, cls_ref, count_ref, got_ref, key_ref, value_ref, out_ref,
                  query_all, scores_a, scores_b, top_a, top_b, run_max, run_acc):
    span = 2 * TOK_DEV
    pair = 4 * block
    supers = ctx_size // 4
    steps = supers * (supers + 1)
    cls = cls_ref[0]
    piece = piece_rows(got_ref.shape[1])
    query_all[...] = jnp.zeros_like(query_all)

    def add(at, rows):
        query_all[pl.ds(at, piece), :] += rows

    start = jnp.int32(0)
    for s in range(ctx_size):
        end = start + count_ref[s]
        merge_pieces(
            rows_below(start, cls, block),
            rows_below(end, cls, block),
            piece,
            lambda at: got_ref[s, pl.ds(at, piece), :],
            add,
        )
        start = end

    upper = 2 * block
    keep_all, lower = slice(0, pair), slice(upper, pair)

    def row_top(found):
        return jnp.broadcast_to(jnp.max(found, axis=1, keepdims=True), (found.shape[0], HD))

    def allowed(first_row, count, first_key):
        ids = lax.broadcasted_iota(jnp.int32, (count, HD), 0) + first_row
        row = ids + cls * block - first_key
        for n in range(1, 4):
            row = row + jnp.where(ids >= n * block, TOK_DEV - block, 0)
        col = lax.broadcasted_iota(jnp.int32, (count, span), 1)
        return col <= jnp.concatenate([row] * (span // HD), axis=1)

    def put(scores, top, part, found):
        scores[part, :] = found
        top[part, :] = row_top(found)

    def dot_keys(i, k, first_row, count):
        at = jnp.minimum(i, supers - 1) * pair + first_row
        rows = query_all[pl.ds(pl.multiple_of(at, TILE), count), :]
        keys = key_ref[:, pl.ds(pl.multiple_of(k * span, HD), span)]
        return jnp.dot(rows, keys, preferred_element_type=jnp.float32)

    def score(scores, top, i, k):
        put(scores, top, keep_all, dot_keys(i, k, 0, pair))

    def score_lower(scores, top, i, k):
        found = dot_keys(i, k, upper, pair - upper)
        found = jnp.where(allowed(upper, pair - upper, span), found, masked_score)
        put(scores, top, lower, found)

    def mask_upper(scores, top):
        found = jnp.where(allowed(0, upper, 0), scores[:upper, :], masked_score)
        put(scores, top, slice(0, upper), found)

    def absorb(scores, top, k, part):
        before = run_max[part, :]
        after = jnp.maximum(before, top[part, :])
        rescale = jnp.exp2((before - after) * exp2_scale)
        run_max[part, :] = after
        weights = jnp.exp2(
            (scores[part, :] - jnp.concatenate([after] * (span // HD), axis=1)) * exp2_scale
        )
        values = value_ref[pl.ds(pl.multiple_of(k * span, TILE), span), :]
        run_acc[part, :] = run_acc[part, :] * jnp.concatenate([rescale, rescale], axis=1) + jnp.dot(
            weights.astype(jnp.bfloat16), values, preferred_element_type=jnp.float32
        )

    def clear():
        run_max[...] = jnp.full_like(run_max, masked_score)
        run_acc[...] = jnp.zeros_like(run_acc)

    buffers_a, buffers_b = (scores_a, top_a), (scores_b, top_b)
    clear()
    score(*buffers_a, 0, 0)
    mask_upper(*buffers_a)

    def two_steps(t, at):
        i, k = at
        last = k == 2 * i

        @pl.when(last)
        def _():
            score_lower(*buffers_b, i, k + 1)
            absorb(*buffers_a, k, keep_all)
            score(*buffers_a, i + 1, 0)
            absorb(*buffers_b, k + 1, lower)
            result = (run_acc[:, :HD] / run_acc[:, HD:]).astype(jnp.bfloat16)
            for n in range(4):
                out_ref[4 * i + n] = result[n * block : (n + 1) * block]
            clear()

        @pl.when(jnp.logical_not(last))
        def _():
            score(*buffers_b, i, k + 1)
            absorb(*buffers_a, k, keep_all)
            score(*buffers_a, i, k + 2)
            absorb(*buffers_b, k + 1, keep_all)

            @pl.when(k + 2 == 2 * i)
            def _():
                mask_upper(*buffers_a)

        return jnp.where(last, i + 1, i), jnp.where(last, 0, k + 2)

    lax.fori_loop(0, steps // 2, two_steps, (jnp.int32(0), jnp.int32(0)))


def attend(cls, counts, got, keys, values, block):
    ctx_size = got.shape[0]
    total = values.shape[0]
    pairs = total * ctx_size * block // 2
    return pl.pallas_call(
        functools.partial(attend_kernel, ctx_size, block),
        in_specs=[whole_smem()] * 2 + [whole_vmem()] * 3,
        out_specs=whole_vmem(),
        out_shape=jax.ShapeDtypeStruct((ctx_size, block, HD), jnp.bfloat16),
        scratch_shapes=[
            pltpu.VMEM((ctx_size * block + PAD, HD), jnp.bfloat16),
            pltpu.VMEM((4 * block, 2 * TOK_DEV), jnp.float32),
            pltpu.VMEM((4 * block, 2 * TOK_DEV), jnp.float32),
            pltpu.VMEM((4 * block, HD), jnp.float32),
            pltpu.VMEM((4 * block, HD), jnp.float32),
            pltpu.VMEM((4 * block, HD), jnp.float32),
            pltpu.VMEM((4 * block, 2 * HD), jnp.float32),
        ],
        compiler_params=params(),
        cost_estimate=pl.CostEstimate(
            flops=pairs * 8 * HD, bytes_accessed=total * HD * 8, transcendentals=pairs
        ),
    )(cls, counts, got, keys, values)


def project_kernel(classes, chunks, column_ref, *rest):
    got_refs, (weight_ref, out_ref, rows_ref) = rest[:chunks], rest[chunks:]
    block = got_refs[0].shape[1]

    @pl.when(pl.program_id(0) == 0)
    def _():
        for j, got_ref in enumerate(got_refs):
            for d in range(got_ref.shape[0]):
                h, r = d // classes, d % classes
                first = (j * classes + r) * block
                rows_ref[first : first + block, h * HD : (h + 1) * HD] = got_ref[d]

    out_ref[...] = jnp.dot(
        rows_ref[...], weight_ref[...], preferred_element_type=jnp.float32
    ).astype(jnp.bfloat16)


def project(first_column, got, weight, columns, classes):
    ctx_size, block, _ = got[0].shape
    rows, depth = len(got) * classes * block, weight.shape[0]
    step = min(512, columns)
    return pl.pallas_call(
        functools.partial(project_kernel, classes, len(got)),
        grid_spec=pltpu.PrefetchScalarGridSpec(
            num_scalar_prefetch=1,
            grid=(columns // step,),
            in_specs=[pl.BlockSpec((ctx_size, block, HD), lambda i, first: (0, 0, 0))] * len(got)
            + [pl.BlockSpec((depth, step), lambda i, first: (0, first[0] + i))],
            out_specs=pl.BlockSpec((rows, step), lambda i, first: (0, i)),
            scratch_shapes=[pltpu.VMEM((rows, depth), jnp.bfloat16)],
        ),
        out_shape=jax.ShapeDtypeStruct((rows, columns), jnp.bfloat16),
        compiler_params=params(),
        cost_estimate=pl.CostEstimate(
            flops=2 * rows * depth * columns, bytes_accessed=2 * depth * columns, transcendentals=0
        ),
    )((first_column // step).astype(jnp.int32).reshape(1), *got, weight)


def add_piece_kernel(sum_ref, part_ref, out_ref):
    out_ref[...] = (
        sum_ref[...].astype(jnp.float32) + part_ref[...].astype(jnp.float32)
    ).astype(jnp.bfloat16)


def add_piece(total_sum, part, j, n):
    rows, width = part.shape
    step = min(1024, width)
    steps = width // step
    here = pl.BlockSpec((rows, step), lambda i: (j, n * steps + i))
    return pl.pallas_call(
        add_piece_kernel,
        grid=(steps,),
        in_specs=[here, pl.BlockSpec((rows, step), lambda i: (0, i))],
        out_specs=here,
        out_shape=jax.ShapeDtypeStruct(total_sum.shape, total_sum.dtype),
        input_output_aliases={0: 0},
        compiler_params=params(),
        cost_estimate=pl.CostEstimate(
            flops=rows * width, bytes_accessed=6 * rows * width, transcendentals=0
        ),
    )(total_sum, part)


def tables(query_rows):
    half_dim = HD // 2
    positions = lax.axis_index("ctx") * query_rows + jnp.arange(query_rows, dtype=jnp.int32)
    lane = jnp.arange(HD, dtype=jnp.int32)
    pair_id = jnp.where(lane < half_dim, lane, lane - half_dim)
    inv_freq = rope_base ** (-(pair_id.astype(jnp.float32) * 2.0 / HD))
    angles = positions.astype(jnp.float32)[:, None] * inv_freq[None, :]
    sine = jnp.sin(angles)
    return jnp.cos(angles), jnp.where(lane[None, :] < half_dim, -sine, sine)


def local(query, key, value, keep_rank, kept_count, out_weight):
    ctx_size = lax.axis_size("ctx")
    tp_size = lax.axis_size("tp")
    me = lax.axis_index("ctx")
    tp_me = lax.axis_index("tp")
    orig_rows = query.shape[0]
    heads = query.shape[1] // HD
    kv_heads = key.shape[1] // HD
    members = ctx_size // kv_heads
    classes = ctx_size // heads
    chunks = CHUNKS if classes == 1 else 1
    block = TOK_DEV // (chunks * classes)
    total = ctx_size * TOK_DEV
    reach = orig_rows // TOK_DEV
    cap = reach * block + TILE
    cap_kv = orig_rows + TILE
    columns = out_weight.shape[1] // tp_size

    kv_slots, q_slots = find_slots(
        me.reshape(1), kept_count, keep_rank, reach, chunks * classes, block, cap
    )
    cosine, sine = tables(orig_rows)

    across = [[z * members + m for z in range(kv_heads)] for m in range(members)]

    member = (me & (members - 1)).reshape(1)

    def pack_shared(rows, turned):
        (packed,) = pack(kv_slots, cosine, sine, rows, turned, 1, 1, cap_kv)
        return packed.reshape(kv_heads, cap_kv, HD)

    def send_across(packed):
        if kv_heads == 1:
            return packed
        return lax.all_to_all(
            packed, "ctx", split_axis=0, concat_axis=0, tiled=True, axis_index_groups=across
        )

    def swap(parts, bit):
        pairs = [(d, d ^ bit) for d in range(ctx_size)]
        return parts + [lax.ppermute(part, "ctx", pairs) for part in parts]

    bits = [members >> n for n in range(1, members.bit_length())]
    offsets = [0]
    for bit in bits:
        offsets = offsets + [offset ^ bit for offset in offsets]

    def send_query(packed):
        return lax.all_to_all(
            packed.reshape(ctx_size, cap, HD), "ctx", split_axis=0, concat_axis=0, tiled=True
        )

    both = [(0, 1), (1, 0)]
    key_parts = [send_across(pack_shared(key, True))]
    value_packed, key_parts = lax.optimization_barrier((pack_shared(value, False), key_parts))
    key_parts = swap(key_parts, bits[0])
    value_parts = [send_across(value_packed)]
    packed_q = list(pack(q_slots, cosine, sine, query, True, chunks, classes, cap))
    packed_q[0], key_parts, value_parts = lax.optimization_barrier(
        (packed_q[0], key_parts, value_parts)
    )
    got_q = [send_query(packed_q[0])]
    value_parts = swap(value_parts, bits[0])
    for bit in bits[1:]:
        key_parts = swap(key_parts, bit)
    keys = compact(member, kept_count, key_parts, offsets, total, True)
    if chunks > 1:
        packed_q[1], value_parts, keys = lax.optimization_barrier((packed_q[1], value_parts, keys))
    for bit in bits[1:]:
        value_parts = swap(value_parts, bit)
    if chunks > 1:
        got_q.append(send_query(packed_q[1]))
    values = compact(member, kept_count, value_parts, offsets, total, False)

    got, done = [], None
    for j in range(chunks):
        cls_j = j * classes + (me & (classes - 1))
        if j > 0:
            got_q[j], done = lax.optimization_barrier((got_q[j], done))
            got.append(lax.all_to_all(done, "ctx", split_axis=0, concat_axis=0, tiled=True))
        done = attend(cls_j.reshape(1), kept_count, got_q[j], keys, values, block)
        if j > 1:
            done, got[j - 2] = lax.optimization_barrier((done, got[j - 2]))
        if j + 2 < chunks:
            packed_q[j + 2], done = lax.optimization_barrier((packed_q[j + 2], done))
            got_q.append(send_query(packed_q[j + 2]))
    half = columns // 2

    def for_peer(one):
        return [
            project((1 - tp_me) * columns + n * half, [one], out_weight, half, classes)
            for n in range(2)
        ]

    def trade(parts):
        return [lax.ppermute(part, "tp", [(0, 1), (1, 0)]) for part in parts]

    paired = tp_size == 2 and chunks == 2
    if paired:
        first = for_peer(got[0])
        done, first[0] = lax.optimization_barrier((done, first[0]))
    last = lax.all_to_all(done, "ctx", split_axis=0, concat_axis=0, tiled=True)
    if paired:
        last, first[1] = lax.optimization_barrier((last, first[1]))
        came = [trade(first), trade(for_peer(last))]
        total_sum = project(tp_me * columns, got + [last], out_weight, columns, classes)
        for j, parts in enumerate(came):
            for n, part in enumerate(parts):
                total_sum = add_piece(total_sum, part, j, n)
        return total_sum
    got.append(last)
    full = project(jnp.int32(0) * tp_me, got, out_weight, columns * tp_size, classes)
    split = jnp.transpose(full.reshape(full.shape[0], tp_size, columns), (1, 0, 2))
    swapped = lax.all_to_all(split, "tp", split_axis=0, concat_axis=0, tiled=True)
    return jnp.sum(swapped.astype(jnp.float32), axis=0).astype(jnp.bfloat16)


def solution(mesh):
    placed = (P("ctx", "tp"), P("ctx", "tp"), P("ctx", "tp"), P("ctx", None), P(), P("tp", None))
    return jax.shard_map(
        local, mesh=mesh, in_specs=placed, out_specs=P("ctx", "tp"), check_vma=False
    )
```

```python
import functools
import math

import jax
import jax.numpy as jnp
from jax import lax
from jax.experimental import pallas as pl
from jax.experimental.pallas import tpu as pltpu
from jax.sharding import PartitionSpec as P

HD = 128
TOK_DEV = 384
TILE = 16
PAD = 288
CHUNKS = 2

rope_base = 1000000.0
masked_score = -1e30
exp2_scale = math.log2(math.e) / math.sqrt(HD)
VMEM_BYTES = 58 * 1024 * 1024


def whole_vmem():
    return pl.BlockSpec(memory_space=pltpu.VMEM)


def whole_smem():
    return pl.BlockSpec(memory_space=pltpu.SMEM)


def params():
    return pltpu.CompilerParams(vmem_limit_bytes=VMEM_BYTES)


def turn(rows, cosine, sine):
    as_float = rows.astype(jnp.float32)
    swapped = pltpu.roll(as_float, HD // 2, 1)
    return (as_float * cosine + swapped * sine).astype(jnp.bfloat16)


def rows_below(start, cls, block):
    whole = lax.div(start, TOK_DEV)
    return whole * block + jnp.clip(start - whole * TOK_DEV - cls * block, 0, block)


def slots_kernel(reach, groups, block, cap, me_ref, count_ref, rank_ref, kv_out, q_out):
    me = me_ref[0]
    rows = rank_ref.shape[1]
    start = jnp.int32(0)
    for s in range(count_ref.shape[0]):
        start = start + jnp.where(s < me, count_ref[s], 0)
    kept = rank_ref[...] < count_ref[me]
    upper = lax.broadcasted_iota(jnp.int32, (rows, rows), 0) <= lax.broadcasted_iota(
        jnp.int32, (rows, rows), 1
    )
    flags = jnp.broadcast_to(kept.astype(jnp.float32), (8, rows)).astype(jnp.bfloat16)
    order = (
        jnp.dot(
            flags, upper.astype(jnp.float32).astype(jnp.bfloat16), preferred_element_type=jnp.float32
        )[:1].astype(jnp.int32)
        - 1
    )
    kv_out[...] = jnp.where(kept, order + (start & (TILE - 1)), -1)
    place = start + order
    first = lax.div(start, TOK_DEV)
    device = first + jnp.zeros_like(place)
    for step in range(1, reach + 1):
        device = device + (place >= (first + step) * TOK_DEV).astype(jnp.int32)
    within = place - device * TOK_DEV
    cls = jnp.zeros_like(place)
    for step in range(1, groups):
        cls = cls + (within >= step * block).astype(jnp.int32)
    low = first * block + jnp.clip(start - first * TOK_DEV - cls * block, 0, block)
    slot = cls * cap + device * block + within - cls * block - low + (low & (TILE - 1))
    q_out[...] = jnp.where(kept, slot, -1)


def find_slots(me, counts, ranks, reach, groups, block, cap):
    shape = jax.ShapeDtypeStruct(ranks.shape, jnp.int32)
    return pl.pallas_call(
        functools.partial(slots_kernel, reach, groups, block, cap),
        in_specs=[whole_smem(), whole_smem(), whole_vmem()],
        out_specs=[whole_vmem()] * 2,
        out_shape=[shape, shape],
        compiler_params=params(),
        cost_estimate=pl.CostEstimate(flops=2**20, bytes_accessed=2**14, transcendentals=0),
    )(me, counts, ranks)


def pack_kernel(turned, classes, cap, width, slot_ref, cos_ref, sin_ref, row_ref, *rest):
    out_refs, hot_ref = rest[:-1], rest[-1]

    @pl.when(pl.program_id(0) == 0)
    def _():
        ids = lax.broadcasted_iota(jnp.int32, hot_ref.shape, 0)
        hot_ref[...] = (ids == slot_ref[...]).astype(jnp.float32).astype(jnp.bfloat16)

    if turned:
        rows = jnp.concatenate(
            [
                turn(row_ref[:, h * HD : (h + 1) * HD], cos_ref[...], sin_ref[...])
                for h in range(width)
            ],
            axis=1,
        )
    else:
        rows = row_ref[...]
    for j, out_ref in enumerate(out_refs):
        for r in range(classes):
            first = (j * classes + r) * cap
            moved = jnp.dot(
                hot_ref[first : first + cap, :], rows, preferred_element_type=jnp.float32
            ).astype(jnp.bfloat16)
            for h in range(width):
                out_ref[h, r] = moved[:, h * HD : (h + 1) * HD]


def pack(slots, cosine, sine, rows, turned, chunks, classes, cap):
    count = rows.shape[0]
    heads = rows.shape[1] // HD
    width = min(2, heads)
    fixed = lambda i: (0, 0)
    total = chunks * classes * cap
    return pl.pallas_call(
        functools.partial(pack_kernel, turned, classes, cap, width),
        grid=(heads // width,),
        in_specs=[
            pl.BlockSpec((1, count), fixed),
            pl.BlockSpec((count, HD), fixed),
            pl.BlockSpec((count, HD), fixed),
            pl.BlockSpec((count, width * HD), lambda i: (0, i)),
        ],
        out_specs=[pl.BlockSpec((width, classes, cap, HD), lambda i: (i, 0, 0, 0))] * chunks,
        out_shape=[jax.ShapeDtypeStruct((heads, classes, cap, HD), jnp.bfloat16)] * chunks,
        scratch_shapes=[pltpu.VMEM((total, count), jnp.bfloat16)],
        compiler_params=params(),
        cost_estimate=pl.CostEstimate(
            flops=2 * heads * total * count * HD, bytes_accessed=count * heads * HD * 4, transcendentals=0
        ),
    )(slots, cosine, sine, rows)


def piece_rows(cap):
    return max(rows for rows in range(TILE, PAD + 1, TILE) if cap % rows == 0)


def merge_pieces(low, high, piece, source, add):
    shift = low & (TILE - 1)
    pieces = jnp.where(high > low, lax.div(high - low + shift + piece - 1, piece), 0)
    first = low - shift

    def one(i, carry):
        at = pl.multiple_of(first + i * piece, TILE)
        add(at, source(pl.multiple_of(i * piece, TILE)))
        return carry

    lax.fori_loop(0, pieces, one, 0)


def compact_kernel(offsets, per, total, as_keys, member_ref, count_ref, *rest):
    parts, out, all_rows, starts = rest[:-3], rest[-3], rest[-2], rest[-1]
    members = len(parts)
    piece = piece_rows(parts[0].shape[1])
    all_rows[...] = jnp.zeros_like(all_rows)
    start = jnp.int32(0)
    for s in range(count_ref.shape[0]):
        starts[s] = start
        start = start + count_ref[s]

    def add(at, rows):
        all_rows[pl.ds(at, piece), :] += rows

    for part, offset in zip(parts, offsets):
        for z in range(per):
            source = z * members + (member_ref[0] ^ offset)
            low = starts[source]
            merge_pieces(
                low,
                low + count_ref[source],
                piece,
                lambda at: part[z, pl.ds(at, piece), :],
                add,
            )
    if as_keys:
        for first in range(0, total, 2 * TOK_DEV):
            out[:, first : first + 2 * TOK_DEV] = jnp.transpose(
                all_rows[first : first + 2 * TOK_DEV, :]
            )
    else:
        out[...] = all_rows[:total, :]


def compact(member, counts, parts, offsets, total, as_keys):
    per = parts[0].shape[0]
    return pl.pallas_call(
        functools.partial(compact_kernel, offsets, per, total, as_keys),
        in_specs=[whole_smem(), whole_smem()] + [whole_vmem()] * len(parts),
        out_specs=whole_vmem(),
        out_shape=jax.ShapeDtypeStruct(
            (HD, total) if as_keys else (total, HD), jnp.bfloat16
        ),
        scratch_shapes=[
            pltpu.VMEM((total + PAD, HD), jnp.bfloat16),
            pltpu.SMEM(counts.shape, jnp.int32),
        ],
        compiler_params=params(),
        cost_estimate=pl.CostEstimate(flops=total * HD * 8, bytes_accessed=total * HD * 8, transcendentals=0),
    )(member, counts, *parts)


def attend_kernel(ctx_size, block, cls_ref, count_ref, got_ref, key_ref, value_ref, out_ref,
                  query_all, scores_a, scores_b, top_a, top_b, run_max, run_acc):
    span = 2 * TOK_DEV
    pair = 4 * block
    supers = ctx_size // 4
    steps = supers * (supers + 1)
    cls = cls_ref[0]
    piece = piece_rows(got_ref.shape[1])
    query_all[...] = jnp.zeros_like(query_all)

    def add(at, rows):
        query_all[pl.ds(at, piece), :] += rows

    start = jnp.int32(0)
    for s in range(ctx_size):
        end = start + count_ref[s]
        merge_pieces(
            rows_below(start, cls, block),
            rows_below(end, cls, block),
            piece,
            lambda at: got_ref[s, pl.ds(at, piece), :],
            add,
        )
        start = end

    upper = 2 * block
    keep_all, lower = slice(0, pair), slice(upper, pair)

    def row_top(found):
        return jnp.broadcast_to(jnp.max(found, axis=1, keepdims=True), (found.shape[0], HD))

    def allowed(first_row, count, first_key):
        ids = lax.broadcasted_iota(jnp.int32, (count, HD), 0) + first_row
        row = ids + cls * block - first_key
        for n in range(1, 4):
            row = row + jnp.where(ids >= n * block, TOK_DEV - block, 0)
        col = lax.broadcasted_iota(jnp.int32, (count, span), 1)
        return col <= jnp.concatenate([row] * (span // HD), axis=1)

    def put(scores, top, part, found):
        scores[part, :] = found
        top[part, :] = row_top(found)

    def dot_keys(i, k, first_row, count):
        at = jnp.minimum(i, supers - 1) * pair + first_row
        rows = query_all[pl.ds(pl.multiple_of(at, TILE), count), :]
        keys = key_ref[:, pl.ds(pl.multiple_of(k * span, HD), span)]
        return jnp.dot(rows, keys, preferred_element_type=jnp.float32)

    def score(scores, top, i, k):
        put(scores, top, keep_all, dot_keys(i, k, 0, pair))

    def score_lower(scores, top, i, k):
        found = dot_keys(i, k, upper, pair - upper)
        found = jnp.where(allowed(upper, pair - upper, span), found, masked_score)
        put(scores, top, lower, found)

    def mask_upper(scores, top):
        found = jnp.where(allowed(0, upper, 0), scores[:upper, :], masked_score)
        put(scores, top, slice(0, upper), found)

    def absorb(scores, top, k, part):
        before = run_max[part, :]
        after = jnp.maximum(before, top[part, :])
        rescale = jnp.exp2((before - after) * exp2_scale)
        run_max[part, :] = after
        weights = jnp.exp2(
            (scores[part, :] - jnp.concatenate([after] * (span // HD), axis=1)) * exp2_scale
        )
        values = jnp.concatenate(
            [
                value_ref[pl.ds(pl.multiple_of(k * span, TILE), span), :],
                jnp.ones((span, HD), jnp.bfloat16),
            ],
            axis=1,
        )
        run_acc[part, :] = run_acc[part, :] * jnp.concatenate([rescale, rescale], axis=1) + jnp.dot(
            weights.astype(jnp.bfloat16), values, preferred_element_type=jnp.float32
        )

    def clear():
        run_max[...] = jnp.full_like(run_max, masked_score)
        run_acc[...] = jnp.zeros_like(run_acc)

    buffers_a, buffers_b = (scores_a, top_a), (scores_b, top_b)
    clear()
    score(*buffers_a, 0, 0)
    mask_upper(*buffers_a)

    def two_steps(t, at):
        i, k = at
        last = k == 2 * i

        @pl.when(last)
        def _():
            score_lower(*buffers_b, i, k + 1)
            absorb(*buffers_a, k, keep_all)
            score(*buffers_a, i + 1, 0)
            absorb(*buffers_b, k + 1, lower)
            result = (run_acc[:, :HD] / run_acc[:, HD:]).astype(jnp.bfloat16)
            for n in range(4):
                out_ref[4 * i + n] = result[n * block : (n + 1) * block]
            clear()

        @pl.when(jnp.logical_not(last))
        def _():
            score(*buffers_b, i, k + 1)
            absorb(*buffers_a, k, keep_all)
            score(*buffers_a, i, k + 2)
            absorb(*buffers_b, k + 1, keep_all)

            @pl.when(k + 2 == 2 * i)
            def _():
                mask_upper(*buffers_a)

        return jnp.where(last, i + 1, i), jnp.where(last, 0, k + 2)

    lax.fori_loop(0, steps // 2, two_steps, (jnp.int32(0), jnp.int32(0)))


def attend(cls, counts, got, keys, values, block):
    ctx_size = got.shape[0]
    total = values.shape[0]
    pairs = total * ctx_size * block // 2
    return pl.pallas_call(
        functools.partial(attend_kernel, ctx_size, block),
        in_specs=[whole_smem()] * 2 + [whole_vmem()] * 3,
        out_specs=whole_vmem(),
        out_shape=jax.ShapeDtypeStruct((ctx_size, block, HD), jnp.bfloat16),
        scratch_shapes=[
            pltpu.VMEM((ctx_size * block + PAD, HD), jnp.bfloat16),
            pltpu.VMEM((4 * block, 2 * TOK_DEV), jnp.float32),
            pltpu.VMEM((4 * block, 2 * TOK_DEV), jnp.float32),
            pltpu.VMEM((4 * block, HD), jnp.float32),
            pltpu.VMEM((4 * block, HD), jnp.float32),
            pltpu.VMEM((4 * block, HD), jnp.float32),
            pltpu.VMEM((4 * block, 2 * HD), jnp.float32),
        ],
        compiler_params=params(),
        cost_estimate=pl.CostEstimate(
            flops=pairs * 8 * HD, bytes_accessed=total * HD * 8, transcendentals=pairs
        ),
    )(cls, counts, got, keys, values)


def project_kernel(classes, chunks, column_ref, *rest):
    got_refs, (weight_ref, out_ref, rows_ref) = rest[:chunks], rest[chunks:]
    block = got_refs[0].shape[1]

    @pl.when(pl.program_id(0) == 0)
    def _():
        for j, got_ref in enumerate(got_refs):
            for d in range(got_ref.shape[0]):
                h, r = d // classes, d % classes
                first = (j * classes + r) * block
                rows_ref[first : first + block, h * HD : (h + 1) * HD] = got_ref[d]

    out_ref[...] = jnp.dot(
        rows_ref[...], weight_ref[...], preferred_element_type=jnp.float32
    ).astype(jnp.bfloat16)


def project(first_column, got, weight, columns, classes):
    ctx_size, block, _ = got[0].shape
    rows, depth = len(got) * classes * block, weight.shape[0]
    step = min(512, columns)
    return pl.pallas_call(
        functools.partial(project_kernel, classes, len(got)),
        grid_spec=pltpu.PrefetchScalarGridSpec(
            num_scalar_prefetch=1,
            grid=(columns // step,),
            in_specs=[pl.BlockSpec((ctx_size, block, HD), lambda i, first: (0, 0, 0))] * len(got)
            + [pl.BlockSpec((depth, step), lambda i, first: (0, first[0] + i))],
            out_specs=pl.BlockSpec((rows, step), lambda i, first: (0, i)),
            scratch_shapes=[pltpu.VMEM((rows, depth), jnp.bfloat16)],
        ),
        out_shape=jax.ShapeDtypeStruct((rows, columns), jnp.bfloat16),
        compiler_params=params(),
        cost_estimate=pl.CostEstimate(
            flops=2 * rows * depth * columns, bytes_accessed=2 * depth * columns, transcendentals=0
        ),
    )((first_column // step).astype(jnp.int32).reshape(1), *got, weight)


def add_piece_kernel(sum_ref, part_ref, out_ref):
    out_ref[...] = (
        sum_ref[...].astype(jnp.float32) + part_ref[...].astype(jnp.float32)
    ).astype(jnp.bfloat16)


def add_piece(total_sum, part, j, first):
    rows, width = part.shape
    step = 512
    steps = width // step
    here = pl.BlockSpec((rows, step), lambda i: (j, first // step + i))
    return pl.pallas_call(
        add_piece_kernel,
        grid=(steps,),
        in_specs=[here, pl.BlockSpec((rows, step), lambda i: (0, i))],
        out_specs=here,
        out_shape=jax.ShapeDtypeStruct(total_sum.shape, total_sum.dtype),
        input_output_aliases={0: 0},
        compiler_params=params(),
        cost_estimate=pl.CostEstimate(
            flops=rows * width, bytes_accessed=6 * rows * width, transcendentals=0
        ),
    )(total_sum, part)


def tables(query_rows):
    half_dim = HD // 2
    positions = lax.axis_index("ctx") * query_rows + jnp.arange(query_rows, dtype=jnp.int32)
    lane = jnp.arange(HD, dtype=jnp.int32)
    pair_id = jnp.where(lane < half_dim, lane, lane - half_dim)
    inv_freq = rope_base ** (-(pair_id.astype(jnp.float32) * 2.0 / HD))
    angles = positions.astype(jnp.float32)[:, None] * inv_freq[None, :]
    sine = jnp.sin(angles)
    return jnp.cos(angles), jnp.where(lane[None, :] < half_dim, -sine, sine)


def local(query, key, value, keep_rank, kept_count, out_weight):
    ctx_size = lax.axis_size("ctx")
    tp_size = lax.axis_size("tp")
    me = lax.axis_index("ctx")
    tp_me = lax.axis_index("tp")
    orig_rows = query.shape[0]
    heads = query.shape[1] // HD
    kv_heads = key.shape[1] // HD
    members = ctx_size // kv_heads
    classes = ctx_size // heads
    chunks = CHUNKS if classes == 1 else 1
    block = TOK_DEV // (chunks * classes)
    total = ctx_size * TOK_DEV
    reach = orig_rows // TOK_DEV
    cap = reach * block + TILE
    cap_kv = orig_rows + TILE
    columns = out_weight.shape[1] // tp_size

    kv_slots, q_slots = find_slots(
        me.reshape(1), kept_count, keep_rank, reach, chunks * classes, block, cap
    )
    cosine, sine = tables(orig_rows)

    across = [[z * members + m for z in range(kv_heads)] for m in range(members)]

    member = (me & (members - 1)).reshape(1)

    def pack_shared(rows, turned):
        (packed,) = pack(kv_slots, cosine, sine, rows, turned, 1, 1, cap_kv)
        return packed.reshape(kv_heads, cap_kv, HD)

    def send_across(packed):
        if kv_heads == 1:
            return packed
        return lax.all_to_all(
            packed, "ctx", split_axis=0, concat_axis=0, tiled=True, axis_index_groups=across
        )

    def swap(parts, bit):
        pairs = [(d, d ^ bit) for d in range(ctx_size)]
        return parts + [lax.ppermute(part, "ctx", pairs) for part in parts]

    bits = [members >> n for n in range(1, members.bit_length())]
    offsets = [0]
    for bit in bits:
        offsets = offsets + [offset ^ bit for offset in offsets]

    def send_query(packed):
        return lax.all_to_all(
            packed.reshape(ctx_size, cap, HD), "ctx", split_axis=0, concat_axis=0, tiled=True
        )

    both = [(0, 1), (1, 0)]
    key_parts = [send_across(pack_shared(key, True))]
    value_packed, key_parts = lax.optimization_barrier((pack_shared(value, False), key_parts))
    key_parts = swap(key_parts, bits[0])
    value_parts = [send_across(value_packed)]
    packed_q = list(pack(q_slots, cosine, sine, query, True, chunks, classes, cap))
    packed_q[0], key_parts, value_parts = lax.optimization_barrier(
        (packed_q[0], key_parts, value_parts)
    )
    got_q = [send_query(packed_q[0])]
    value_parts = swap(value_parts, bits[0])
    for bit in bits[1:]:
        key_parts = swap(key_parts, bit)
    keys = compact(member, kept_count, key_parts, offsets, total, True)
    if chunks > 1:
        packed_q[1], value_parts, keys = lax.optimization_barrier((packed_q[1], value_parts, keys))
    for bit in bits[1:]:
        value_parts = swap(value_parts, bit)
    if chunks > 1:
        got_q.append(send_query(packed_q[1]))
    values = compact(member, kept_count, value_parts, offsets, total, False)

    got, done = [], None
    for j in range(chunks):
        cls_j = j * classes + (me & (classes - 1))
        if j > 0:
            got_q[j], done = lax.optimization_barrier((got_q[j], done))
            got.append(lax.all_to_all(done, "ctx", split_axis=0, concat_axis=0, tiled=True))
        done = attend(cls_j.reshape(1), kept_count, got_q[j], keys, values, block)
        if j > 1:
            done, got[j - 2] = lax.optimization_barrier((done, got[j - 2]))
        if j + 2 < chunks:
            packed_q[j + 2], done = lax.optimization_barrier((packed_q[j + 2], done))
            got_q.append(send_query(packed_q[j + 2]))
    quarter = columns // 4
    widths = [(quarter, 3 * quarter), (3 * quarter, quarter)]

    def for_peer(one, j):
        return [
            project((1 - tp_me) * columns + first, [one], out_weight, width, classes)
            for first, width in zip((0, widths[j][0]), widths[j])
        ]

    def trade(parts):
        return [lax.ppermute(part, "tp", [(0, 1), (1, 0)]) for part in parts]

    paired = tp_size == 2 and chunks == 2
    if paired:
        first = for_peer(got[0], 0)
        done, first[0] = lax.optimization_barrier((done, first[0]))
    last = lax.all_to_all(done, "ctx", split_axis=0, concat_axis=0, tiled=True)
    if paired:
        last, first[1] = lax.optimization_barrier((last, first[1]))
        came = [trade(first), trade(for_peer(last, 1))]
        total_sum = project(tp_me * columns, got + [last], out_weight, columns, classes)
        for j, parts in enumerate(came):
            total_sum = add_piece(total_sum, parts[0], j, 0)
            total_sum = add_piece(total_sum, parts[1], j, widths[j][0])
        return total_sum
    got.append(last)
    full = project(jnp.int32(0) * tp_me, got, out_weight, columns * tp_size, classes)
    split = jnp.transpose(full.reshape(full.shape[0], tp_size, columns), (1, 0, 2))
    swapped = lax.all_to_all(split, "tp", split_axis=0, concat_axis=0, tiled=True)
    return jnp.sum(swapped.astype(jnp.float32), axis=0).astype(jnp.bfloat16)


def solution(mesh):
    placed = (P("ctx", "tp"), P("ctx", "tp"), P("ctx", "tp"), P("ctx", None), P(), P("tp", None))
    return jax.shard_map(
        local, mesh=mesh, in_specs=placed, out_specs=P("ctx", "tp"), check_vma=False
    )
```

```python
import functools
import math

import jax
import jax.numpy as jnp
from jax import lax
from jax.experimental import pallas as pl
from jax.experimental.pallas import tpu as pltpu
from jax.sharding import PartitionSpec as P

HD = 128
TOK_DEV = 384
TILE = 16
PAD = 288
CHUNKS = 2

rope_base = 1000000.0
masked_score = -1e30
exp2_scale = math.log2(math.e) / math.sqrt(HD)
VMEM_BYTES = 58 * 1024 * 1024


def whole_vmem():
    return pl.BlockSpec(memory_space=pltpu.VMEM)


def whole_smem():
    return pl.BlockSpec(memory_space=pltpu.SMEM)


def params():
    return pltpu.CompilerParams(vmem_limit_bytes=VMEM_BYTES)


def turn(rows, cosine, sine):
    as_float = rows.astype(jnp.float32)
    swapped = pltpu.roll(as_float, HD // 2, 1)
    return (as_float * cosine + swapped * sine).astype(jnp.bfloat16)


def rows_below(start, cls, block):
    whole = lax.div(start, TOK_DEV)
    return whole * block + jnp.clip(start - whole * TOK_DEV - cls * block, 0, block)


def slots_kernel(reach, groups, block, cap, me_ref, count_ref, rank_ref, kv_out, q_out):
    me = me_ref[0]
    rows = rank_ref.shape[1]
    start = jnp.int32(0)
    for s in range(count_ref.shape[0]):
        start = start + jnp.where(s < me, count_ref[s], 0)
    kept = rank_ref[...] < count_ref[me]
    upper = lax.broadcasted_iota(jnp.int32, (rows, rows), 0) <= lax.broadcasted_iota(
        jnp.int32, (rows, rows), 1
    )
    flags = jnp.broadcast_to(kept.astype(jnp.float32), (8, rows)).astype(jnp.bfloat16)
    order = (
        jnp.dot(
            flags, upper.astype(jnp.float32).astype(jnp.bfloat16), preferred_element_type=jnp.float32
        )[:1].astype(jnp.int32)
        - 1
    )
    kv_out[...] = jnp.where(kept, order + (start & (TILE - 1)), -1)
    place = start + order
    first = lax.div(start, TOK_DEV)
    device = first + jnp.zeros_like(place)
    for step in range(1, reach + 1):
        device = device + (place >= (first + step) * TOK_DEV).astype(jnp.int32)
    within = place - device * TOK_DEV
    cls = jnp.zeros_like(place)
    for step in range(1, groups):
        cls = cls + (within >= step * block).astype(jnp.int32)
    low = first * block + jnp.clip(start - first * TOK_DEV - cls * block, 0, block)
    slot = cls * cap + device * block + within - cls * block - low + (low & (TILE - 1))
    q_out[...] = jnp.where(kept, slot, -1)


def find_slots(me, counts, ranks, reach, groups, block, cap):
    shape = jax.ShapeDtypeStruct(ranks.shape, jnp.int32)
    return pl.pallas_call(
        functools.partial(slots_kernel, reach, groups, block, cap),
        in_specs=[whole_smem(), whole_smem(), whole_vmem()],
        out_specs=[whole_vmem()] * 2,
        out_shape=[shape, shape],
        compiler_params=params(),
        cost_estimate=pl.CostEstimate(flops=2**20, bytes_accessed=2**14, transcendentals=0),
    )(me, counts, ranks)


def pack_kernel(turned, classes, cap, width, slot_ref, cos_ref, sin_ref, row_ref, *rest):
    out_refs, hot_ref = rest[:-1], rest[-1]

    @pl.when(pl.program_id(0) == 0)
    def _():
        ids = lax.broadcasted_iota(jnp.int32, hot_ref.shape, 0)
        hot_ref[...] = (ids == slot_ref[...]).astype(jnp.float32).astype(jnp.bfloat16)

    if turned:
        rows = jnp.concatenate(
            [
                turn(row_ref[:, h * HD : (h + 1) * HD], cos_ref[...], sin_ref[...])
                for h in range(width)
            ],
            axis=1,
        )
    else:
        rows = row_ref[...]
    for j, out_ref in enumerate(out_refs):
        for r in range(classes):
            first = (j * classes + r) * cap
            moved = jnp.dot(
                hot_ref[first : first + cap, :], rows, preferred_element_type=jnp.float32
            ).astype(jnp.bfloat16)
            for h in range(width):
                out_ref[h, r] = moved[:, h * HD : (h + 1) * HD]


def pack(slots, cosine, sine, rows, turned, chunks, classes, cap):
    count = rows.shape[0]
    heads = rows.shape[1] // HD
    width = min(2, heads)
    fixed = lambda i: (0, 0)
    total = chunks * classes * cap
    return pl.pallas_call(
        functools.partial(pack_kernel, turned, classes, cap, width),
        grid=(heads // width,),
        in_specs=[
            pl.BlockSpec((1, count), fixed),
            pl.BlockSpec((count, HD), fixed),
            pl.BlockSpec((count, HD), fixed),
            pl.BlockSpec((count, width * HD), lambda i: (0, i)),
        ],
        out_specs=[pl.BlockSpec((width, classes, cap, HD), lambda i: (i, 0, 0, 0))] * chunks,
        out_shape=[jax.ShapeDtypeStruct((heads, classes, cap, HD), jnp.bfloat16)] * chunks,
        scratch_shapes=[pltpu.VMEM((total, count), jnp.bfloat16)],
        compiler_params=params(),
        cost_estimate=pl.CostEstimate(
            flops=2 * heads * total * count * HD, bytes_accessed=count * heads * HD * 4, transcendentals=0
        ),
    )(slots, cosine, sine, rows)


def piece_rows(cap):
    return max(rows for rows in range(TILE, PAD + 1, TILE) if cap % rows == 0)


def merge_pieces(low, high, piece, source, add):
    shift = low & (TILE - 1)
    pieces = jnp.where(high > low, lax.div(high - low + shift + piece - 1, piece), 0)
    first = low - shift

    def one(i, carry):
        at = pl.multiple_of(first + i * piece, TILE)
        add(at, source(pl.multiple_of(i * piece, TILE)))
        return carry

    lax.fori_loop(0, pieces, one, 0)


def compact_kernel(offsets, per, total, as_keys, member_ref, count_ref, *rest):
    parts, out, all_rows, starts = rest[:-3], rest[-3], rest[-2], rest[-1]
    members = len(parts)
    piece = piece_rows(parts[0].shape[1])
    all_rows[...] = jnp.zeros_like(all_rows)
    start = jnp.int32(0)
    for s in range(count_ref.shape[0]):
        starts[s] = start
        start = start + count_ref[s]

    def add(at, rows):
        all_rows[pl.ds(at, piece), :] += rows

    for part, offset in zip(parts, offsets):
        for z in range(per):
            source = z * members + (member_ref[0] ^ offset)
            low = starts[source]
            merge_pieces(
                low,
                low + count_ref[source],
                piece,
                lambda at: part[z, pl.ds(at, piece), :],
                add,
            )
    if as_keys:
        for first in range(0, total, 2 * TOK_DEV):
            out[:, first : first + 2 * TOK_DEV] = jnp.transpose(
                all_rows[first : first + 2 * TOK_DEV, :]
            )
    else:
        out[...] = all_rows[:total, :]


def compact(member, counts, parts, offsets, total, as_keys):
    per = parts[0].shape[0]
    return pl.pallas_call(
        functools.partial(compact_kernel, offsets, per, total, as_keys),
        in_specs=[whole_smem(), whole_smem()] + [whole_vmem()] * len(parts),
        out_specs=whole_vmem(),
        out_shape=jax.ShapeDtypeStruct(
            (HD, total) if as_keys else (total, HD), jnp.bfloat16
        ),
        scratch_shapes=[
            pltpu.VMEM((total + PAD, HD), jnp.bfloat16),
            pltpu.SMEM(counts.shape, jnp.int32),
        ],
        compiler_params=params(),
        cost_estimate=pl.CostEstimate(flops=total * HD * 8, bytes_accessed=total * HD * 8, transcendentals=0),
    )(member, counts, *parts)


def attend_kernel(ctx_size, block, cls_ref, count_ref, got_ref, key_ref, value_ref, out_ref,
                  query_all, scores_a, scores_b, top_a, top_b, run_max, run_acc):
    span = 2 * TOK_DEV
    pair = 4 * block
    supers = ctx_size // 4
    steps = supers * (supers + 1)
    cls = cls_ref[0]
    piece = piece_rows(got_ref.shape[1])
    query_all[...] = jnp.zeros_like(query_all)

    def add(at, rows):
        query_all[pl.ds(at, piece), :] += rows

    start = jnp.int32(0)
    for s in range(ctx_size):
        end = start + count_ref[s]
        merge_pieces(
            rows_below(start, cls, block),
            rows_below(end, cls, block),
            piece,
            lambda at: got_ref[s, pl.ds(at, piece), :],
            add,
        )
        start = end

    upper = 2 * block
    keep_all, lower = slice(0, pair), slice(upper, pair)

    def row_top(found):
        return jnp.broadcast_to(jnp.max(found, axis=1, keepdims=True), (found.shape[0], HD))

    def allowed(first_row, count, first_key):
        ids = lax.broadcasted_iota(jnp.int32, (count, HD), 0) + first_row
        row = ids + cls * block - first_key
        for n in range(1, 4):
            row = row + jnp.where(ids >= n * block, TOK_DEV - block, 0)
        col = lax.broadcasted_iota(jnp.int32, (count, span), 1)
        return col <= jnp.concatenate([row] * (span // HD), axis=1)

    def put(scores, top, part, found):
        scores[part, :] = found
        top[part, :] = row_top(found)

    def dot_keys(i, k, first_row, count):
        at = jnp.minimum(i, supers - 1) * pair + first_row
        rows = query_all[pl.ds(pl.multiple_of(at, TILE), count), :]
        keys = key_ref[:, pl.ds(pl.multiple_of(k * span, HD), span)]
        return jnp.dot(rows, keys, preferred_element_type=jnp.float32)

    def score(scores, top, i, k):
        put(scores, top, keep_all, dot_keys(i, k, 0, pair))

    def score_lower(scores, top, i, k):
        found = dot_keys(i, k, upper, pair - upper)
        found = jnp.where(allowed(upper, pair - upper, span), found, masked_score)
        put(scores, top, lower, found)

    def mask_upper(scores, top):
        found = jnp.where(allowed(0, upper, 0), scores[:upper, :], masked_score)
        put(scores, top, slice(0, upper), found)

    def absorb(scores, top, k, part):
        before = run_max[part, :]
        after = jnp.maximum(before, top[part, :])
        rescale = jnp.exp2((before - after) * exp2_scale)
        run_max[part, :] = after
        weights = jnp.exp2(
            (scores[part, :] - jnp.concatenate([after] * (span // HD), axis=1)) * exp2_scale
        )
        values = jnp.concatenate(
            [
                value_ref[pl.ds(pl.multiple_of(k * span, TILE), span), :],
                jnp.ones((span, HD), jnp.bfloat16),
            ],
            axis=1,
        )
        run_acc[part, :] = run_acc[part, :] * jnp.concatenate([rescale, rescale], axis=1) + jnp.dot(
            weights.astype(jnp.bfloat16), values, preferred_element_type=jnp.float32
        )

    def clear():
        run_max[...] = jnp.full_like(run_max, masked_score)
        run_acc[...] = jnp.zeros_like(run_acc)

    buffers_a, buffers_b = (scores_a, top_a), (scores_b, top_b)
    clear()
    score(*buffers_a, 0, 0)
    mask_upper(*buffers_a)

    def two_steps(t, at):
        i, k = at
        last = k == 2 * i

        @pl.when(last)
        def _():
            score_lower(*buffers_b, i, k + 1)
            absorb(*buffers_a, k, keep_all)
            score(*buffers_a, i + 1, 0)
            absorb(*buffers_b, k + 1, lower)
            result = (run_acc[:, :HD] / run_acc[:, HD:]).astype(jnp.bfloat16)
            for n in range(4):
                out_ref[4 * i + n] = result[n * block : (n + 1) * block]
            clear()

        @pl.when(jnp.logical_not(last))
        def _():
            score(*buffers_b, i, k + 1)
            absorb(*buffers_a, k, keep_all)
            score(*buffers_a, i, k + 2)
            absorb(*buffers_b, k + 1, keep_all)

            @pl.when(k + 2 == 2 * i)
            def _():
                mask_upper(*buffers_a)

        return jnp.where(last, i + 1, i), jnp.where(last, 0, k + 2)

    lax.fori_loop(0, steps // 2, two_steps, (jnp.int32(0), jnp.int32(0)))


def attend(cls, counts, got, keys, values, block):
    ctx_size = got.shape[0]
    total = values.shape[0]
    pairs = total * ctx_size * block // 2
    return pl.pallas_call(
        functools.partial(attend_kernel, ctx_size, block),
        in_specs=[whole_smem()] * 2 + [whole_vmem()] * 3,
        out_specs=whole_vmem(),
        out_shape=jax.ShapeDtypeStruct((ctx_size, block, HD), jnp.bfloat16),
        scratch_shapes=[
            pltpu.VMEM((ctx_size * block + PAD, HD), jnp.bfloat16),
            pltpu.VMEM((4 * block, 2 * TOK_DEV), jnp.float32),
            pltpu.VMEM((4 * block, 2 * TOK_DEV), jnp.float32),
            pltpu.VMEM((4 * block, HD), jnp.float32),
            pltpu.VMEM((4 * block, HD), jnp.float32),
            pltpu.VMEM((4 * block, HD), jnp.float32),
            pltpu.VMEM((4 * block, 2 * HD), jnp.float32),
        ],
        compiler_params=params(),
        cost_estimate=pl.CostEstimate(
            flops=pairs * 8 * HD, bytes_accessed=total * HD * 8, transcendentals=pairs
        ),
    )(cls, counts, got, keys, values)


def project_kernel(classes, chunks, column_ref, *rest):
    got_refs, (weight_ref, out_ref, rows_ref) = rest[:chunks], rest[chunks:]
    block = got_refs[0].shape[1]

    @pl.when(pl.program_id(0) == 0)
    def _():
        for j, got_ref in enumerate(got_refs):
            for d in range(got_ref.shape[0]):
                h, r = d // classes, d % classes
                first = (j * classes + r) * block
                rows_ref[first : first + block, h * HD : (h + 1) * HD] = got_ref[d]

    out_ref[...] = jnp.dot(
        rows_ref[...], weight_ref[...], preferred_element_type=jnp.float32
    ).astype(jnp.bfloat16)


def project(first_column, got, weight, columns, classes):
    ctx_size, block, _ = got[0].shape
    rows, depth = len(got) * classes * block, weight.shape[0]
    step = min(512, columns)
    return pl.pallas_call(
        functools.partial(project_kernel, classes, len(got)),
        grid_spec=pltpu.PrefetchScalarGridSpec(
            num_scalar_prefetch=1,
            grid=(columns // step,),
            in_specs=[pl.BlockSpec((ctx_size, block, HD), lambda i, first: (0, 0, 0))] * len(got)
            + [pl.BlockSpec((depth, step), lambda i, first: (0, first[0] + i))],
            out_specs=pl.BlockSpec((rows, step), lambda i, first: (0, i)),
            scratch_shapes=[pltpu.VMEM((rows, depth), jnp.bfloat16)],
        ),
        out_shape=jax.ShapeDtypeStruct((rows, columns), jnp.bfloat16),
        compiler_params=params(),
        cost_estimate=pl.CostEstimate(
            flops=2 * rows * depth * columns, bytes_accessed=2 * depth * columns, transcendentals=0
        ),
    )((first_column // step).astype(jnp.int32).reshape(1), *got, weight)


def add_piece_kernel(sum_ref, part_ref, out_ref):
    out_ref[...] = (
        sum_ref[...].astype(jnp.float32) + part_ref[...].astype(jnp.float32)
    ).astype(jnp.bfloat16)


def add_piece(total_sum, part, j, n):
    rows, width = part.shape
    step = min(1024, width)
    steps = width // step
    here = pl.BlockSpec((rows, step), lambda i: (j, n * steps + i))
    return pl.pallas_call(
        add_piece_kernel,
        grid=(steps,),
        in_specs=[here, pl.BlockSpec((rows, step), lambda i: (0, i))],
        out_specs=here,
        out_shape=jax.ShapeDtypeStruct(total_sum.shape, total_sum.dtype),
        input_output_aliases={0: 0},
        compiler_params=params(),
        cost_estimate=pl.CostEstimate(
            flops=rows * width, bytes_accessed=6 * rows * width, transcendentals=0
        ),
    )(total_sum, part)


def tables(query_rows):
    half_dim = HD // 2
    positions = lax.axis_index("ctx") * query_rows + jnp.arange(query_rows, dtype=jnp.int32)
    lane = jnp.arange(HD, dtype=jnp.int32)
    pair_id = jnp.where(lane < half_dim, lane, lane - half_dim)
    inv_freq = rope_base ** (-(pair_id.astype(jnp.float32) * 2.0 / HD))
    angles = positions.astype(jnp.float32)[:, None] * inv_freq[None, :]
    sine = jnp.sin(angles)
    return jnp.cos(angles), jnp.where(lane[None, :] < half_dim, -sine, sine)


def local(query, key, value, keep_rank, kept_count, out_weight):
    ctx_size = lax.axis_size("ctx")
    tp_size = lax.axis_size("tp")
    me = lax.axis_index("ctx")
    tp_me = lax.axis_index("tp")
    orig_rows = query.shape[0]
    heads = query.shape[1] // HD
    kv_heads = key.shape[1] // HD
    members = ctx_size // kv_heads
    classes = ctx_size // heads
    chunks = CHUNKS if classes == 1 else 1
    block = TOK_DEV // (chunks * classes)
    total = ctx_size * TOK_DEV
    reach = orig_rows // TOK_DEV
    cap = reach * block + TILE
    cap_kv = orig_rows + TILE
    columns = out_weight.shape[1] // tp_size

    kv_slots, q_slots = find_slots(
        me.reshape(1), kept_count, keep_rank, reach, chunks * classes, block, cap
    )
    cosine, sine = tables(orig_rows)

    across = [[z * members + m for z in range(kv_heads)] for m in range(members)]

    member = (me & (members - 1)).reshape(1)

    def pack_shared(rows, turned):
        (packed,) = pack(kv_slots, cosine, sine, rows, turned, 1, 1, cap_kv)
        return packed.reshape(kv_heads, cap_kv, HD)

    def send_across(packed):
        if kv_heads == 1:
            return packed
        return lax.all_to_all(
            packed, "ctx", split_axis=0, concat_axis=0, tiled=True, axis_index_groups=across
        )

    def swap(parts, bit):
        pairs = [(d, d ^ bit) for d in range(ctx_size)]
        return parts + [lax.ppermute(part, "ctx", pairs) for part in parts]

    bits = [members >> n for n in range(1, members.bit_length())]
    offsets = [0]
    for bit in bits:
        offsets = offsets + [offset ^ bit for offset in offsets]

    def send_query(packed):
        return lax.all_to_all(
            packed.reshape(ctx_size, cap, HD), "ctx", split_axis=0, concat_axis=0, tiled=True
        )

    both = [(0, 1), (1, 0)]
    key_parts = [send_across(pack_shared(key, True))]
    value_packed, key_parts = lax.optimization_barrier((pack_shared(value, False), key_parts))
    key_parts = swap(key_parts, bits[0])
    value_parts = [send_across(value_packed)]
    packed_q = list(pack(q_slots, cosine, sine, query, True, chunks, classes, cap))
    packed_q[0], key_parts, value_parts = lax.optimization_barrier(
        (packed_q[0], key_parts, value_parts)
    )
    got_q = [send_query(packed_q[0])]
    value_parts = swap(value_parts, bits[0])
    for bit in bits[1:]:
        key_parts = swap(key_parts, bit)
    keys = compact(member, kept_count, key_parts, offsets, total, True)
    if chunks > 1:
        packed_q[1], value_parts, keys = lax.optimization_barrier((packed_q[1], value_parts, keys))
    for bit in bits[1:]:
        value_parts = swap(value_parts, bit)
    if chunks > 1:
        got_q.append(send_query(packed_q[1]))
    values = compact(member, kept_count, value_parts, offsets, total, False)

    got, done = [], None
    for j in range(chunks):
        cls_j = j * classes + (me & (classes - 1))
        if j > 0:
            got_q[j], done = lax.optimization_barrier((got_q[j], done))
            got.append(lax.all_to_all(done, "ctx", split_axis=0, concat_axis=0, tiled=True))
        done = attend(cls_j.reshape(1), kept_count, got_q[j], keys, values, block)
        if j > 1:
            done, got[j - 2] = lax.optimization_barrier((done, got[j - 2]))
        if j + 2 < chunks:
            packed_q[j + 2], done = lax.optimization_barrier((packed_q[j + 2], done))
            got_q.append(send_query(packed_q[j + 2]))
    half = columns // 2

    def for_peer(one):
        return [
            project((1 - tp_me) * columns + n * half, [one], out_weight, half, classes)
            for n in range(2)
        ]

    def trade(parts):
        return [lax.ppermute(part, "tp", [(0, 1), (1, 0)]) for part in parts]

    paired = tp_size == 2 and chunks == 2
    if paired:
        first = for_peer(got[0])
        done, first[0] = lax.optimization_barrier((done, first[0]))
    last = lax.all_to_all(done, "ctx", split_axis=0, concat_axis=0, tiled=True)
    if paired:
        last, first[1] = lax.optimization_barrier((last, first[1]))
        came = [trade(first), trade(for_peer(last))]
        total_sum = project(tp_me * columns, got + [last], out_weight, columns, classes)
        for j, parts in enumerate(came):
            for n, part in enumerate(parts):
                total_sum = add_piece(total_sum, part, j, n)
        return total_sum
    got.append(last)
    full = project(jnp.int32(0) * tp_me, got, out_weight, columns * tp_size, classes)
    split = jnp.transpose(full.reshape(full.shape[0], tp_size, columns), (1, 0, 2))
    swapped = lax.all_to_all(split, "tp", split_axis=0, concat_axis=0, tiled=True)
    return jnp.sum(swapped.astype(jnp.float32), axis=0).astype(jnp.bfloat16)


def solution(mesh):
    placed = (P("ctx", "tp"), P("ctx", "tp"), P("ctx", "tp"), P("ctx", None), P(), P("tp", None))
    return jax.shard_map(
        local, mesh=mesh, in_specs=placed, out_specs=P("ctx", "tp"), check_vma=False
    )
```

```python
import functools
import math

import jax
import jax.numpy as jnp
from jax import lax
from jax.experimental import pallas as pl
from jax.experimental.pallas import tpu as pltpu
from jax.sharding import PartitionSpec as P

HD = 128
TOK_DEV = 384
TILE = 16
PAD = 288
CHUNKS = 2

rope_base = 1000000.0
masked_score = -1e30
exp2_scale = math.log2(math.e) / math.sqrt(HD)
VMEM_BYTES = 58 * 1024 * 1024


def whole_vmem():
    return pl.BlockSpec(memory_space=pltpu.VMEM)


def whole_smem():
    return pl.BlockSpec(memory_space=pltpu.SMEM)


def params():
    return pltpu.CompilerParams(vmem_limit_bytes=VMEM_BYTES)


def turn(rows, cosine, sine):
    as_float = rows.astype(jnp.float32)
    swapped = pltpu.roll(as_float, HD // 2, 1)
    return (as_float * cosine + swapped * sine).astype(jnp.bfloat16)


def rows_below(start, cls, block):
    whole = lax.div(start, TOK_DEV)
    return whole * block + jnp.clip(start - whole * TOK_DEV - cls * block, 0, block)


def slots_kernel(reach, groups, block, cap, me_ref, count_ref, rank_ref, kv_out, q_out):
    me = me_ref[0]
    rows = rank_ref.shape[1]
    start = jnp.int32(0)
    for s in range(count_ref.shape[0]):
        start = start + jnp.where(s < me, count_ref[s], 0)
    kept = rank_ref[...] < count_ref[me]
    upper = lax.broadcasted_iota(jnp.int32, (rows, rows), 0) <= lax.broadcasted_iota(
        jnp.int32, (rows, rows), 1
    )
    flags = jnp.broadcast_to(kept.astype(jnp.float32), (8, rows)).astype(jnp.bfloat16)
    order = (
        jnp.dot(
            flags, upper.astype(jnp.float32).astype(jnp.bfloat16), preferred_element_type=jnp.float32
        )[:1].astype(jnp.int32)
        - 1
    )
    kv_out[...] = jnp.where(kept, order + (start & (TILE - 1)), -1)
    place = start + order
    first = lax.div(start, TOK_DEV)
    device = first + jnp.zeros_like(place)
    for step in range(1, reach + 1):
        device = device + (place >= (first + step) * TOK_DEV).astype(jnp.int32)
    within = place - device * TOK_DEV
    cls = jnp.zeros_like(place)
    for step in range(1, groups):
        cls = cls + (within >= step * block).astype(jnp.int32)
    low = first * block + jnp.clip(start - first * TOK_DEV - cls * block, 0, block)
    slot = cls * cap + device * block + within - cls * block - low + (low & (TILE - 1))
    q_out[...] = jnp.where(kept, slot, -1)


def find_slots(me, counts, ranks, reach, groups, block, cap):
    shape = jax.ShapeDtypeStruct(ranks.shape, jnp.int32)
    return pl.pallas_call(
        functools.partial(slots_kernel, reach, groups, block, cap),
        in_specs=[whole_smem(), whole_smem(), whole_vmem()],
        out_specs=[whole_vmem()] * 2,
        out_shape=[shape, shape],
        compiler_params=params(),
        cost_estimate=pl.CostEstimate(flops=2**20, bytes_accessed=2**14, transcendentals=0),
    )(me, counts, ranks)


def pack_kernel(turned, classes, cap, width, slot_ref, cos_ref, sin_ref, row_ref, *rest):
    out_refs, hot_ref = rest[:-1], rest[-1]

    @pl.when(pl.program_id(0) == 0)
    def _():
        ids = lax.broadcasted_iota(jnp.int32, hot_ref.shape, 0)
        hot_ref[...] = (ids == slot_ref[...]).astype(jnp.float32).astype(jnp.bfloat16)

    if turned:
        rows = jnp.concatenate(
            [
                turn(row_ref[:, h * HD : (h + 1) * HD], cos_ref[...], sin_ref[...])
                for h in range(width)
            ],
            axis=1,
        )
    else:
        rows = row_ref[...]
    for j, out_ref in enumerate(out_refs):
        for r in range(classes):
            first = (j * classes + r) * cap
            moved = jnp.dot(
                hot_ref[first : first + cap, :], rows, preferred_element_type=jnp.float32
            ).astype(jnp.bfloat16)
            for h in range(width):
                out_ref[h, r] = moved[:, h * HD : (h + 1) * HD]


def pack(slots, cosine, sine, rows, turned, chunks, classes, cap):
    count = rows.shape[0]
    heads = rows.shape[1] // HD
    width = min(2, heads)
    fixed = lambda i: (0, 0)
    total = chunks * classes * cap
    return pl.pallas_call(
        functools.partial(pack_kernel, turned, classes, cap, width),
        grid=(heads // width,),
        in_specs=[
            pl.BlockSpec((1, count), fixed),
            pl.BlockSpec((count, HD), fixed),
            pl.BlockSpec((count, HD), fixed),
            pl.BlockSpec((count, width * HD), lambda i: (0, i)),
        ],
        out_specs=[pl.BlockSpec((width, classes, cap, HD), lambda i: (i, 0, 0, 0))] * chunks,
        out_shape=[jax.ShapeDtypeStruct((heads, classes, cap, HD), jnp.bfloat16)] * chunks,
        scratch_shapes=[pltpu.VMEM((total, count), jnp.bfloat16)],
        compiler_params=params(),
        cost_estimate=pl.CostEstimate(
            flops=2 * heads * total * count * HD, bytes_accessed=count * heads * HD * 4, transcendentals=0
        ),
    )(slots, cosine, sine, rows)


def piece_rows(cap):
    return max(rows for rows in range(TILE, PAD + 1, TILE) if cap % rows == 0)


def merge_pieces(low, high, piece, source, add):
    shift = low & (TILE - 1)
    pieces = jnp.where(high > low, lax.div(high - low + shift + piece - 1, piece), 0)
    first = low - shift

    def one(i, carry):
        at = pl.multiple_of(first + i * piece, TILE)
        add(at, source(pl.multiple_of(i * piece, TILE)))
        return carry

    lax.fori_loop(0, pieces, one, 0)


def compact_kernel(offsets, per, total, as_keys, member_ref, count_ref, *rest):
    parts, out, all_rows, starts = rest[:-3], rest[-3], rest[-2], rest[-1]
    members = len(parts)
    piece = piece_rows(parts[0].shape[1])
    all_rows[...] = jnp.zeros_like(all_rows)
    start = jnp.int32(0)
    for s in range(count_ref.shape[0]):
        starts[s] = start
        start = start + count_ref[s]

    def add(at, rows):
        all_rows[pl.ds(at, piece), :] += rows

    for part, offset in zip(parts, offsets):
        for z in range(per):
            source = z * members + (member_ref[0] ^ offset)
            low = starts[source]
            merge_pieces(
                low,
                low + count_ref[source],
                piece,
                lambda at: part[z, pl.ds(at, piece), :],
                add,
            )
    if as_keys:
        for first in range(0, total, 2 * TOK_DEV):
            out[:, first : first + 2 * TOK_DEV] = jnp.transpose(
                all_rows[first : first + 2 * TOK_DEV, :]
            )
    else:
        out[...] = all_rows[:total, :]


def compact(member, counts, parts, offsets, total, as_keys):
    per = parts[0].shape[0]
    return pl.pallas_call(
        functools.partial(compact_kernel, offsets, per, total, as_keys),
        in_specs=[whole_smem(), whole_smem()] + [whole_vmem()] * len(parts),
        out_specs=whole_vmem(),
        out_shape=jax.ShapeDtypeStruct(
            (HD, total) if as_keys else (total, HD), jnp.bfloat16
        ),
        scratch_shapes=[
            pltpu.VMEM((total + PAD, HD), jnp.bfloat16),
            pltpu.SMEM(counts.shape, jnp.int32),
        ],
        compiler_params=params(),
        cost_estimate=pl.CostEstimate(flops=total * HD * 8, bytes_accessed=total * HD * 8, transcendentals=0),
    )(member, counts, *parts)


def attend_kernel(ctx_size, block, cls_ref, count_ref, got_ref, key_ref, value_ref, out_ref,
                  query_all, scores_a, scores_b, top_a, top_b, run_max, run_acc):
    span = 2 * TOK_DEV
    pair = 4 * block
    supers = ctx_size // 4
    steps = supers * (supers + 1)
    cls = cls_ref[0]
    piece = piece_rows(got_ref.shape[1])
    query_all[...] = jnp.zeros_like(query_all)

    def add(at, rows):
        query_all[pl.ds(at, piece), :] += rows

    start = jnp.int32(0)
    for s in range(ctx_size):
        end = start + count_ref[s]
        merge_pieces(
            rows_below(start, cls, block),
            rows_below(end, cls, block),
            piece,
            lambda at: got_ref[s, pl.ds(at, piece), :],
            add,
        )
        start = end

    upper = 2 * block
    keep_all, lower = slice(0, pair), slice(upper, pair)

    def row_top(found):
        return jnp.broadcast_to(jnp.max(found, axis=1, keepdims=True), (found.shape[0], HD))

    def allowed(first_row, count, first_key):
        ids = lax.broadcasted_iota(jnp.int32, (count, HD), 0) + first_row
        row = ids + cls * block - first_key
        for n in range(1, 4):
            row = row + jnp.where(ids >= n * block, TOK_DEV - block, 0)
        col = lax.broadcasted_iota(jnp.int32, (count, span), 1)
        return col <= jnp.concatenate([row] * (span // HD), axis=1)

    def put(scores, top, part, found):
        scores[part, :] = found
        top[part, :] = row_top(found)

    def dot_keys(i, k, first_row, count):
        at = jnp.minimum(i, supers - 1) * pair + first_row
        rows = query_all[pl.ds(pl.multiple_of(at, TILE), count), :]
        keys = key_ref[:, pl.ds(pl.multiple_of(k * span, HD), span)]
        return jnp.dot(rows, keys, preferred_element_type=jnp.float32)

    def score(scores, top, i, k):
        put(scores, top, keep_all, dot_keys(i, k, 0, pair))

    def score_lower(scores, top, i, k):
        found = dot_keys(i, k, upper, pair - upper)
        found = jnp.where(allowed(upper, pair - upper, span), found, masked_score)
        put(scores, top, lower, found)

    def mask_upper(scores, top):
        found = jnp.where(allowed(0, upper, 0), scores[:upper, :], masked_score)
        put(scores, top, slice(0, upper), found)

    def absorb(scores, top, k, part):
        before = run_max[part, :]
        after = jnp.maximum(before, top[part, :])
        rescale = jnp.exp2((before - after) * exp2_scale)
        run_max[part, :] = after
        weights = jnp.exp2(
            (scores[part, :] - jnp.concatenate([after] * (span // HD), axis=1)) * exp2_scale
        )
        values = jnp.concatenate(
            [
                value_ref[pl.ds(pl.multiple_of(k * span, TILE), span), :],
                jnp.ones((span, HD), jnp.bfloat16),
            ],
            axis=1,
        )
        run_acc[part, :] = run_acc[part, :] * jnp.concatenate([rescale, rescale], axis=1) + jnp.dot(
            weights.astype(jnp.bfloat16), values, preferred_element_type=jnp.float32
        )

    def clear():
        run_max[...] = jnp.full_like(run_max, masked_score)
        run_acc[...] = jnp.zeros_like(run_acc)

    buffers_a, buffers_b = (scores_a, top_a), (scores_b, top_b)
    clear()
    score(*buffers_a, 0, 0)
    mask_upper(*buffers_a)

    def two_steps(t, at):
        i, k = at
        last = k == 2 * i

        @pl.when(last)
        def _():
            score_lower(*buffers_b, i, k + 1)
            absorb(*buffers_a, k, keep_all)
            score(*buffers_a, i + 1, 0)
            absorb(*buffers_b, k + 1, lower)
            result = (run_acc[:, :HD] / run_acc[:, HD:]).astype(jnp.bfloat16)
            for n in range(4):
                out_ref[4 * i + n] = result[n * block : (n + 1) * block]
            clear()

        @pl.when(jnp.logical_not(last))
        def _():
            score(*buffers_b, i, k + 1)
            absorb(*buffers_a, k, keep_all)
            score(*buffers_a, i, k + 2)
            absorb(*buffers_b, k + 1, keep_all)

            @pl.when(k + 2 == 2 * i)
            def _():
                mask_upper(*buffers_a)

        return jnp.where(last, i + 1, i), jnp.where(last, 0, k + 2)

    lax.fori_loop(0, steps // 2, two_steps, (jnp.int32(0), jnp.int32(0)))


def attend(cls, counts, got, keys, values, block):
    ctx_size = got.shape[0]
    total = values.shape[0]
    pairs = total * ctx_size * block // 2
    return pl.pallas_call(
        functools.partial(attend_kernel, ctx_size, block),
        in_specs=[whole_smem()] * 2 + [whole_vmem()] * 3,
        out_specs=whole_vmem(),
        out_shape=jax.ShapeDtypeStruct((ctx_size, block, HD), jnp.bfloat16),
        scratch_shapes=[
            pltpu.VMEM((ctx_size * block + PAD, HD), jnp.bfloat16),
            pltpu.VMEM((4 * block, 2 * TOK_DEV), jnp.float32),
            pltpu.VMEM((4 * block, 2 * TOK_DEV), jnp.float32),
            pltpu.VMEM((4 * block, HD), jnp.float32),
            pltpu.VMEM((4 * block, HD), jnp.float32),
            pltpu.VMEM((4 * block, HD), jnp.float32),
            pltpu.VMEM((4 * block, 2 * HD), jnp.float32),
        ],
        compiler_params=params(),
        cost_estimate=pl.CostEstimate(
            flops=pairs * 8 * HD, bytes_accessed=total * HD * 8, transcendentals=pairs
        ),
    )(cls, counts, got, keys, values)


def project_kernel(classes, chunks, column_ref, *rest):
    got_refs, (weight_ref, out_ref, rows_ref) = rest[:chunks], rest[chunks:]
    block = got_refs[0].shape[1]

    @pl.when(pl.program_id(0) == 0)
    def _():
        for j, got_ref in enumerate(got_refs):
            for d in range(got_ref.shape[0]):
                h, r = d // classes, d % classes
                first = (j * classes + r) * block
                rows_ref[first : first + block, h * HD : (h + 1) * HD] = got_ref[d]

    out_ref[...] = jnp.dot(
        rows_ref[...], weight_ref[...], preferred_element_type=jnp.float32
    ).astype(jnp.bfloat16)


def project(first_column, got, weight, columns, classes):
    ctx_size, block, _ = got[0].shape
    rows, depth = len(got) * classes * block, weight.shape[0]
    step = min(512, columns)
    return pl.pallas_call(
        functools.partial(project_kernel, classes, len(got)),
        grid_spec=pltpu.PrefetchScalarGridSpec(
            num_scalar_prefetch=1,
            grid=(columns // step,),
            in_specs=[pl.BlockSpec((ctx_size, block, HD), lambda i, first: (0, 0, 0))] * len(got)
            + [pl.BlockSpec((depth, step), lambda i, first: (0, first[0] + i))],
            out_specs=pl.BlockSpec((rows, step), lambda i, first: (0, i)),
            scratch_shapes=[pltpu.VMEM((rows, depth), jnp.bfloat16)],
        ),
        out_shape=jax.ShapeDtypeStruct((rows, columns), jnp.bfloat16),
        compiler_params=params(),
        cost_estimate=pl.CostEstimate(
            flops=2 * rows * depth * columns, bytes_accessed=2 * depth * columns, transcendentals=0
        ),
    )((first_column // step).astype(jnp.int32).reshape(1), *got, weight)


def add_piece_kernel(sum_ref, part_ref, out_ref):
    out_ref[...] = (
        sum_ref[...].astype(jnp.float32) + part_ref[...].astype(jnp.float32)
    ).astype(jnp.bfloat16)


def add_piece(total_sum, part, j, n):
    rows, width = part.shape
    step = min(1024, width)
    steps = width // step
    here = pl.BlockSpec((rows, step), lambda i: (j, n * steps + i))
    return pl.pallas_call(
        add_piece_kernel,
        grid=(steps,),
        in_specs=[here, pl.BlockSpec((rows, step), lambda i: (0, i))],
        out_specs=here,
        out_shape=jax.ShapeDtypeStruct(total_sum.shape, total_sum.dtype),
        input_output_aliases={0: 0},
        compiler_params=params(),
        cost_estimate=pl.CostEstimate(
            flops=rows * width, bytes_accessed=6 * rows * width, transcendentals=0
        ),
    )(total_sum, part)


def tables(query_rows):
    half_dim = HD // 2
    positions = lax.axis_index("ctx") * query_rows + jnp.arange(query_rows, dtype=jnp.int32)
    lane = jnp.arange(HD, dtype=jnp.int32)
    pair_id = jnp.where(lane < half_dim, lane, lane - half_dim)
    inv_freq = rope_base ** (-(pair_id.astype(jnp.float32) * 2.0 / HD))
    angles = positions.astype(jnp.float32)[:, None] * inv_freq[None, :]
    sine = jnp.sin(angles)
    return jnp.cos(angles), jnp.where(lane[None, :] < half_dim, -sine, sine)


def local(query, key, value, keep_rank, kept_count, out_weight):
    ctx_size = lax.axis_size("ctx")
    tp_size = lax.axis_size("tp")
    me = lax.axis_index("ctx")
    tp_me = lax.axis_index("tp")
    orig_rows = query.shape[0]
    heads = query.shape[1] // HD
    kv_heads = key.shape[1] // HD
    members = ctx_size // kv_heads
    classes = ctx_size // heads
    chunks = CHUNKS if classes == 1 else 1
    block = TOK_DEV // (chunks * classes)
    total = ctx_size * TOK_DEV
    reach = orig_rows // TOK_DEV
    cap = reach * block + TILE
    cap_kv = orig_rows + TILE
    columns = out_weight.shape[1] // tp_size

    kv_slots, q_slots = find_slots(
        me.reshape(1), kept_count, keep_rank, reach, chunks * classes, block, cap
    )
    cosine, sine = tables(orig_rows)

    across = [[z * members + m for z in range(kv_heads)] for m in range(members)]

    member = (me & (members - 1)).reshape(1)

    def pack_shared(rows, turned):
        (packed,) = pack(kv_slots, cosine, sine, rows, turned, 1, 1, cap_kv)
        return packed.reshape(kv_heads, cap_kv, HD)

    def send_across(packed):
        if kv_heads == 1:
            return packed
        return lax.all_to_all(
            packed, "ctx", split_axis=0, concat_axis=0, tiled=True, axis_index_groups=across
        )

    def swap(parts, bit):
        pairs = [(d, d ^ bit) for d in range(ctx_size)]
        return parts + [lax.ppermute(part, "ctx", pairs) for part in parts]

    bits = [members >> n for n in range(1, members.bit_length())]
    offsets = [0]
    for bit in bits:
        offsets = offsets + [offset ^ bit for offset in offsets]

    def send_query(packed):
        return lax.all_to_all(
            packed.reshape(ctx_size, cap, HD), "ctx", split_axis=0, concat_axis=0, tiled=True
        )

    both = [(0, 1), (1, 0)]
    key_parts = [send_across(pack_shared(key, True))]
    value_packed, key_parts = lax.optimization_barrier((pack_shared(value, False), key_parts))
    key_parts = swap(key_parts, bits[0])
    value_parts = [send_across(value_packed)]
    packed_q = list(pack(q_slots, cosine, sine, query, True, chunks, classes, cap))
    packed_q[0], key_parts, value_parts = lax.optimization_barrier(
        (packed_q[0], key_parts, value_parts)
    )
    got_q = [send_query(packed_q[0])]
    early = swap(value_parts, bits[1])[1:] if len(bits) == 2 else []
    value_parts = swap(value_parts, bits[0])
    for bit in bits[1:]:
        key_parts = swap(key_parts, bit)
    keys = compact(member, kept_count, key_parts, offsets, total, True)
    if chunks > 1:
        packed_q[1], value_parts, keys = lax.optimization_barrier((packed_q[1], value_parts, keys))
    if len(bits) == 2:
        value_parts = value_parts + early + swap(value_parts[1:], bits[1])[1:]
    else:
        for bit in bits[1:]:
            value_parts = swap(value_parts, bit)
    if chunks > 1:
        got_q.append(send_query(packed_q[1]))
    values = compact(member, kept_count, value_parts, offsets, total, False)

    got, done = [], None
    for j in range(chunks):
        cls_j = j * classes + (me & (classes - 1))
        if j > 0:
            got_q[j], done = lax.optimization_barrier((got_q[j], done))
            got.append(lax.all_to_all(done, "ctx", split_axis=0, concat_axis=0, tiled=True))
        done = attend(cls_j.reshape(1), kept_count, got_q[j], keys, values, block)
        if j > 1:
            done, got[j - 2] = lax.optimization_barrier((done, got[j - 2]))
        if j + 2 < chunks:
            packed_q[j + 2], done = lax.optimization_barrier((packed_q[j + 2], done))
            got_q.append(send_query(packed_q[j + 2]))
    half = columns // 2

    def for_peer(one):
        return [
            project((1 - tp_me) * columns + n * half, [one], out_weight, half, classes)
            for n in range(2)
        ]

    def trade(parts):
        return [lax.ppermute(part, "tp", [(0, 1), (1, 0)]) for part in parts]

    paired = tp_size == 2 and chunks == 2
    if paired:
        first = for_peer(got[0])
        done, first[0] = lax.optimization_barrier((done, first[0]))
    last = lax.all_to_all(done, "ctx", split_axis=0, concat_axis=0, tiled=True)
    if paired:
        last, first[1] = lax.optimization_barrier((last, first[1]))
        came = [trade(first), trade(for_peer(last))]
        total_sum = project(tp_me * columns, got + [last], out_weight, columns, classes)
        for j, parts in enumerate(came):
            for n, part in enumerate(parts):
                total_sum = add_piece(total_sum, part, j, n)
        return total_sum
    got.append(last)
    full = project(jnp.int32(0) * tp_me, got, out_weight, columns * tp_size, classes)
    split = jnp.transpose(full.reshape(full.shape[0], tp_size, columns), (1, 0, 2))
    swapped = lax.all_to_all(split, "tp", split_axis=0, concat_axis=0, tiled=True)
    return jnp.sum(swapped.astype(jnp.float32), axis=0).astype(jnp.bfloat16)


def solution(mesh):
    placed = (P("ctx", "tp"), P("ctx", "tp"), P("ctx", "tp"), P("ctx", None), P(), P("tp", None))
    return jax.shard_map(
        local, mesh=mesh, in_specs=placed, out_specs=P("ctx", "tp"), check_vma=False
    )
```
